32 devices in a mesh: groups: 2 (over y), wide: 4 (over z), narrow: 4 (over x, core).
Axes of the slice: x: 2, y: 2, z: 4, core: 2. Of those that a mesh axis runs over, the one named last changes fastest.
Arguments:
- homolog_embedding: bfloat16 [256, 192, 256], P(('groups', 'narrow'), 'wide'), parts along dimension 0, may hold values from -6 to 6
- normalize_scale: float32 [256], replicated, may hold values from 0.1 to 1.9
- normalize_shift: float32 [256], replicated, may hold values from -3 to 3
- lhs_factor_matrix: bfloat16 [256, 32], replicated, may hold values from -0.375 to 0.375
- lhs_factor_shift: float32 [32], replicated, may hold values from -1 to 1
- rhs_factor_matrix: bfloat16 [256, 32], replicated, may hold values from -0.375 to 0.375
- rhs_factor_shift: float32 [32], replicated, may hold values from -1 to 1
- pair_update_matrix: bfloat16 [1024, 128], replicated, may hold values from -1.796875 to 1.796875
- pair_update_shift: float32 [128], replicated, may hold values from -3 to 3
Outputs:
- pair_update: bfloat16 [384, 192, 128], P(('groups', 'wide', 'narrow')), parts along dimension 0
The draws below stay inside these ranges and needn't reach their ends.
There are 2 independent parts, one for each index of `groups`. The reference program is written for one: setup_inputs(seed, part) draws one part's arguments, and reference() takes and returns one part's arrays. A program takes and returns all parts, laid end to end along the dimension named above; an argument that names none is the same for every part. Nothing has to cross between parts.
All inputs are finite; a program needn't handle non-finite values.
Results may differ from the reference program's by a relative error of at most 0.0053.
Values may be sent and summed in bfloat16 or wider, within the bound.
No kernel may reach another device: no remote copies, remote signals or barrier semaphores. Data moves between devices by JAX's collectives and lax.ppermute only.
A program may use at most 64 MiB of HBM per device.

```python
import jax
import jax.numpy as jnp
from jax import lax

HOMOLOG_TOTAL = 128
EMBED_DEPTH = 256
HIDDEN_DEPTH = 32
CZ = 128
ROWS_DEV = 12
CHAIN_LENGTH = 192


def steps_of(stream_key, dims, split, smallest, high):
    factor_of = 1.0
    for position, shards_of in split:
        draws = jax.random.uniform(jax.random.fold_in(jax.random.fold_in(stream_key, 6), position), (shards_of,), jnp.float32, smallest / len(split), high / len(split))
        factor_of = factor_of * jnp.repeat(jnp.exp(draws), dims[position] // shards_of).reshape((-1,) + (1,) * (len(dims) - 1 - position))
    return factor_of


def bell_draw(key, dims, deviation, limit, cuts=(), kind=jnp.bfloat16):
    factor_of = steps_of(key, dims, cuts, -0.22, 0.18) if cuts else 1.0
    drawn = jax.random.normal(key, dims, jnp.float32) * deviation * factor_of
    return jnp.minimum(jnp.maximum(drawn, -limit), limit).astype(kind)


def setup_inputs(seed: int = 0, part: int = 0) -> dict:
    key_of = jax.random.split(jax.random.key(seed), 10)
    part_splits = jax.random.split(jax.random.fold_in(key_of[9], part), 10)
    homolog_embedding = bell_draw(part_splits[0], (HOMOLOG_TOTAL, CHAIN_LENGTH, EMBED_DEPTH), 1.0, 6.0, ((0, 4), (1, 4)))
    normalize_scale = jnp.clip(1.0 + 0.18 * jax.random.normal(key_of[1], (EMBED_DEPTH,), jnp.float32), 0.1, 1.9)
    normalize_shift = bell_draw(key_of[2], (EMBED_DEPTH,), 0.5, 3.0, (), jnp.float32)
    lhs_factor_matrix = bell_draw(key_of[3], (EMBED_DEPTH, HIDDEN_DEPTH), EMBED_DEPTH ** -0.5, 0.375)
    lhs_factor_shift = bell_draw(key_of[4], (HIDDEN_DEPTH,), 0.2, 1.0, (), jnp.float32)
    rhs_factor_matrix = bell_draw(key_of[5], (EMBED_DEPTH, HIDDEN_DEPTH), EMBED_DEPTH ** -0.5, 0.375)
    rhs_factor_shift = bell_draw(key_of[6], (HIDDEN_DEPTH,), 0.2, 1.0, (), jnp.float32)
    pair_update_matrix = bell_draw(key_of[7], (HIDDEN_DEPTH * HIDDEN_DEPTH, CZ), 0.3, 1.796875)
    pair_update_shift = bell_draw(key_of[8], (CZ,), 0.5, 3.0, (), jnp.float32)
    return {"homolog_embedding": homolog_embedding, "normalize_scale": normalize_scale, "normalize_shift": normalize_shift, "lhs_factor_matrix": lhs_factor_matrix, "lhs_factor_shift": lhs_factor_shift, "rhs_factor_matrix": rhs_factor_matrix, "rhs_factor_shift": rhs_factor_shift, "pair_update_matrix": pair_update_matrix, "pair_update_shift": pair_update_shift}


def map_through_matrix(homolog_embedding, normalize_scale, normalize_shift, mapping_matrix, additive_shift):
    source_tensor = homolog_embedding.astype(jnp.float32)
    center = lax.optimization_barrier(jnp.mean(source_tensor, axis=-1, keepdims=True))
    spread = lax.optimization_barrier(jnp.mean((source_tensor - center) ** 2, axis=-1, keepdims=True))
    normed = ((source_tensor - center) / jnp.sqrt(spread + 1e-05) * normalize_scale + normalize_shift).astype(jnp.bfloat16)
    flat = normed.reshape(-1, normed.shape[-1])
    return (jnp.dot(flat, mapping_matrix, preferred_element_type=jnp.float32) + additive_shift).astype(jnp.bfloat16)

def pair_block(left_rows, right_cols, pair_update_matrix, pair_update_shift):
    count_rows = left_rows.shape[1] // HIDDEN_DEPTH
    count_cols = right_cols.shape[1] // HIDDEN_DEPTH
    outer = lax.dot_general(left_rows, right_cols, (((0,), (0,)), ((), ())), preferred_element_type=jnp.float32) / HOMOLOG_TOTAL
    outer = outer.reshape(count_rows, HIDDEN_DEPTH, count_cols, HIDDEN_DEPTH).transpose(0, 2, 1, 3)
    outer = outer.reshape(count_rows * count_cols, HIDDEN_DEPTH * HIDDEN_DEPTH).astype(jnp.bfloat16)
    result = jnp.dot(outer, pair_update_matrix, preferred_element_type=jnp.float32) + pair_update_shift
    return result.astype(jnp.bfloat16).reshape(count_rows, count_cols, CZ)

def reference(homolog_embedding, normalize_scale, normalize_shift, lhs_factor_matrix, lhs_factor_shift, rhs_factor_matrix, rhs_factor_shift, pair_update_matrix, pair_update_shift):
    lhs_factor_tensor = map_through_matrix(homolog_embedding, normalize_scale, normalize_shift, lhs_factor_matrix, lhs_factor_shift).reshape(HOMOLOG_TOTAL, CHAIN_LENGTH * HIDDEN_DEPTH)
    rhs_factor_tensor = map_through_matrix(homolog_embedding, normalize_scale, normalize_shift, rhs_factor_matrix, rhs_factor_shift).reshape(HOMOLOG_TOTAL, CHAIN_LENGTH * HIDDEN_DEPTH)
    blocks = jnp.moveaxis(lhs_factor_tensor.reshape(HOMOLOG_TOTAL, CHAIN_LENGTH // ROWS_DEV, ROWS_DEV * HIDDEN_DEPTH), 1, 0)
    result = lax.map(lambda rows: pair_block(rows, rhs_factor_tensor, pair_update_matrix, pair_update_shift), blocks)
    return result.reshape(CHAIN_LENGTH, CHAIN_LENGTH, CZ)
```

```python
import functools

import jax
import jax.numpy as jnp
from jax import lax
from jax.experimental import pallas as pl
from jax.experimental.pallas import tpu as pltpu
from jax.sharding import PartitionSpec as P

LANES = 128
VMEM_LIMIT = 50 * 1024 * 1024


def iota(shape, dim):
    return lax.broadcasted_iota(jnp.int32, shape, dim)


def features_kernel(
    x_ref, gain_ref, bias_ref, lm_ref, lb_ref, rm_ref, rb_ref,
    left_ref, right_ref,
    lo_ref, hi_ref, turned_ref, rows_ref,
):
    seqs, residues, depth = x_ref.shape
    hidden = lm_ref.shape[1]
    per = LANES // hidden
    slots = LANES // seqs
    minor = hidden // slots
    groups = residues // per
    own = lax.axis_index("narrow")

    gain = gain_ref[...].reshape(1, depth)
    bias = bias_ref[...].reshape(1, depth)
    step = 4
    for s in range(0, seqs, step):
        x = x_ref[s : s + step].reshape(step * residues, depth).astype(jnp.float32)
        x = x - jnp.mean(x, axis=-1, keepdims=True)
        spread = jnp.mean(x * x, axis=-1, keepdims=True)
        x = x * lax.rsqrt(spread + 1e-05) * gain + bias
        rows = pl.ds(s * residues, step * residues)
        lo_ref[rows, :] = x[:, :LANES]
        hi_ref[rows, :] = x[:, LANES:]

    spread_l = (iota((hidden, LANES), 1) % hidden == iota((hidden, LANES), 0))
    spread_r = iota((hidden, LANES), 1) % hidden == (iota((hidden, LANES), 0) + own * minor) % hidden
    spread_l = spread_l.astype(jnp.float32)
    spread_r = spread_r.astype(jnp.float32)

    def widen(m, pick):
        return jnp.dot(m, pick.astype(jnp.bfloat16), preferred_element_type=jnp.float32)

    def widen_bias(b, pick):
        b = jnp.broadcast_to(b.reshape(1, hidden), (8, hidden))
        return jnp.dot(
            b, pick, precision=lax.Precision.HIGHEST, preferred_element_type=jnp.float32
        )[:1]

    weights = jnp.concatenate(
        [widen(lm_ref[...], spread_l), widen(rm_ref[...], spread_r)], axis=1
    )
    shift = jnp.concatenate(
        [widen_bias(lb_ref[...], spread_l), widen_bias(rb_ref[...], spread_r)], axis=1
    )
    place = iota((depth, 2 * LANES), 1) % LANES // hidden
    total = None
    for k in range(per):
        part = jnp.concatenate(
            [
                jnp.concatenate(
                    [half[pl.ds(g * per + k, seqs, stride=residues), :] for half in (lo_ref, hi_ref)],
                    axis=1,
                )
                for g in range(groups)
            ],
            axis=0,
        ).astype(jnp.bfloat16)
        placed = jnp.where(place == k, weights, 0.0).astype(jnp.bfloat16)
        term = jnp.dot(part, placed, preferred_element_type=jnp.float32)
        total = term if total is None else total + term
    total = total + shift
    left_ref[...] = total[:, :LANES].astype(left_ref.dtype).reshape(groups, seqs, LANES)

    slot = iota((minor, LANES), 1) // seqs
    for block in range(groups // slots):
        turned_ref[...] = total[block * LANES : (block + 1) * LANES, LANES:].T
        for k in range(per):
            pieces = [turned_ref[pl.ds(k * hidden + q * minor, minor), :] for q in range(slots)]
            for g in range(slots):
                out = None
                for q in range(slots):
                    piece = pieces[q]
                    if q != g:
                        piece = pltpu.roll(piece, (q - g) % slots * seqs, axis=1)
                    out = piece if out is None else jnp.where(slot == q, piece, out)
                j = (block * slots + g) * per + k
                rows_ref[pl.ds(j, minor, stride=residues), :] = out
    right_ref[...] = rows_ref[...].astype(right_ref.dtype).reshape(minor, residues, LANES)


def pair_kernel(left_ref, right_ref, w_ref, shift_ref, out_ref, wf_ref, wide_ref, outer_ref, *, seqs_total):
    parts, groups, seqs, _ = left_ref.shape
    wides, _, minor, residues, _ = right_ref.shape
    cz = w_ref.shape[1]
    hidden = minor * parts
    per = LANES // hidden
    cols = wides * residues

    @pl.when(pl.program_id(0) == 0)
    def _():
        wf_ref[...] = w_ref[...].astype(jnp.float32)
        wide_ref[...] = jnp.zeros_like(wide_ref)
        for e in range(hidden):
            rows = wf_ref[pl.ds(e, hidden, stride=hidden), :].astype(jnp.bfloat16)
            for k in range(per):
                wide_ref[pl.ds(e * LANES + k * hidden, hidden), k * cz : (k + 1) * cz] = rows

    slot = iota((minor * residues, LANES), 1) // seqs
    for q in range(parts):
        left = jnp.concatenate(
            [
                jnp.concatenate([left_ref[(k - q) % parts, g] for k in range(parts)], axis=0)
                for g in range(groups)
            ],
            axis=1,
        )
        for w in range(wides):
            right = None
            for k in range(parts):
                chunk = right_ref[w, (k - q) % parts].reshape(minor * residues, LANES)
                right = chunk if right is None else jnp.where(slot == k, chunk, right)
            outer = jnp.dot(right, left, preferred_element_type=jnp.float32).astype(jnp.bfloat16)
            for e in range(minor):
                for g in range(groups):
                    outer_ref[
                        pl.ds(g * cols + w * residues, residues),
                        (q * minor + e) * LANES : (q * minor + e + 1) * LANES,
                    ] = outer[e * residues : (e + 1) * residues, g * LANES : (g + 1) * LANES]

    shift = shift_ref[...].reshape(1, cz)
    for g in range(groups):
        pair = jnp.dot(
            outer_ref[pl.ds(g * cols, cols), :], wide_ref[...], preferred_element_type=jnp.float32
        )
        for k in range(per):
            out_ref[g * per + k] = (
                pair[:, k * cz : (k + 1) * cz] * (1.0 / seqs_total) + shift
            ).astype(out_ref.dtype)


def vmem(count):
    return [pl.BlockSpec(memory_space=pltpu.VMEM)] * count


def on_device(wide, narrow, x, gain, bias, lm, lb, rm, rb, w, shift):
    seqs, residues, depth = x.shape
    hidden = lm.shape[1]
    cz = w.shape[1]
    per = LANES // hidden
    slots = LANES // seqs
    minor = hidden // slots
    own_rows = residues // narrow
    groups = own_rows // per
    left, right = pl.pallas_call(
        features_kernel,
        out_shape=(
            jax.ShapeDtypeStruct((residues // per, seqs, LANES), jnp.bfloat16),
            jax.ShapeDtypeStruct((minor, residues, LANES), jnp.bfloat16),
        ),
        in_specs=vmem(7),
        out_specs=tuple(vmem(2)),
        scratch_shapes=[
            pltpu.VMEM((seqs * residues, LANES), jnp.float32),
            pltpu.VMEM((seqs * residues, LANES), jnp.float32),
            pltpu.VMEM((LANES, LANES), jnp.float32),
            pltpu.VMEM((minor * residues, LANES), jnp.float32),
        ],
        compiler_params=pltpu.CompilerParams(vmem_limit_bytes=VMEM_LIMIT),
        name="features",
    )(x, gain, bias, lm, lb, rm, rb)
    right = lax.all_gather(right, ("wide", "narrow"), axis=0, tiled=False)
    right = right.reshape(wide, narrow, minor, residues, LANES)
    left = left.reshape(narrow, groups, seqs, LANES)
    left = lax.all_to_all(left, "narrow", split_axis=0, concat_axis=0, tiled=True)
    block = wide
    while block % 2 == 0 and block * residues > 192:
        block //= 2
    cols = block * residues
    return pl.pallas_call(
        functools.partial(pair_kernel, seqs_total=seqs * narrow),
        grid=(wide // block,),
        out_shape=jax.ShapeDtypeStruct((own_rows, wide * residues, cz), jnp.bfloat16),
        in_specs=[
            pl.BlockSpec((narrow, groups, seqs, LANES), lambda b: (0, 0, 0, 0)),
            pl.BlockSpec((block, narrow, minor, residues, LANES), lambda b: (b, 0, 0, 0, 0)),
            pl.BlockSpec(w.shape, lambda b: (0, 0)),
            pl.BlockSpec(shift.shape, lambda b: (0,)),
        ],
        out_specs=pl.BlockSpec((own_rows, cols, cz), lambda b: (0, b, 0)),
        scratch_shapes=[
            pltpu.VMEM(w.shape, jnp.float32),
            pltpu.VMEM((hidden * LANES, per * cz), jnp.bfloat16),
            pltpu.VMEM((groups * cols, hidden * LANES), jnp.bfloat16),
        ],
        compiler_params=pltpu.CompilerParams(vmem_limit_bytes=VMEM_LIMIT),
        name="pairs",
    )(left, right, w, shift)


def solution(mesh):
    in_specs = (P(("groups", "narrow"), "wide", None), P(), P(), P(), P(), P(), P(), P(), P())
    out_specs = P(("groups", "wide", "narrow"), None, None)
    return jax.shard_map(
        functools.partial(on_device, mesh.shape["wide"], mesh.shape["narrow"]),
        mesh=mesh,
        in_specs=in_specs,
        out_specs=out_specs,
        check_vma=False,
    )
```

```python
import functools

import jax
import jax.numpy as jnp
from jax import lax
from jax.experimental import pallas as pl
from jax.experimental.pallas import tpu as pltpu
from jax.sharding import PartitionSpec as P

LANES = 128
VMEM_LIMIT = 40 * 1024 * 1024
VMEM_ALL = 62 * 1024 * 1024


def iota(shape, dim):
    return lax.broadcasted_iota(jnp.int32, shape, dim)


def features_kernel(
    x_hbm, gain_hbm, bias_hbm, lm_hbm, lb_hbm, rm_hbm, rb_hbm,
    *refs, parts, pieces,
):
    left_refs, right_ref = refs[:parts], refs[parts]
    (x_ref, gain_ref, bias_ref, lm_ref, lb_ref, rm_ref, rb_ref,
     lo_ref, hi_ref, left_all, turned_ref, rows_ref, sems) = refs[parts + 1 :]
    seqs, residues, depth = x_ref.shape
    hidden = lm_ref.shape[0]
    per = LANES // hidden
    slots = LANES // seqs
    minor = hidden // slots
    groups = residues // per
    own = lax.axis_index("narrow")

    piece = seqs // pieces
    copies = [
        pltpu.make_async_copy(
            x_hbm.at[pl.ds(p * piece, piece)], x_ref.at[pl.ds(p * piece, piece)], sems.at[p]
        )
        for p in range(pieces)
    ]
    small = ((gain_hbm, gain_ref), (bias_hbm, bias_ref), (lm_hbm, lm_ref),
             (lb_hbm, lb_ref), (rm_hbm, rm_ref), (rb_hbm, rb_ref))
    rest = [pltpu.make_async_copy(a, b, sems.at[pieces + i]) for i, (a, b) in enumerate(small)]
    copies[0].start()
    for copy in rest:
        copy.start()
    for copy in copies[1:]:
        copy.start()
    for copy in rest:
        copy.wait()

    column, row = iota((hidden, LANES), 1) % hidden, iota((hidden, LANES), 0)
    spread_l = (column == row).astype(jnp.float32)
    spread_r = (column == (row ^ (own * minor))).astype(jnp.float32)

    def widen(m, pick):
        return lax.dot_general(
            m, pick.astype(jnp.bfloat16), (((0,), (0,)), ((), ())),
            preferred_element_type=jnp.float32,
        )

    def widen_bias(b, pick):
        b = jnp.broadcast_to(b.reshape(1, hidden), (8, hidden))
        return jnp.dot(
            b, pick, precision=lax.Precision.HIGHEST, preferred_element_type=jnp.float32
        )[:1]

    weights = jnp.concatenate(
        [widen(lm_ref[...], spread_l), widen(rm_ref[...], spread_r)], axis=1
    )
    shift = jnp.concatenate(
        [widen_bias(lb_ref[...], spread_l), widen_bias(rb_ref[...], spread_r)], axis=1
    )
    place = iota((depth, 2 * LANES), 1) % LANES // hidden

    gain = gain_ref[...].reshape(1, depth)
    bias = bias_ref[...].reshape(1, depth)
    step = 4
    for s in range(0, seqs, step):
        if s % piece == 0:
            copies[s // piece].wait()
        x = x_ref[s : s + step].reshape(step * residues, depth).astype(jnp.float32)
        x = x - jnp.mean(x, axis=-1, keepdims=True)
        spread = jnp.mean(x * x, axis=-1, keepdims=True)
        x = x * lax.rsqrt(spread + 1e-05) * gain + bias
        rows = pl.ds(s * residues, step * residues)
        lo_ref[rows, :] = x[:, :LANES]
        hi_ref[rows, :] = x[:, LANES:]

    total = None
    for k in range(per):
        part = jnp.concatenate(
            [
                jnp.concatenate(
                    [half[pl.ds(g * per + k, seqs, stride=residues), :] for half in (lo_ref, hi_ref)],
                    axis=1,
                )
                for g in range(groups)
            ],
            axis=0,
        ).astype(jnp.bfloat16)
        placed = jnp.where(place == k, weights, 0.0).astype(jnp.bfloat16)
        term = jnp.dot(part, placed, preferred_element_type=jnp.float32)
        total = term if total is None else total + term
    total = total + shift
    left_all[...] = total[:, :LANES].astype(left_all.dtype).reshape(groups, seqs, LANES)
    mine = groups // parts
    for m in range(parts):
        left_refs[m][...] = left_all[pl.ds((own ^ m) * mine, mine)]

    slot = iota((minor, LANES), 1) // seqs
    for block in range(groups // slots):
        turned_ref[...] = total[block * LANES : (block + 1) * LANES, LANES:].T
        for k in range(per):
            parts_of = [turned_ref[pl.ds(k * hidden + q * minor, minor), :] for q in range(slots)]
            for g in range(slots):
                out = None
                for q in range(slots):
                    moved = parts_of[q]
                    if q != g:
                        moved = pltpu.roll(moved, (q - g) % slots * seqs, axis=1)
                    out = moved if out is None else jnp.where(slot == q, moved, out)
                j = (block * slots + g) * per + k
                rows_ref[pl.ds(j, minor, stride=residues), :] = out
    right_ref[...] = rows_ref[...].astype(right_ref.dtype).reshape(minor, residues, LANES)


def weights_kernel(w_hbm, wide_ref, w_ref, wf_ref, sem, *, parts, hidden):
    copy = pltpu.make_async_copy(w_hbm, w_ref, sem)
    copy.start()
    cz = w_ref.shape[1]
    per = LANES // hidden
    minor = hidden // parts
    own = lax.axis_index("narrow")
    wide_ref[...] = jnp.zeros_like(wide_ref)
    copy.wait()
    wf_ref[...] = w_ref[...].astype(jnp.float32)
    for e in range(hidden):
        rows = wf_ref[pl.ds(e ^ (own * minor), hidden, stride=hidden), :].astype(jnp.bfloat16)
        for k in range(per):
            wide_ref[pl.ds(e * LANES + k * hidden, hidden), k * cz : (k + 1) * cz] = rows


def pair_kernel(*refs, wides, parts, relative, seqs_total):
    left_refs = refs[:parts]
    wide_ref, shift_ref, out_ref, outer_ref = refs[-4:]
    chunks = refs[parts:-4]
    groups, seqs, _ = left_refs[0].shape
    if relative:
        chunk_of = lambda d, m: chunks[d * parts + m][...]
    else:
        chunk_of = lambda d, m: chunks[0][d, m]
    minor, residues, _ = chunk_of(0, 0).shape
    cz = shift_ref.shape[0]
    per = LANES // (minor * parts)
    cols = wides * residues

    slot = iota((minor * residues, LANES), 1) // seqs
    for q in range(parts):
        left = jnp.concatenate(
            [
                jnp.concatenate([left_refs[q ^ k][g] for k in range(parts)], axis=0)
                for g in range(groups)
            ],
            axis=1,
        )
        for d in range(wides):
            if relative:
                at = lax.rem(lax.axis_index("wide") + (wides - d), wides)
            else:
                at = d
            right = None
            for k in range(parts):
                chunk = chunk_of(d, q ^ k).reshape(minor * residues, LANES)
                right = chunk if right is None else jnp.where(slot == k, chunk, right)
            outer = jnp.dot(right, left, preferred_element_type=jnp.float32).astype(jnp.bfloat16)
            for e in range(minor):
                for g in range(groups):
                    outer_ref[
                        pl.ds(pl.multiple_of(g * cols + at * residues, 16), residues),
                        (q * minor + e) * LANES : (q * minor + e + 1) * LANES,
                    ] = outer[e * residues : (e + 1) * residues, g * LANES : (g + 1) * LANES]

    shift = shift_ref[...].reshape(1, cz)
    for g in range(groups):
        pair = jnp.dot(
            outer_ref[pl.ds(g * cols, cols), :], wide_ref[...], preferred_element_type=jnp.float32
        )
        for k in range(per):
            out_ref[g * per + k] = (
                pair[:, k * cz : (k + 1) * cz] * (1.0 / seqs_total) + shift
            ).astype(out_ref.dtype)


def on_device(wide, narrow, x, gain, bias, lm, lb, rm, rb, w, shift):
    seqs, residues, depth = x.shape
    hidden = lm.shape[1]
    cz = w.shape[1]
    per = LANES // hidden
    slots = LANES // seqs
    minor = hidden // slots
    own_rows = residues // narrow
    groups = own_rows // per
    pieces = 4
    hbm = pl.BlockSpec(memory_space=pltpu.HBM)
    vmem = pl.BlockSpec(memory_space=pltpu.VMEM)
    params = pltpu.CompilerParams(vmem_limit_bytes=VMEM_LIMIT)
    left_shape = jax.ShapeDtypeStruct((groups, seqs, LANES), jnp.bfloat16)
    right_shape = jax.ShapeDtypeStruct((minor, residues, LANES), jnp.bfloat16)
    args = (x, gain, bias, lm.T, lb, rm.T, rb)
    *lefts, right = pl.pallas_call(
        functools.partial(features_kernel, parts=narrow, pieces=pieces),
        out_shape=(left_shape,) * narrow + (right_shape,),
        in_specs=[hbm] * len(args),
        out_specs=(vmem,) * (narrow + 1),
        scratch_shapes=[pltpu.VMEM(a.shape, a.dtype) for a in args]
        + [
            pltpu.VMEM((seqs * residues, LANES), jnp.float32),
            pltpu.VMEM((seqs * residues, LANES), jnp.float32),
            pltpu.VMEM((residues // per, seqs, LANES), jnp.bfloat16),
            pltpu.VMEM((LANES, LANES), jnp.float32),
            pltpu.VMEM((minor * residues, LANES), jnp.float32),
            pltpu.SemaphoreType.DMA((pieces + len(args) - 1,)),
        ],
        compiler_params=pltpu.CompilerParams(vmem_limit_bytes=VMEM_ALL),
        name="features",
    )(*args)

    def across(a, m):
        return lax.ppermute(a, "narrow", [(i, i ^ m) for i in range(narrow)])

    def along(a, d):
        return lax.ppermute(a, "wide", [(i, (i + d) % wide) for i in range(wide)])

    relative = wide * narrow <= 16
    lefts = [lefts[0]] + [across(lefts[m], m) for m in range(1, narrow)]
    if relative:
        rows = [right] + [along(right, d) for d in range(1, wide)]
        rights = [[chunk] for chunk in rows]
        bit, order = narrow // 2, [0]
        while bit:
            rights = [row + [across(chunk, bit) for chunk in row] for row in rights]
            order = order + [m ^ bit for m in order]
            bit //= 2
        rights = [row[order.index(m)] for row in rights for m in range(narrow)]
    else:
        every = lax.all_gather(right, ("wide", "narrow"), axis=0, tiled=False)
        every = every.reshape(wide, narrow, minor, residues, LANES)
        rights = [jnp.take(every, lax.axis_index("narrow") ^ jnp.arange(narrow), axis=1)]

    block_weights = pl.pallas_call(
        functools.partial(weights_kernel, parts=narrow, hidden=hidden),
        out_shape=jax.ShapeDtypeStruct((hidden * LANES, per * cz), jnp.bfloat16),
        in_specs=[hbm],
        out_specs=vmem,
        scratch_shapes=[
            pltpu.VMEM(w.shape, w.dtype),
            pltpu.VMEM(w.shape, jnp.float32),
            pltpu.SemaphoreType.DMA,
        ],
        compiler_params=params,
        name="block_weights",
    )(w)

    block = wide
    if not relative:
        while block % 2 == 0 and block * residues > 192:
            block //= 2
    cols = block * residues
    out_shape = jax.ShapeDtypeStruct((own_rows, wide * residues, cz), jnp.bfloat16)
    scratch = [pltpu.VMEM((groups * cols, hidden * LANES), jnp.bfloat16)]
    body = functools.partial(
        pair_kernel, wides=block, parts=narrow, relative=relative, seqs_total=seqs * narrow
    )
    if relative:
        specs = dict(in_specs=[vmem] * (narrow + len(rights) + 2), out_specs=vmem)
    else:
        specs = dict(
            grid=(wide // block,),
            in_specs=[pl.BlockSpec((groups, seqs, LANES), lambda b: (0, 0, 0))] * narrow
            + [
                pl.BlockSpec((block, narrow, minor, residues, LANES), lambda b: (b, 0, 0, 0, 0)),
                pl.BlockSpec((hidden * LANES, per * cz), lambda b: (0, 0)),
                pl.BlockSpec((cz,), lambda b: (0,)),
            ],
            out_specs=pl.BlockSpec((own_rows, cols, cz), lambda b: (0, b, 0)),
        )
    return pl.pallas_call(
        body,
        out_shape=out_shape,
        scratch_shapes=scratch,
        compiler_params=params,
        name="pairs",
        **specs,
    )(*lefts, *rights, block_weights, shift)


def solution(mesh):
    in_specs = (P(("groups", "narrow"), "wide", None), P(), P(), P(), P(), P(), P(), P(), P())
    out_specs = P(("groups", "wide", "narrow"), None, None)
    return jax.shard_map(
        functools.partial(on_device, mesh.shape["wide"], mesh.shape["narrow"]),
        mesh=mesh,
        in_specs=in_specs,
        out_specs=out_specs,
        check_vma=False,
    )
```

```python
import functools

import jax
import jax.numpy as jnp
from jax import lax
from jax.experimental import pallas as pl
from jax.experimental.pallas import tpu as pltpu
from jax.sharding import PartitionSpec as P

LANES = 128
RIGHT = -1
VMEM_LIMIT = 40 * 1024 * 1024
VMEM_ALL = 62 * 1024 * 1024


def iota(shape, dim):
    return lax.broadcasted_iota(jnp.int32, shape, dim)


def features_kernel(
    x_hbm, gain_hbm, bias_hbm, lm_hbm, lb_hbm, rm_hbm, rb_hbm,
    *refs, packs, parts, pieces,
):
    outs = refs[: len(packs)]
    (x_ref, gain_ref, bias_ref, lm_ref, lb_ref, rm_ref, rb_ref,
     lo_ref, hi_ref, left_all, turned_ref, rows_ref, sems) = refs[len(packs) :]
    seqs, residues, depth = x_ref.shape
    hidden = lm_ref.shape[0]
    per = LANES // hidden
    slots = LANES // seqs
    minor = hidden // slots
    groups = residues // per
    own = lax.axis_index("narrow")

    piece = seqs // pieces
    copies = [
        pltpu.make_async_copy(
            x_hbm.at[pl.ds(p * piece, piece)], x_ref.at[pl.ds(p * piece, piece)], sems.at[p]
        )
        for p in range(pieces)
    ]
    small = ((gain_hbm, gain_ref), (bias_hbm, bias_ref), (lm_hbm, lm_ref),
             (lb_hbm, lb_ref), (rm_hbm, rm_ref), (rb_hbm, rb_ref))
    rest = [pltpu.make_async_copy(a, b, sems.at[pieces + i]) for i, (a, b) in enumerate(small)]
    copies[0].start()
    for copy in rest:
        copy.start()
    for copy in copies[1:]:
        copy.start()
    for copy in rest:
        copy.wait()

    column, row = iota((hidden, LANES), 1) % hidden, iota((hidden, LANES), 0)
    spread_l = (column == row).astype(jnp.float32)
    spread_r = (column == (row ^ (own * minor))).astype(jnp.float32)

    def widen(m, pick):
        return lax.dot_general(
            m, pick.astype(jnp.bfloat16), (((0,), (0,)), ((), ())),
            preferred_element_type=jnp.float32,
        )

    def widen_bias(b, pick):
        b = jnp.broadcast_to(b.reshape(1, hidden), (8, hidden))
        return jnp.dot(
            b, pick, precision=lax.Precision.HIGHEST, preferred_element_type=jnp.float32
        )[:1]

    weights = jnp.concatenate(
        [widen(lm_ref[...], spread_l), widen(rm_ref[...], spread_r)], axis=1
    )
    shift = jnp.concatenate(
        [widen_bias(lb_ref[...], spread_l), widen_bias(rb_ref[...], spread_r)], axis=1
    )
    place = iota((depth, 2 * LANES), 1) % LANES // hidden

    gain = gain_ref[...].reshape(1, depth)
    bias = bias_ref[...].reshape(1, depth)
    step = 4
    for s in range(0, seqs, step):
        if s % piece == 0:
            copies[s // piece].wait()
        x = x_ref[s : s + step].reshape(step * residues, depth).astype(jnp.float32)
        x = x - jnp.mean(x, axis=-1, keepdims=True)
        spread = jnp.mean(x * x, axis=-1, keepdims=True)
        x = x * lax.rsqrt(spread + 1e-05) * gain + bias
        rows = pl.ds(s * residues, step * residues)
        lo_ref[rows, :] = x[:, :LANES]
        hi_ref[rows, :] = x[:, LANES:]

    total = None
    for k in range(per):
        part = jnp.concatenate(
            [
                jnp.concatenate(
                    [half[pl.ds(g * per + k, seqs, stride=residues), :] for half in (lo_ref, hi_ref)],
                    axis=1,
                )
                for g in range(groups)
            ],
            axis=0,
        ).astype(jnp.bfloat16)
        placed = jnp.where(place == k, weights, 0.0).astype(jnp.bfloat16)
        term = jnp.dot(part, placed, preferred_element_type=jnp.float32)
        total = term if total is None else total + term
    total = total + shift
    left_all[...] = total[:, :LANES].astype(left_all.dtype).reshape(groups, seqs, LANES)
    mine = groups // parts

    slot = iota((minor, LANES), 1) // seqs
    for block in range(groups // slots):
        turned_ref[...] = total[block * LANES : (block + 1) * LANES, LANES:].T
        for k in range(per):
            parts_of = [turned_ref[pl.ds(k * hidden + q * minor, minor), :] for q in range(slots)]
            for g in range(slots):
                out = None
                for q in range(slots):
                    moved = parts_of[q]
                    if q != g:
                        moved = pltpu.roll(moved, (q - g) % slots * seqs, axis=1)
                    out = moved if out is None else jnp.where(slot == q, moved, out)
                j = (block * slots + g) * per + k
                rows_ref[pl.ds(j, minor, stride=residues), :] = out
    right = rows_ref[...].astype(jnp.bfloat16)
    for out, pack in zip(outs, packs):
        at = 0
        for item in pack:
            if item == RIGHT:
                rows = right
            else:
                rows = left_all[pl.ds((own ^ item) * mine, mine)].reshape(mine * seqs, LANES)
            out[at : at + rows.shape[0], :] = rows
            at += rows.shape[0]


def weights_kernel(w_hbm, wide_ref, w_ref, wf_ref, sem, *, parts, hidden):
    copy = pltpu.make_async_copy(w_hbm, w_ref, sem)
    copy.start()
    cz = w_ref.shape[1]
    per = LANES // hidden
    minor = hidden // parts
    own = lax.axis_index("narrow")
    wide_ref[...] = jnp.zeros_like(wide_ref)
    copy.wait()
    wf_ref[...] = w_ref[...].astype(jnp.float32)
    for e in range(hidden):
        rows = wf_ref[pl.ds(e ^ (own * minor), hidden, stride=hidden), :].astype(jnp.bfloat16)
        for k in range(per):
            wide_ref[pl.ds(e * LANES + k * hidden, hidden), k * cz : (k + 1) * cz] = rows


def pair_rows(left_of, right_of, wide_ref, shift_ref, outer_ref, store, *, wides, parts, minor, seqs_total):
    cz = shift_ref.shape[0]
    per = LANES // (minor * parts)
    seqs = LANES // parts
    groups = left_of(0).shape[0] // seqs
    residues = right_of(0, 0).shape[0] // minor
    cols = wides * residues
    lefts = [left_of(m) for m in range(parts)]
    slot = iota((minor * residues, LANES), 1) // seqs
    for q in range(parts):
        left = jnp.concatenate(
            [
                jnp.concatenate([lefts[q ^ k][g * seqs : (g + 1) * seqs] for k in range(parts)], axis=0)
                for g in range(groups)
            ],
            axis=1,
        )
        for d in range(wides):
            right = None
            for k in range(parts):
                chunk = right_of(d, q ^ k)
                right = chunk if right is None else jnp.where(slot == k, chunk, right)
            outer = jnp.dot(right, left, preferred_element_type=jnp.float32).astype(jnp.bfloat16)
            for e in range(minor):
                for g in range(groups):
                    outer_ref[
                        pl.ds(g * cols + d * residues, residues),
                        (q * minor + e) * LANES : (q * minor + e + 1) * LANES,
                    ] = outer[e * residues : (e + 1) * residues, g * LANES : (g + 1) * LANES]

    shift = shift_ref[...].reshape(1, cz)
    pairs = jnp.dot(outer_ref[...], wide_ref[...], preferred_element_type=jnp.float32)
    for g in range(groups):
        for k in range(per):
            pair = pairs[g * cols : (g + 1) * cols, k * cz : (k + 1) * cz]
            store(g * per + k, pair * (1.0 / seqs_total) + shift)


def pair_kernel(*refs, places, block, **sizes):
    wide_ref, shift_ref = refs[-7:-5] if block else refs[-6:-4]
    out_hbm, outer_ref, done_ref, sem = refs[-4:]
    parts, minor = sizes["parts"], sizes["minor"]
    residues = done_ref.shape[1]
    count = done_ref.shape[0] * minor * parts // LANES * (LANES // parts)

    def left_of(m):
        ref, at = places[m][:2]
        return refs[ref][at : at + count, :]

    def right_of(d, m):
        ref, at = places[m][2:]
        return refs[ref][at : at + minor * residues, :]

    def store(row, pair):
        done_ref[row] = pair.astype(done_ref.dtype)

    pair_rows(left_of, right_of, wide_ref, shift_ref, outer_ref, store, wides=1, **sizes)
    at = pl.multiple_of((lax.axis_index("wide") ^ block) * residues, 16)
    copy = pltpu.make_async_copy(done_ref, out_hbm.at[:, pl.ds(at, residues), :], sem)
    copy.start()
    copy.wait()


def pair_blocks_kernel(*refs, wides, parts, minor, **sizes):
    left_refs, (right_ref, wide_ref, shift_ref, out_ref, outer_ref) = refs[:parts], refs[parts:]

    def store(row, pair):
        out_ref[row] = pair.astype(out_ref.dtype)

    pair_rows(
        lambda m: left_refs[m][...], lambda d, m: right_ref[d, m], wide_ref, shift_ref, outer_ref, store,
        wides=wides, parts=parts, minor=minor, **sizes,
    )


def on_device(wide, narrow, x, gain, bias, lm, lb, rm, rb, w, shift):
    seqs, residues, depth = x.shape
    hidden = lm.shape[1]
    cz = w.shape[1]
    per = LANES // hidden
    slots = LANES // seqs
    minor = hidden // slots
    own_rows = residues // narrow
    groups = own_rows // per
    pieces = 4
    hbm = pl.BlockSpec(memory_space=pltpu.HBM)
    vmem = pl.BlockSpec(memory_space=pltpu.VMEM)
    params = pltpu.CompilerParams(vmem_limit_bytes=VMEM_LIMIT)
    direct = wide == 4 and narrow == 4
    if direct:
        packs = ((0,), (RIGHT,), (1, RIGHT), (2, 3, RIGHT))
    else:
        packs = tuple((m,) for m in range(narrow)) + ((RIGHT,),)
    left_count, right_count = groups * seqs, minor * residues
    args = (x, gain, bias, lm.T, lb, rm.T, rb)
    made = pl.pallas_call(
        functools.partial(features_kernel, packs=packs, parts=narrow, pieces=pieces),
        out_shape=tuple(
            jax.ShapeDtypeStruct(
                (sum(right_count if i == RIGHT else left_count for i in pack), LANES), jnp.bfloat16
            )
            for pack in packs
        ),
        in_specs=[hbm] * len(args),
        out_specs=(vmem,) * len(packs),
        scratch_shapes=[pltpu.VMEM(a.shape, a.dtype) for a in args]
        + [
            pltpu.VMEM((seqs * residues, LANES), jnp.float32),
            pltpu.VMEM((seqs * residues, LANES), jnp.float32),
            pltpu.VMEM((residues // per, seqs, LANES), jnp.bfloat16),
            pltpu.VMEM((LANES, LANES), jnp.float32),
            pltpu.VMEM((minor * residues, LANES), jnp.float32),
            pltpu.SemaphoreType.DMA((pieces + len(args) - 1,)),
        ],
        compiler_params=pltpu.CompilerParams(vmem_limit_bytes=VMEM_ALL),
        name="features",
    )(*args)

    block_weights = pl.pallas_call(
        functools.partial(weights_kernel, parts=narrow, hidden=hidden),
        out_shape=jax.ShapeDtypeStruct((hidden * LANES, per * cz), jnp.bfloat16),
        in_specs=[hbm],
        out_specs=vmem,
        scratch_shapes=[
            pltpu.VMEM(w.shape, w.dtype),
            pltpu.VMEM(w.shape, jnp.float32),
            pltpu.SemaphoreType.DMA,
        ],
        compiler_params=params,
        name="block_weights",
    )(w)

    def across(a, m):
        return lax.ppermute(a, "narrow", [(i, i ^ m) for i in range(narrow)])

    def along(a, d):
        return lax.ppermute(a, "wide", [(i, i ^ d) for i in range(wide)])

    sizes = dict(parts=narrow, minor=minor, seqs_total=seqs * narrow)
    out_shape = jax.ShapeDtypeStruct((own_rows, wide * residues, cz), jnp.bfloat16)
    if direct:
        return pairs_by_block(made, across, along, block_weights, shift, out_shape, residues, sizes, params)

    lefts = [made[0]] + [across(made[m], m) for m in range(1, narrow)]
    every = lax.all_gather(made[narrow], ("wide", "narrow"), axis=0, tiled=False)
    every = every.reshape(wide, narrow, right_count, LANES)
    every = jnp.take(every, lax.axis_index("narrow") ^ jnp.arange(narrow), axis=1)
    block = wide
    while block % 2 == 0 and block * residues > 192:
        block //= 2
    cols = block * residues
    return pl.pallas_call(
        functools.partial(pair_blocks_kernel, wides=block, **sizes),
        grid=(wide // block,),
        in_specs=[pl.BlockSpec((left_count, LANES), lambda b: (0, 0))] * narrow
        + [
            pl.BlockSpec((block, narrow, right_count, LANES), lambda b: (b, 0, 0, 0)),
            pl.BlockSpec((hidden * LANES, per * cz), lambda b: (0, 0)),
            pl.BlockSpec((cz,), lambda b: (0,)),
        ],
        out_specs=pl.BlockSpec((own_rows, cols, cz), lambda b: (0, b, 0)),
        out_shape=out_shape,
        scratch_shapes=[pltpu.VMEM((groups * cols, hidden * LANES), jnp.bfloat16)],
        compiler_params=params,
        name="pairs",
    )(*lefts, every, block_weights, shift)


def pairs_by_block(made, across, along, block_weights, shift, out_shape, residues, sizes, params):
    left_own, right, to_core, to_chip = made
    far = {d: along(right, d) for d in (2, 3, 1)}
    left_count, right_count = left_own.shape[0], right.shape[0]
    chip = across(to_chip, 2)
    core = across(to_core, 1)
    both = across(chip, 1)

    hbm = pl.BlockSpec(memory_space=pltpu.HBM)
    vmem = pl.BlockSpec(memory_space=pltpu.VMEM)
    own_rows, cols, cz = out_shape.shape
    hidden = sizes["parts"] * sizes["minor"]
    out = None
    for d in range(cols // residues):
        operands = [left_own, core, chip, both]
        if d == 0:
            operands.append(right)
            rights = ((4, 0), (1, left_count), (2, 2 * left_count), (3, 2 * left_count))
        else:
            other = across(far[d], 2)
            operands += [far[d], across(far[d], 1), other, across(other, 1)]
            rights = tuple((4 + m, 0) for m in range(4))
        places = tuple(
            (m, left_count if m == 3 else 0) + rights[m] for m in range(4)
        )
        operands += [block_weights, shift]
        specs = [vmem] * len(operands)
        aliases = {}
        if out is not None:
            aliases = {len(operands): 0}
            operands.append(out)
            specs.append(hbm)
        out = pl.pallas_call(
            functools.partial(pair_kernel, places=places, block=d, **sizes),
            out_shape=out_shape,
            in_specs=specs,
            out_specs=hbm,
            input_output_aliases=aliases,
            scratch_shapes=[
                pltpu.VMEM((own_rows * hidden // LANES * residues, hidden * LANES), jnp.bfloat16),
                pltpu.VMEM((own_rows, residues, cz), jnp.bfloat16),
                pltpu.SemaphoreType.DMA,
            ],
            compiler_params=params,
            cost_estimate=pl.CostEstimate(flops=1_500_000_000, bytes_accessed=5_000_000, transcendentals=0),
            name=f"pairs_{d}",
        )(*operands)
    return out


def solution(mesh):
    in_specs = (P(("groups", "narrow"), "wide", None), P(), P(), P(), P(), P(), P(), P(), P())
    out_specs = P(("groups", "wide", "narrow"), None, None)
    return jax.shard_map(
        functools.partial(on_device, mesh.shape["wide"], mesh.shape["narrow"]),
        mesh=mesh,
        in_specs=in_specs,
        out_specs=out_specs,
        check_vma=False,
    )
```

```python
import functools

import jax
import jax.numpy as jnp
from jax import lax
from jax.experimental import pallas as pl
from jax.experimental.pallas import tpu as pltpu
from jax.sharding import PartitionSpec as P

LANES = 128
VMEM_LIMIT = 40 * 1024 * 1024
VMEM_ALL = 62 * 1024 * 1024


def iota(shape, dim):
    return lax.broadcasted_iota(jnp.int32, shape, dim)


def features_kernel(
    x_hbm, gain_hbm, bias_hbm, lm_hbm, lb_hbm, rm_hbm, rb_hbm,
    *refs, halves, pieces,
):
    left_ref, right_refs = refs[0], refs[1 : 1 + halves]
    (x_ref, gain_ref, bias_ref, lm_ref, lb_ref, rm_ref, rb_ref,
     lo_ref, hi_ref, turned_ref, rows_ref, sems) = refs[1 + halves :]
    seqs, residues, depth = x_ref.shape
    hidden = lm_ref.shape[0]
    per = LANES // hidden
    slots = LANES // seqs
    minor = hidden // slots
    groups = residues // per
    own = lax.axis_index("narrow")

    piece = seqs // pieces
    copies = [
        pltpu.make_async_copy(
            x_hbm.at[pl.ds(p * piece, piece)], x_ref.at[pl.ds(p * piece, piece)], sems.at[p]
        )
        for p in range(pieces)
    ]
    small = ((gain_hbm, gain_ref), (bias_hbm, bias_ref), (lm_hbm, lm_ref),
             (lb_hbm, lb_ref), (rm_hbm, rm_ref), (rb_hbm, rb_ref))
    rest = [pltpu.make_async_copy(a, b, sems.at[pieces + i]) for i, (a, b) in enumerate(small)]
    copies[0].start()
    for copy in rest:
        copy.start()
    for copy in copies[1:]:
        copy.start()
    for copy in rest:
        copy.wait()

    column, row = iota((hidden, LANES), 1) % hidden, iota((hidden, LANES), 0)
    spread_l = (column == row).astype(jnp.float32)
    spread_r = (column == (row ^ (own * minor))).astype(jnp.float32)

    def widen(m, pick):
        return lax.dot_general(
            m, pick.astype(jnp.bfloat16), (((0,), (0,)), ((), ())),
            preferred_element_type=jnp.float32,
        )

    def widen_bias(b, pick):
        b = jnp.broadcast_to(b.reshape(1, hidden), (8, hidden))
        return jnp.dot(
            b, pick, precision=lax.Precision.HIGHEST, preferred_element_type=jnp.float32
        )[:1]

    weights = jnp.concatenate(
        [widen(lm_ref[...], spread_l), widen(rm_ref[...], spread_r)], axis=1
    )
    shift = jnp.concatenate(
        [widen_bias(lb_ref[...], spread_l), widen_bias(rb_ref[...], spread_r)], axis=1
    )
    place = iota((depth, 2 * LANES), 1) % LANES // hidden

    gain = gain_ref[...].reshape(1, depth)
    bias = bias_ref[...].reshape(1, depth)
    step = 4
    for s in range(0, seqs, step):
        if s % piece == 0:
            copies[s // piece].wait()
        x = x_ref[s : s + step].reshape(step * residues, depth).astype(jnp.float32)
        x = x - jnp.mean(x, axis=-1, keepdims=True)
        spread = jnp.mean(x * x, axis=-1, keepdims=True)
        x = x * lax.rsqrt(spread + 1e-05) * gain + bias
        rows = pl.ds(s * residues, step * residues)
        lo_ref[rows, :] = x[:, :LANES]
        hi_ref[rows, :] = x[:, LANES:]

    total = None
    for k in range(per):
        part = jnp.concatenate(
            [
                jnp.concatenate(
                    [half[pl.ds(g * per + k, seqs, stride=residues), :] for half in (lo_ref, hi_ref)],
                    axis=1,
                )
                for g in range(groups)
            ],
            axis=0,
        ).astype(jnp.bfloat16)
        placed = jnp.where(place == k, weights, 0.0).astype(jnp.bfloat16)
        term = jnp.dot(part, placed, preferred_element_type=jnp.float32)
        total = term if total is None else total + term
    total = total + shift
    left_ref[...] = total[:, :LANES].astype(left_ref.dtype).reshape(left_ref.shape)

    slot = iota((minor, LANES), 1) // seqs
    for block in range(groups // slots):
        turned_ref[...] = total[block * LANES : (block + 1) * LANES, LANES:].T
        for k in range(per):
            parts_of = [turned_ref[pl.ds(k * hidden + q * minor, minor), :] for q in range(slots)]
            for g in range(slots):
                out = None
                for q in range(slots):
                    moved = parts_of[q]
                    if q != g:
                        moved = pltpu.roll(moved, (q - g) % slots * seqs, axis=1)
                    out = moved if out is None else jnp.where(slot == q, moved, out)
                j = (block * slots + g) * per + k
                rows_ref[pl.ds(j, minor, stride=residues), :] = out
    right = rows_ref[...].astype(jnp.bfloat16)
    count = minor * residues // halves
    for h, right_ref in enumerate(right_refs):
        for copy in range(right_ref.shape[0]):
            right_ref[copy] = right[h * count : (h + 1) * count]


def weights_kernel(w_hbm, wide_ref, w_ref, wf_ref, sem, *, parts, hidden, halves):
    copy = pltpu.make_async_copy(w_hbm, w_ref, sem)
    copy.start()
    cz = w_ref.shape[1]
    per = LANES // hidden
    minor = hidden // parts
    count = minor // halves
    own = lax.axis_index("narrow")
    wide_ref[...] = jnp.zeros_like(wide_ref)
    copy.wait()
    wf_ref[...] = w_ref[...].astype(jnp.float32)
    for e in range(hidden):
        q, h, i = e // minor, e % minor // count, e % count
        rows = wf_ref[pl.ds(e ^ (own * minor), hidden, stride=hidden), :].astype(jnp.bfloat16)
        for k in range(per):
            at = ((h * parts + q) * count + i) * LANES + k * hidden
            wide_ref[at : at + hidden, k * cz : (k + 1) * cz] = rows


def outer_rows(left_ref, right_of, outer_ref, *, wides, parts, minor):
    seqs = LANES // parts
    own = lax.axis_index("narrow")
    lefts = [left_ref[own ^ m] for m in range(parts)]
    groups = lefts[0].shape[0] // seqs
    residues = right_of(0, 0).shape[0] // minor
    cols = wides * residues
    slot = iota((minor * residues, LANES), 1) // seqs
    for q in range(parts):
        left = jnp.concatenate(
            [
                jnp.concatenate([lefts[q ^ k][g * seqs : (g + 1) * seqs] for k in range(parts)], axis=0)
                for g in range(groups)
            ],
            axis=1,
        )
        for d in range(wides):
            right = None
            for k in range(parts):
                chunk = right_of(d, q ^ k)
                right = chunk if right is None else jnp.where(slot == k, chunk, right)
            outer = jnp.dot(right, left, preferred_element_type=jnp.float32).astype(jnp.bfloat16)
            for e in range(minor):
                for g in range(groups):
                    outer_ref[
                        pl.ds(g * cols + d * residues, residues),
                        (q * minor + e) * LANES : (q * minor + e + 1) * LANES,
                    ] = outer[e * residues : (e + 1) * residues, g * LANES : (g + 1) * LANES]


def sums_kernel(left_ref, *refs, part, **sizes):
    rights, (wide_ref, sums_ref, outer_ref) = refs[: sizes["parts"]], refs[sizes["parts"] :]
    outer_rows(left_ref, lambda d, m: rights[m][d], outer_ref, **sizes)
    depth = outer_ref.shape[1]
    sums_ref[...] = jnp.dot(
        outer_ref[...], wide_ref[part * depth : (part + 1) * depth], preferred_element_type=jnp.float32
    )


def pairs_kernel(left_ref, *refs, part, seqs_total, **sizes):
    rights, refs = refs[: sizes["parts"]], refs[sizes["parts"] :]
    wide_ref, sums_ref, shift_ref, out_hbm, outer_ref, done_ref, sems = refs
    outer_rows(left_ref, lambda d, m: rights[m][d], outer_ref, **sizes)
    depth = outer_ref.shape[1]
    own_rows, cols, cz = done_ref.shape
    per = wide_ref.shape[1] // cz
    shift = shift_ref[...].reshape(1, cz)
    copies = []
    for g in range(own_rows // per):
        rows = slice(g * cols, (g + 1) * cols)
        pairs = sums_ref[rows] + jnp.dot(
            outer_ref[rows], wide_ref[part * depth : (part + 1) * depth], preferred_element_type=jnp.float32
        )
        for k in range(per):
            pair = pairs[:, k * cz : (k + 1) * cz] * (1.0 / seqs_total) + shift
            done_ref[g * per + k] = pair.astype(done_ref.dtype)
        copies.append(
            pltpu.make_async_copy(
                done_ref.at[pl.ds(g * per, per)], out_hbm.at[pl.ds(g * per, per)], sems.at[g]
            )
        )
        copies[-1].start()
    for copy in copies:
        copy.wait()


def pair_blocks_kernel(left_ref, right_ref, wide_ref, shift_ref, out_ref, outer_ref, *, seqs_total, **sizes):
    outer_rows(left_ref, lambda d, m: right_ref[d, m], outer_ref, **sizes)
    own_rows, cols, cz = out_ref.shape
    per = wide_ref.shape[1] // cz
    shift = shift_ref[...].reshape(1, cz)
    for g in range(own_rows // per):
        pairs = jnp.dot(
            outer_ref[pl.ds(g * cols, cols), :], wide_ref[...], preferred_element_type=jnp.float32
        )
        for k in range(per):
            pair = pairs[:, k * cz : (k + 1) * cz] * (1.0 / seqs_total) + shift
            out_ref[g * per + k] = pair.astype(out_ref.dtype)


def on_device(wide, narrow, x, gain, bias, lm, lb, rm, rb, w, shift):
    seqs, residues, depth = x.shape
    hidden = lm.shape[1]
    cz = w.shape[1]
    per = LANES // hidden
    slots = LANES // seqs
    minor = hidden // slots
    own_rows = residues // narrow
    groups = own_rows // per
    pieces = 4
    hbm = pl.BlockSpec(memory_space=pltpu.HBM)
    vmem = pl.BlockSpec(memory_space=pltpu.VMEM)
    params = pltpu.CompilerParams(vmem_limit_bytes=VMEM_LIMIT)
    direct = wide * narrow <= 16
    halves, copies = (2, wide) if direct else (1, 1)
    count = minor // halves
    args = (x, gain, bias, lm.T, lb, rm.T, rb)
    left, *rights = pl.pallas_call(
        functools.partial(features_kernel, halves=halves, pieces=pieces),
        out_shape=(jax.ShapeDtypeStruct((narrow, groups * seqs, LANES), jnp.bfloat16),)
        + (jax.ShapeDtypeStruct((copies, count * residues, LANES), jnp.bfloat16),) * halves,
        in_specs=[hbm] * len(args),
        out_specs=(vmem,) * (1 + halves),
        scratch_shapes=[pltpu.VMEM(a.shape, a.dtype) for a in args]
        + [
            pltpu.VMEM((seqs * residues, LANES), jnp.float32),
            pltpu.VMEM((seqs * residues, LANES), jnp.float32),
            pltpu.VMEM((LANES, LANES), jnp.float32),
            pltpu.VMEM((minor * residues, LANES), jnp.float32),
            pltpu.SemaphoreType.DMA((pieces + len(args) - 1,)),
        ],
        compiler_params=pltpu.CompilerParams(vmem_limit_bytes=VMEM_ALL),
        name="features",
    )(*args)

    block_weights = pl.pallas_call(
        functools.partial(weights_kernel, parts=narrow, hidden=hidden, halves=halves),
        out_shape=jax.ShapeDtypeStruct((hidden * LANES, per * cz), jnp.bfloat16),
        in_specs=[hbm],
        out_specs=vmem,
        scratch_shapes=[
            pltpu.VMEM(w.shape, w.dtype),
            pltpu.VMEM(w.shape, jnp.float32),
            pltpu.SemaphoreType.DMA,
        ],
        compiler_params=params,
        name="block_weights",
    )(w)

    out_shape = jax.ShapeDtypeStruct((own_rows, wide * residues, cz), jnp.bfloat16)
    if direct:
        held = []
        for right in rights:
            chunks = [lax.all_to_all(right, "wide", split_axis=0, concat_axis=0, tiled=True)]
            bit, order = narrow // 2, [0]
            while bit:
                chunks += [lax.ppermute(c, "narrow", [(i, i ^ bit) for i in range(narrow)]) for c in chunks]
                order += [m ^ bit for m in order]
                bit //= 2
            held.append([chunks[order.index(m)] for m in range(narrow)])
        left = lax.all_to_all(left, "narrow", split_axis=0, concat_axis=0, tiled=True)
        sizes = dict(wides=wide, parts=narrow, minor=count)
        cols = wide * residues
        cost = pl.CostEstimate(flops=2_000_000_000, bytes_accessed=5_000_000, transcendentals=0)
        outer = pltpu.VMEM((groups * cols, narrow * count * LANES), jnp.bfloat16)
        sums = pl.pallas_call(
            functools.partial(sums_kernel, part=0, **sizes),
            out_shape=jax.ShapeDtypeStruct((groups * cols, per * cz), jnp.float32),
            in_specs=[vmem] * (2 + narrow),
            out_specs=vmem,
            scratch_shapes=[outer],
            compiler_params=params,
            cost_estimate=cost,
            name="sums",
        )(left, *held[0], block_weights)
        return pl.pallas_call(
            functools.partial(pairs_kernel, part=1, seqs_total=seqs * narrow, **sizes),
            out_shape=out_shape,
            in_specs=[vmem] * (4 + narrow),
            out_specs=hbm,
            scratch_shapes=[
                outer, pltpu.VMEM(out_shape.shape, out_shape.dtype), pltpu.SemaphoreType.DMA((groups,))
            ],
            compiler_params=params,
            cost_estimate=cost,
            name="pairs",
        )(left, *held[1], block_weights, sums, shift)

    left = lax.all_to_all(left, "narrow", split_axis=0, concat_axis=0, tiled=True)
    every = lax.all_gather(rights[0][0], ("wide", "narrow"), axis=0, tiled=False)
    every = every.reshape(wide, narrow, minor * residues, LANES)
    every = jnp.take(every, lax.axis_index("narrow") ^ jnp.arange(narrow), axis=1)
    block = wide
    while block % 2 == 0 and block * residues > 192:
        block //= 2
    cols = block * residues
    return pl.pallas_call(
        functools.partial(
            pair_blocks_kernel, wides=block, parts=narrow, minor=minor, seqs_total=seqs * narrow
        ),
        grid=(wide // block,),
        in_specs=[
            pl.BlockSpec(left.shape, lambda b: (0, 0, 0)),
            pl.BlockSpec((block, narrow, minor * residues, LANES), lambda b: (b, 0, 0, 0)),
            pl.BlockSpec((hidden * LANES, per * cz), lambda b: (0, 0)),
            pl.BlockSpec((cz,), lambda b: (0,)),
        ],
        out_specs=pl.BlockSpec((own_rows, cols, cz), lambda b: (0, b, 0)),
        out_shape=out_shape,
        scratch_shapes=[pltpu.VMEM((groups * cols, hidden * LANES), jnp.bfloat16)],
        compiler_params=params,
        name="pairs",
    )(left, every, block_weights, shift)


def solution(mesh):
    in_specs = (P(("groups", "narrow"), "wide", None), P(), P(), P(), P(), P(), P(), P(), P())
    out_specs = P(("groups", "wide", "narrow"), None, None)
    return jax.shard_map(
        functools.partial(on_device, mesh.shape["wide"], mesh.shape["narrow"]),
        mesh=mesh,
        in_specs=in_specs,
        out_specs=out_specs,
        check_vma=False,
    )
```

```python
import functools

import jax
import jax.numpy as jnp
from jax import lax
from jax.experimental import pallas as pl
from jax.experimental.pallas import tpu as pltpu
from jax.sharding import PartitionSpec as P

LANES = 128
RIGHT = -1
VMEM_LIMIT = 40 * 1024 * 1024
VMEM_ALL = 62 * 1024 * 1024


def iota(shape, dim):
    return lax.broadcasted_iota(jnp.int32, shape, dim)


def features_kernel(
    x_hbm, gain_hbm, bias_hbm, lm_hbm, lb_hbm, rm_hbm, rb_hbm,
    *refs, packs, parts, pieces,
):
    outs = refs[: len(packs)]
    (x_ref, gain_ref, bias_ref, lm_ref, lb_ref, rm_ref, rb_ref,
     lo_ref, hi_ref, left_all, turned_ref, rows_ref, sems) = refs[len(packs) :]
    seqs, residues, depth = x_ref.shape
    hidden = lm_ref.shape[0]
    per = LANES // hidden
    slots = LANES // seqs
    minor = hidden // slots
    groups = residues // per
    own = lax.axis_index("narrow")

    piece = seqs // pieces
    copies = [
        pltpu.make_async_copy(
            x_hbm.at[pl.ds(p * piece, piece)], x_ref.at[pl.ds(p * piece, piece)], sems.at[p]
        )
        for p in range(pieces)
    ]
    small = ((gain_hbm, gain_ref), (bias_hbm, bias_ref), (lm_hbm, lm_ref),
             (lb_hbm, lb_ref), (rm_hbm, rm_ref), (rb_hbm, rb_ref))
    rest = [pltpu.make_async_copy(a, b, sems.at[pieces + i]) for i, (a, b) in enumerate(small)]
    copies[0].start()
    for copy in rest:
        copy.start()
    for copy in copies[1:]:
        copy.start()
    for copy in rest:
        copy.wait()

    column, row = iota((hidden, LANES), 1) % hidden, iota((hidden, LANES), 0)
    spread_l = (column == row).astype(jnp.float32)
    spread_r = (column == (row ^ (own * minor))).astype(jnp.float32)

    def widen(m, pick):
        return lax.dot_general(
            m, pick.astype(jnp.bfloat16), (((0,), (0,)), ((), ())),
            preferred_element_type=jnp.float32,
        )

    def widen_bias(b, pick):
        b = jnp.broadcast_to(b.reshape(1, hidden), (8, hidden))
        return jnp.dot(
            b, pick, precision=lax.Precision.HIGHEST, preferred_element_type=jnp.float32
        )[:1]

    weights = jnp.concatenate(
        [widen(lm_ref[...], spread_l), widen(rm_ref[...], spread_r)], axis=1
    )
    shift = jnp.concatenate(
        [widen_bias(lb_ref[...], spread_l), widen_bias(rb_ref[...], spread_r)], axis=1
    )
    place = iota((depth, 2 * LANES), 1) % LANES // hidden

    gain = gain_ref[...].reshape(1, depth)
    bias = bias_ref[...].reshape(1, depth)
    step = 4
    for s in range(0, seqs, step):
        if s % piece == 0:
            copies[s // piece].wait()
        x = x_ref[s : s + step].reshape(step * residues, depth).astype(jnp.float32)
        x = x - jnp.mean(x, axis=-1, keepdims=True)
        spread = jnp.mean(x * x, axis=-1, keepdims=True)
        x = x * lax.rsqrt(spread + 1e-05) * gain + bias
        rows = pl.ds(s * residues, step * residues)
        lo_ref[rows, :] = x[:, :LANES]
        hi_ref[rows, :] = x[:, LANES:]

    total = None
    for k in range(per):
        part = jnp.concatenate(
            [
                jnp.concatenate(
                    [half[pl.ds(g * per + k, seqs, stride=residues), :] for half in (lo_ref, hi_ref)],
                    axis=1,
                )
                for g in range(groups)
            ],
            axis=0,
        ).astype(jnp.bfloat16)
        placed = jnp.where(place == k, weights, 0.0).astype(jnp.bfloat16)
        term = jnp.dot(part, placed, preferred_element_type=jnp.float32)
        total = term if total is None else total + term
    total = total + shift
    left_all[...] = total[:, :LANES].astype(left_all.dtype).reshape(groups, seqs, LANES)
    mine = groups // parts

    slot = iota((minor, LANES), 1) // seqs
    for block in range(groups // slots):
        turned_ref[...] = total[block * LANES : (block + 1) * LANES, LANES:].T
        for k in range(per):
            parts_of = [turned_ref[pl.ds(k * hidden + q * minor, minor), :] for q in range(slots)]
            for g in range(slots):
                out = None
                for q in range(slots):
                    moved = parts_of[q]
                    if q != g:
                        moved = pltpu.roll(moved, (q - g) % slots * seqs, axis=1)
                    out = moved if out is None else jnp.where(slot == q, moved, out)
                j = (block * slots + g) * per + k
                rows_ref[pl.ds(j, minor, stride=residues), :] = out
    right = rows_ref[...].astype(jnp.bfloat16)
    for out, pack in zip(outs, packs):
        at = 0
        for item in pack:
            if item == RIGHT:
                rows = right
            else:
                rows = left_all[pl.ds((own ^ item) * mine, mine)].reshape(mine * seqs, LANES)
            out[at : at + rows.shape[0], :] = rows
            at += rows.shape[0]


def weights_kernel(w_hbm, after_ref, wide_ref, w_ref, wf_ref, sem, *, parts, hidden):
    del after_ref
    copy = pltpu.make_async_copy(w_hbm, w_ref, sem)
    copy.start()
    cz = w_ref.shape[1]
    per = LANES // hidden
    minor = hidden // parts
    own = lax.axis_index("narrow")
    wide_ref[...] = jnp.zeros_like(wide_ref)
    copy.wait()
    wf_ref[...] = w_ref[...].astype(jnp.float32)
    for e in range(hidden):
        rows = wf_ref[pl.ds(e ^ (own * minor), hidden, stride=hidden), :].astype(jnp.bfloat16)
        for k in range(per):
            wide_ref[pl.ds(e * LANES + k * hidden, hidden), k * cz : (k + 1) * cz] = rows


def pack_kernel(first_ref, second_ref, after_ref, out_ref):
    del after_ref
    count = first_ref.shape[0]
    out_ref[:count] = first_ref[...]
    out_ref[count:] = second_ref[...]


def pair_rows(left_of, right_of, wide_ref, shift_ref, outer_ref, store, *, wides, parts, minor, seqs_total):
    cz = shift_ref.shape[0]
    per = LANES // (minor * parts)
    seqs = LANES // parts
    groups = left_of(0).shape[0] // seqs
    residues = right_of(0, 0).shape[0] // minor
    cols = wides * residues
    lefts = [left_of(m) for m in range(parts)]
    slot = iota((minor * residues, LANES), 1) // seqs
    for q in range(parts):
        left = jnp.concatenate(
            [
                jnp.concatenate([lefts[q ^ k][g * seqs : (g + 1) * seqs] for k in range(parts)], axis=0)
                for g in range(groups)
            ],
            axis=1,
        )
        for d in range(wides):
            right = None
            for k in range(parts):
                chunk = right_of(d, q ^ k)
                right = chunk if right is None else jnp.where(slot == k, chunk, right)
            outer = jnp.dot(right, left, preferred_element_type=jnp.float32).astype(jnp.bfloat16)
            for e in range(minor):
                for g in range(groups):
                    outer_ref[
                        pl.ds(g * cols + d * residues, residues),
                        (q * minor + e) * LANES : (q * minor + e + 1) * LANES,
                    ] = outer[e * residues : (e + 1) * residues, g * LANES : (g + 1) * LANES]

    shift = shift_ref[...].reshape(1, cz)
    pairs = jnp.dot(outer_ref[...], wide_ref[...], preferred_element_type=jnp.float32)
    for g in range(groups):
        for k in range(per):
            pair = pairs[g * cols : (g + 1) * cols, k * cz : (k + 1) * cz]
            store(g * per + k, pair * (1.0 / seqs_total) + shift)


def pair_kernel(*refs, places, blocks, **sizes):
    out_hbm, outer_ref, done_ref, sems = refs[-4:]
    wide_ref, shift_ref = refs[sizes.pop("operands") : ][:2]
    parts, minor = sizes["parts"], sizes["minor"]
    own_rows, cols, _ = done_ref.shape
    residues = cols // len(blocks)
    left_count = own_rows * minor
    right_count = minor * residues

    def left_of(m):
        ref, at = places[m][:2]
        return refs[ref][at : at + left_count, :]

    def right_of(d, m):
        ref, at = places[m][2:]
        return refs[ref][at + d * right_count : at + (d + 1) * right_count, :]

    def store(row, pair):
        done_ref[row] = pair.astype(done_ref.dtype)

    pair_rows(left_of, right_of, wide_ref, shift_ref, outer_ref, store, wides=len(blocks), **sizes)
    copies = []
    for d, block in enumerate(blocks):
        at = pl.multiple_of((lax.axis_index("wide") ^ block) * residues, 16)
        copies.append(
            pltpu.make_async_copy(
                done_ref.at[:, pl.ds(d * residues, residues), :],
                out_hbm.at[:, pl.ds(at, residues), :],
                sems.at[d],
            )
        )
        copies[-1].start()
    for copy in copies:
        copy.wait()


def pair_blocks_kernel(*refs, wides, parts, minor, **sizes):
    left_refs, (right_ref, wide_ref, shift_ref, out_ref, outer_ref) = refs[:parts], refs[parts:]

    def store(row, pair):
        out_ref[row] = pair.astype(out_ref.dtype)

    pair_rows(
        lambda m: left_refs[m][...], lambda d, m: right_ref[d, m], wide_ref, shift_ref, outer_ref, store,
        wides=wides, parts=parts, minor=minor, **sizes,
    )


def on_device(wide, narrow, x, gain, bias, lm, lb, rm, rb, w, shift):
    seqs, residues, depth = x.shape
    hidden = lm.shape[1]
    cz = w.shape[1]
    per = LANES // hidden
    slots = LANES // seqs
    minor = hidden // slots
    own_rows = residues // narrow
    groups = own_rows // per
    pieces = 4
    hbm = pl.BlockSpec(memory_space=pltpu.HBM)
    vmem = pl.BlockSpec(memory_space=pltpu.VMEM)
    params = pltpu.CompilerParams(vmem_limit_bytes=VMEM_LIMIT)
    direct = wide == 4 and narrow == 4
    if direct:
        packs = ((0,), (RIGHT,), (1, RIGHT), (2, 3, RIGHT))
    else:
        packs = tuple((m,) for m in range(narrow)) + ((RIGHT,),)
    left_count, right_count = groups * seqs, minor * residues
    args = (x, gain, bias, lm.T, lb, rm.T, rb)
    made = pl.pallas_call(
        functools.partial(features_kernel, packs=packs, parts=narrow, pieces=pieces),
        out_shape=tuple(
            jax.ShapeDtypeStruct(
                (sum(right_count if i == RIGHT else left_count for i in pack), LANES), jnp.bfloat16
            )
            for pack in packs
        ),
        in_specs=[hbm] * len(args),
        out_specs=(vmem,) * len(packs),
        scratch_shapes=[pltpu.VMEM(a.shape, a.dtype) for a in args]
        + [
            pltpu.VMEM((seqs * residues, LANES), jnp.float32),
            pltpu.VMEM((seqs * residues, LANES), jnp.float32),
            pltpu.VMEM((residues // per, seqs, LANES), jnp.bfloat16),
            pltpu.VMEM((LANES, LANES), jnp.float32),
            pltpu.VMEM((minor * residues, LANES), jnp.float32),
            pltpu.SemaphoreType.DMA((pieces + len(args) - 1,)),
        ],
        compiler_params=pltpu.CompilerParams(vmem_limit_bytes=VMEM_ALL),
        name="features",
    )(*args)

    block_weights = pl.pallas_call(
        functools.partial(weights_kernel, parts=narrow, hidden=hidden),
        out_shape=jax.ShapeDtypeStruct((hidden * LANES, per * cz), jnp.bfloat16),
        in_specs=[hbm, pl.BlockSpec(memory_space=pl.ANY)],
        out_specs=vmem,
        scratch_shapes=[
            pltpu.VMEM(w.shape, w.dtype),
            pltpu.VMEM(w.shape, jnp.float32),
            pltpu.SemaphoreType.DMA,
        ],
        compiler_params=params,
        name="block_weights",
    )(w, made[0])

    def across(a, m):
        return lax.ppermute(a, "narrow", [(i, i ^ m) for i in range(narrow)])

    def along(a, d):
        return lax.ppermute(a, "wide", [(i, i ^ d) for i in range(wide)])

    sizes = dict(parts=narrow, minor=minor, seqs_total=seqs * narrow)
    out_shape = jax.ShapeDtypeStruct((own_rows, wide * residues, cz), jnp.bfloat16)
    if direct:
        return pairs_by_block(made, across, along, block_weights, shift, out_shape, residues, sizes, params)

    lefts = [made[0]] + [across(made[m], m) for m in range(1, narrow)]
    every = lax.all_gather(made[narrow], ("wide", "narrow"), axis=0, tiled=False)
    every = every.reshape(wide, narrow, right_count, LANES)
    every = jnp.take(every, lax.axis_index("narrow") ^ jnp.arange(narrow), axis=1)
    block = wide
    while block % 2 == 0 and block * residues > 192:
        block //= 2
    cols = block * residues
    return pl.pallas_call(
        functools.partial(pair_blocks_kernel, wides=block, **sizes),
        grid=(wide // block,),
        in_specs=[pl.BlockSpec((left_count, LANES), lambda b: (0, 0))] * narrow
        + [
            pl.BlockSpec((block, narrow, right_count, LANES), lambda b: (b, 0, 0, 0)),
            pl.BlockSpec((hidden * LANES, per * cz), lambda b: (0, 0)),
            pl.BlockSpec((cz,), lambda b: (0,)),
        ],
        out_specs=pl.BlockSpec((own_rows, cols, cz), lambda b: (0, b, 0)),
        out_shape=out_shape,
        scratch_shapes=[pltpu.VMEM((groups * cols, hidden * LANES), jnp.bfloat16)],
        compiler_params=params,
        name="pairs",
    )(*lefts, every, block_weights, shift)


def pairs_by_block(made, across, along, block_weights, shift, out_shape, residues, sizes, params):
    left_own, right, to_core, to_chip = made
    left_count, right_count = left_own.shape[0], right.shape[0]
    hbm = pl.BlockSpec(memory_space=pltpu.HBM)
    vmem = pl.BlockSpec(memory_space=pltpu.VMEM)
    anywhere = pl.BlockSpec(memory_space=pl.ANY)

    far = along(right, 2)
    near = along(right, 1)
    last = along(far, 1)
    chip = across(to_chip, 2)
    core = across(to_core, 1)
    both = across(chip, 1)
    middle = pl.pallas_call(
        pack_kernel,
        out_shape=jax.ShapeDtypeStruct((2 * right_count, LANES), jnp.bfloat16),
        in_specs=[vmem, vmem, anywhere],
        out_specs=vmem,
        compiler_params=params,
        name="pack",
    )(near, far, block_weights)

    own_rows, _, cz = out_shape.shape
    hidden = sizes["parts"] * sizes["minor"]
    groups = own_rows * hidden // LANES
    out = None
    for blocks, chunk in (((0,), right), ((1, 2), middle), ((3,), last)):
        operands = [left_own, core, chip, both]
        if chunk is right:
            operands.append(right)
            rights = ((4, 0), (1, left_count), (2, 2 * left_count), (3, 2 * left_count))
        else:
            other = across(chunk, 2)
            operands += [chunk, across(chunk, 1), other, across(other, 1)]
            rights = tuple((4 + m, 0) for m in range(4))
        places = tuple((m, left_count if m == 3 else 0) + rights[m] for m in range(4))
        count = len(operands)
        operands += [block_weights, shift]
        specs = [vmem] * len(operands)
        aliases = {}
        if out is not None:
            aliases = {len(operands): 0}
            operands.append(out)
            specs.append(hbm)
        cols = len(blocks) * residues
        out = pl.pallas_call(
            functools.partial(pair_kernel, places=places, blocks=blocks, operands=count, **sizes),
            out_shape=out_shape,
            in_specs=specs,
            out_specs=hbm,
            input_output_aliases=aliases,
            scratch_shapes=[
                pltpu.VMEM((groups * cols, hidden * LANES), jnp.bfloat16),
                pltpu.VMEM((own_rows, cols, cz), jnp.bfloat16),
                pltpu.SemaphoreType.DMA((len(blocks),)),
            ],
            compiler_params=params,
            cost_estimate=pl.CostEstimate(
                flops=1_500_000_000 * len(blocks), bytes_accessed=5_000_000, transcendentals=0
            ),
            name=f"pairs_{blocks[0]}",
        )(*operands)
    return out


def solution(mesh):
    in_specs = (P(("groups", "narrow"), "wide", None), P(), P(), P(), P(), P(), P(), P(), P())
    out_specs = P(("groups", "wide", "narrow"), None, None)
    return jax.shard_map(
        functools.partial(on_device, mesh.shape["wide"], mesh.shape["narrow"]),
        mesh=mesh,
        in_specs=in_specs,
        out_specs=out_specs,
        check_vma=False,
    )
```

```python
import functools

import jax
import jax.numpy as jnp
from jax import lax
from jax.experimental import pallas as pl
from jax.experimental.pallas import tpu as pltpu
from jax.sharding import PartitionSpec as P

LANES = 128
RIGHT = -1
VMEM_LIMIT = 40 * 1024 * 1024
VMEM_ALL = 62 * 1024 * 1024


def iota(shape, dim):
    return lax.broadcasted_iota(jnp.int32, shape, dim)


def features_kernel(
    x_hbm, gain_hbm, bias_hbm, lm_hbm, lb_hbm, rm_hbm, rb_hbm, w_hbm,
    *refs, packs, parts, pieces,
):
    outs, w_ref = refs[: len(packs)], refs[len(packs)]
    (x_ref, gain_ref, bias_ref, lm_ref, lb_ref, rm_ref, rb_ref,
     lo_ref, hi_ref, left_all, turned_ref, rows_ref, sems) = refs[len(packs) + 1 :]
    seqs, residues, depth = x_ref.shape
    hidden = lm_ref.shape[0]
    per = LANES // hidden
    slots = LANES // seqs
    minor = hidden // slots
    groups = residues // per
    own = lax.axis_index("narrow")

    piece = seqs // pieces
    copies = [
        pltpu.make_async_copy(
            x_hbm.at[pl.ds(p * piece, piece)], x_ref.at[pl.ds(p * piece, piece)], sems.at[p]
        )
        for p in range(pieces)
    ]
    small = ((gain_hbm, gain_ref), (bias_hbm, bias_ref), (lm_hbm, lm_ref),
             (lb_hbm, lb_ref), (rm_hbm, rm_ref), (rb_hbm, rb_ref))
    rest = [pltpu.make_async_copy(a, b, sems.at[pieces + i]) for i, (a, b) in enumerate(small)]
    copies[0].start()
    for copy in rest:
        copy.start()
    for copy in copies[1:]:
        copy.start()
    w_copy = pltpu.make_async_copy(w_hbm, w_ref, sems.at[pieces + len(small)])
    w_copy.start()
    for copy in rest:
        copy.wait()

    column, row = iota((hidden, LANES), 1) % hidden, iota((hidden, LANES), 0)
    spread_l = (column == row).astype(jnp.float32)
    spread_r = (column == (row ^ (own * minor))).astype(jnp.float32)

    def widen(m, pick):
        return lax.dot_general(
            m, pick.astype(jnp.bfloat16), (((0,), (0,)), ((), ())),
            preferred_element_type=jnp.float32,
        )

    def widen_bias(b, pick):
        b = jnp.broadcast_to(b.reshape(1, hidden), (8, hidden))
        return jnp.dot(
            b, pick, precision=lax.Precision.HIGHEST, preferred_element_type=jnp.float32
        )[:1]

    weights = jnp.concatenate(
        [widen(lm_ref[...], spread_l), widen(rm_ref[...], spread_r)], axis=1
    )
    shift = jnp.concatenate(
        [widen_bias(lb_ref[...], spread_l), widen_bias(rb_ref[...], spread_r)], axis=1
    )
    place = iota((depth, 2 * LANES), 1) % LANES // hidden

    gain = gain_ref[...].reshape(1, depth)
    bias = bias_ref[...].reshape(1, depth)
    step = 4
    for s in range(0, seqs, step):
        if s % piece == 0:
            copies[s // piece].wait()
        x = x_ref[s : s + step].reshape(step * residues, depth).astype(jnp.float32)
        x = x - jnp.mean(x, axis=-1, keepdims=True)
        spread = jnp.mean(x * x, axis=-1, keepdims=True)
        x = x * lax.rsqrt(spread + 1e-05) * gain + bias
        rows = pl.ds(s * residues, step * residues)
        lo_ref[rows, :] = x[:, :LANES]
        hi_ref[rows, :] = x[:, LANES:]

    total = None
    for k in range(per):
        part = jnp.concatenate(
            [
                jnp.concatenate(
                    [half[pl.ds(g * per + k, seqs, stride=residues), :] for half in (lo_ref, hi_ref)],
                    axis=1,
                )
                for g in range(groups)
            ],
            axis=0,
        ).astype(jnp.bfloat16)
        placed = jnp.where(place == k, weights, 0.0).astype(jnp.bfloat16)
        term = jnp.dot(part, placed, preferred_element_type=jnp.float32)
        total = term if total is None else total + term
    total = total + shift
    left_all[...] = total[:, :LANES].astype(left_all.dtype).reshape(groups, seqs, LANES)
    mine = groups // parts

    slot = iota((minor, LANES), 1) // seqs
    for block in range(groups // slots):
        turned_ref[...] = total[block * LANES : (block + 1) * LANES, LANES:].T
        for k in range(per):
            parts_of = [turned_ref[pl.ds(k * hidden + q * minor, minor), :] for q in range(slots)]
            for g in range(slots):
                out = None
                for q in range(slots):
                    moved = parts_of[q]
                    if q != g:
                        moved = pltpu.roll(moved, (q - g) % slots * seqs, axis=1)
                    out = moved if out is None else jnp.where(slot == q, moved, out)
                j = (block * slots + g) * per + k
                rows_ref[pl.ds(j, minor, stride=residues), :] = out
    right = rows_ref[...].astype(jnp.bfloat16)
    for out, pack in zip(outs, packs):
        at = 0
        for item in pack:
            if item == RIGHT:
                rows = right
            else:
                rows = left_all[pl.ds((own ^ item) * mine, mine)].reshape(mine * seqs, LANES)
            out[at : at + rows.shape[0], :] = rows
            at += rows.shape[0]
    w_copy.wait()


def block_weights(w_ref, wide_ref, wf_ref, *, parts, minor):
    cz = w_ref.shape[1]
    hidden = parts * minor
    half = minor // 2
    rows_each = wide_ref.shape[0] // hidden // hidden
    own = lax.axis_index("narrow")
    wide_ref[...] = jnp.zeros_like(wide_ref)
    wf_ref[...] = w_ref[...].astype(jnp.float32)
    for e in range(hidden):
        rows = wf_ref[pl.ds(e ^ (own * minor), hidden, stride=hidden), :].astype(jnp.bfloat16)
        q, e2, t = e // minor, e % minor // half, e % half
        for k in range(rows_each):
            at = ((((q * half + t) * 2 + e2) * rows_each) + k) * hidden
            wide_ref[at : at + hidden, k * cz : (k + 1) * cz] = rows


def pack_kernel(*refs, count):
    out_ref, at = refs[-1], 0
    for ref in refs[:count]:
        out_ref[at : at + ref.shape[0]] = ref[...]
        at += ref.shape[0]


def pair_rows(left_of, right_of, wide_ref, shift_ref, outer_ref, store, *, wides, parts, minor, seqs_total):
    cz = shift_ref.shape[0]
    half = minor // 2
    seqs = LANES // parts
    groups = left_of(0).shape[0] // seqs
    residues = right_of(0, 0).shape[0] // minor
    cols = wides * residues
    lefts = [left_of(m) for m in range(parts)]
    slot = iota((minor * residues, LANES), 1) // seqs
    low = iota((LANES, LANES), 1) < LANES // 2
    zero = jnp.zeros((LANES, LANES), jnp.float32)
    for q in range(parts):
        blocks = []
        for g in range(groups):
            rows = jnp.concatenate([lefts[q ^ k][g * seqs : (g + 1) * seqs] for k in range(parts)], axis=0)
            rows = rows.astype(jnp.float32)
            turned = pltpu.roll(rows, LANES // 2, axis=1)
            for first, second in ((rows, turned), (turned, rows)):
                blocks.append(
                    jnp.concatenate([jnp.where(low, first, zero), jnp.where(low, zero, second)], axis=0)
                )
        left = jnp.concatenate(blocks, axis=1).astype(jnp.bfloat16)
        for d in range(wides):
            right = None
            for k in range(parts):
                chunk = right_of(d, q ^ k)
                right = chunk if right is None else jnp.where(slot == k, chunk, right)
            right = jnp.concatenate([right[: half * residues], right[half * residues :]], axis=1)
            outer = jnp.dot(right, left, preferred_element_type=jnp.float32).astype(jnp.bfloat16)
            for t in range(half):
                for g in range(2 * groups):
                    outer_ref[
                        pl.ds(g * cols + d * residues, residues),
                        (q * half + t) * LANES : (q * half + t + 1) * LANES,
                    ] = outer[t * residues : (t + 1) * residues, g * LANES : (g + 1) * LANES]

    shift = shift_ref[...].reshape(1, cz)
    pairs = jnp.dot(outer_ref[...], wide_ref[...], preferred_element_type=jnp.float32)
    rows_each = wide_ref.shape[1] // cz
    for g in range(2 * groups):
        for k in range(rows_each):
            pair = pairs[g * cols : (g + 1) * cols, k * cz : (k + 1) * cz]
            store(g * rows_each + k, pair * (1.0 / seqs_total) + shift)


def pair_kernel(*refs, places, blocks, first, **sizes):
    operands = sizes.pop("operands")
    shift_ref = refs[operands + 1]
    if first:
        out_hbm, wide_ref, outer_ref, done_ref, sems, wf_ref = refs[-6:]
    else:
        wide_ref = refs[operands]
        out_hbm, outer_ref, done_ref, sems = refs[-4:]
    parts, minor = sizes["parts"], sizes["minor"]
    own_rows, cols, _ = done_ref.shape
    residues = cols // len(blocks)
    left_count = own_rows * minor
    right_count = minor * residues

    def left_of(m):
        ref, at = places[m][:2]
        return refs[ref][at : at + left_count, :]

    def right_of(d, m):
        ref, at = places[m][2:]
        return refs[ref][at + d * right_count : at + (d + 1) * right_count, :]

    def store(row, pair):
        done_ref[row] = pair.astype(done_ref.dtype)

    if first:
        block_weights(refs[operands], wide_ref, wf_ref, parts=parts, minor=minor)
    pair_rows(left_of, right_of, wide_ref, shift_ref, outer_ref, store, wides=len(blocks), **sizes)
    copies = []
    for d, block in enumerate(blocks):
        at = pl.multiple_of((lax.axis_index("wide") ^ block) * residues, 16)
        copies.append(
            pltpu.make_async_copy(
                done_ref.at[:, pl.ds(d * residues, residues), :],
                out_hbm.at[:, pl.ds(at, residues), :],
                sems.at[d],
            )
        )
        copies[-1].start()
    for copy in copies:
        copy.wait()


def pair_blocks_kernel(*refs, wides, parts, minor, **sizes):
    left_refs, (right_ref, w_ref, shift_ref, out_ref, wide_ref, wf_ref, outer_ref) = refs[:parts], refs[parts:]

    @pl.when(pl.program_id(0) == 0)
    def _():
        block_weights(w_ref, wide_ref, wf_ref, parts=parts, minor=minor)

    def store(row, pair):
        out_ref[row] = pair.astype(out_ref.dtype)

    pair_rows(
        lambda m: left_refs[m][...], lambda d, m: right_ref[d, m], wide_ref, shift_ref, outer_ref, store,
        wides=wides, parts=parts, minor=minor, **sizes,
    )


def on_device(wide, narrow, x, gain, bias, lm, lb, rm, rb, w, shift):
    seqs, residues, depth = x.shape
    hidden = lm.shape[1]
    cz = w.shape[1]
    per = LANES // hidden
    slots = LANES // seqs
    minor = hidden // slots
    own_rows = residues // narrow
    groups = own_rows // per
    pieces = 4
    hbm = pl.BlockSpec(memory_space=pltpu.HBM)
    vmem = pl.BlockSpec(memory_space=pltpu.VMEM)
    params = pltpu.CompilerParams(vmem_limit_bytes=VMEM_LIMIT)
    direct = wide == 4 and narrow == 4
    if direct:
        packs = ((0,), (RIGHT,), (1, RIGHT), (2, 3))
    else:
        packs = tuple((m,) for m in range(narrow)) + ((RIGHT,),)
    left_count, right_count = groups * seqs, minor * residues
    args = (x, gain, bias, lm.T, lb, rm.T, rb)
    *made, w = pl.pallas_call(
        functools.partial(features_kernel, packs=packs, parts=narrow, pieces=pieces),
        out_shape=tuple(
            jax.ShapeDtypeStruct(
                (sum(right_count if i == RIGHT else left_count for i in pack), LANES), jnp.bfloat16
            )
            for pack in packs
        )
        + (jax.ShapeDtypeStruct(w.shape, w.dtype),),
        in_specs=[hbm] * (len(args) + 1),
        out_specs=(vmem,) * (len(packs) + 1),
        scratch_shapes=[pltpu.VMEM(a.shape, a.dtype) for a in args]
        + [
            pltpu.VMEM((seqs * residues, LANES), jnp.float32),
            pltpu.VMEM((seqs * residues, LANES), jnp.float32),
            pltpu.VMEM((residues // per, seqs, LANES), jnp.bfloat16),
            pltpu.VMEM((LANES, LANES), jnp.float32),
            pltpu.VMEM((minor * residues, LANES), jnp.float32),
            pltpu.SemaphoreType.DMA((pieces + len(args),)),
        ],
        compiler_params=pltpu.CompilerParams(vmem_limit_bytes=VMEM_ALL),
        name="features",
    )(*args, w)

    def across(a, m):
        return lax.ppermute(a, "narrow", [(i, i ^ m) for i in range(narrow)])

    def along(a, d):
        return lax.ppermute(a, "wide", [(i, i ^ d) for i in range(wide)])

    sizes = dict(parts=narrow, minor=minor, seqs_total=seqs * narrow)
    out_shape = jax.ShapeDtypeStruct((own_rows, wide * residues, cz), jnp.bfloat16)
    if direct:
        return pairs_by_block(made, across, along, w, shift, out_shape, residues, sizes, params)

    lefts = [made[0]] + [across(made[m], m) for m in range(1, narrow)]
    every = lax.all_gather(made[narrow], ("wide", "narrow"), axis=0, tiled=False)
    every = every.reshape(wide, narrow, right_count, LANES)
    every = jnp.take(every, lax.axis_index("narrow") ^ jnp.arange(narrow), axis=1)
    block = wide
    while block % 2 == 0 and block * residues > 192:
        block //= 2
    cols = block * residues
    return pl.pallas_call(
        functools.partial(pair_blocks_kernel, wides=block, **sizes),
        grid=(wide // block,),
        in_specs=[pl.BlockSpec((left_count, LANES), lambda b: (0, 0))] * narrow
        + [
            pl.BlockSpec((block, narrow, right_count, LANES), lambda b: (b, 0, 0, 0)),
            pl.BlockSpec(w.shape, lambda b: (0, 0)),
            pl.BlockSpec((cz,), lambda b: (0,)),
        ],
        out_specs=pl.BlockSpec((own_rows, cols, cz), lambda b: (0, b, 0)),
        out_shape=out_shape,
        scratch_shapes=[
            pltpu.VMEM((hidden * LANES // 2, 2 * cz), jnp.bfloat16),
            pltpu.VMEM(w.shape, jnp.float32),
            pltpu.VMEM((2 * groups * cols, hidden * LANES // 2), jnp.bfloat16),
        ],
        compiler_params=params,
        name="pairs",
    )(*lefts, every, w, shift)


COST = {0: 4_000_000_000, 1: 1_000_000_000, 3: 1_000_000_000}


def pairs_by_block(made, across, along, w, shift, out_shape, residues, sizes, params):
    left_own, right, to_core, to_chip = made
    left_count, right_count = left_own.shape[0], right.shape[0]
    hbm = pl.BlockSpec(memory_space=pltpu.HBM)
    vmem = pl.BlockSpec(memory_space=pltpu.VMEM)
    own_rows, _, cz = out_shape.shape
    hidden = sizes["parts"] * sizes["minor"]
    groups = own_rows * hidden // LANES

    def pack(*chunks, after):
        return pl.pallas_call(
            functools.partial(pack_kernel, count=len(chunks)),
            out_shape=jax.ShapeDtypeStruct((sum(c.shape[0] for c in chunks), LANES), jnp.bfloat16),
            in_specs=[vmem] * (len(chunks) + len(after)),
            out_specs=vmem,
            compiler_params=params,
            name="pack",
        )(*chunks, *after)

    def pairs(lefts, rights, blocks, weights, out=None, after=()):
        operands = []
        places = []
        for (a, at), (b, bt) in zip(lefts, rights):
            places.append((len(operands), at, len(operands) + 1, bt))
            operands += [a, b]
        count = len(operands)
        operands += [weights, shift, *after]
        specs = [vmem] * len(operands)
        aliases, shapes, outs = {}, [out_shape], [hbm]
        cols = len(blocks) * residues
        scratch = [
            pltpu.VMEM((2 * groups * cols, hidden * LANES // 2), jnp.bfloat16),
            pltpu.VMEM((own_rows, cols, cz), jnp.bfloat16),
            pltpu.SemaphoreType.DMA((len(blocks),)),
        ]
        if out is None:
            shapes.append(jax.ShapeDtypeStruct((hidden * LANES // 2, 2 * cz), jnp.bfloat16))
            outs.append(vmem)
            scratch.append(pltpu.VMEM(weights.shape, jnp.float32))
        else:
            aliases = {len(operands): 0}
            operands.append(out)
            specs.append(hbm)
        return pl.pallas_call(
            functools.partial(
                pair_kernel, places=places, blocks=blocks, operands=count, first=out is None, **sizes
            ),
            out_shape=shapes,
            in_specs=specs,
            out_specs=outs,
            input_output_aliases=aliases,
            scratch_shapes=scratch,
            compiler_params=params,
            cost_estimate=pl.CostEstimate(
                flops=COST[blocks[0]], bytes_accessed=1000, transcendentals=0
            ),
            name=f"pairs_{blocks[0]}",
        )(*operands)

    far = along(right, 2)
    near = along(right, 1)
    last = along(far, 1)
    chip = across(right, 2)
    chip_left = across(to_chip, 2)
    core = across(pack(to_core, chip_left, chip, after=(far, near)), 1)
    split = to_core.shape[0]
    lefts = ((left_own, 0), (core, 0), (chip_left, 0), (core, split + left_count))
    own = ((right, 0), (core, left_count), (chip, 0), (core, split + 2 * left_count))
    out, weights = pairs(lefts, own, (0,), w, after=(last,))

    middle = pack(near, far, after=(chip,))
    beside = across(middle, 1)
    other = across(middle, 2)
    onward = across(pack(other, after=(weights,)), 1)
    middle = ((middle, 0), (beside, 0), (other, 0), (onward, 0))
    (out,) = pairs(lefts, middle, (1, 2), weights, out)

    other = across(last, 2)
    both = across(pack(last, other, after=()), 1)
    (out,) = pairs(lefts, ((last, 0), (both, 0), (other, 0), (both, right_count)), (3,), weights, out)
    return out


def solution(mesh):
    in_specs = (P(("groups", "narrow"), "wide", None), P(), P(), P(), P(), P(), P(), P(), P())
    out_specs = P(("groups", "wide", "narrow"), None, None)
    return jax.shard_map(
        functools.partial(on_device, mesh.shape["wide"], mesh.shape["narrow"]),
        mesh=mesh,
        in_specs=in_specs,
        out_specs=out_specs,
        check_vma=False,
    )
```

```python
import functools

import jax
import jax.numpy as jnp
from jax import lax
from jax.experimental import pallas as pl
from jax.experimental.pallas import tpu as pltpu
from jax.sharding import PartitionSpec as P

LANES = 128
RIGHT = -1
VMEM_LIMIT = 40 * 1024 * 1024
VMEM_ALL = 62 * 1024 * 1024


def iota(shape, dim):
    return lax.broadcasted_iota(jnp.int32, shape, dim)


def features_kernel(
    x_hbm, gain_hbm, bias_hbm, lm_hbm, lb_hbm, rm_hbm, rb_hbm, w_hbm, shift_hbm,
    *refs, packs, parts, pieces,
):
    outs, wf_ref = refs[: len(packs)], refs[len(packs)]
    (x_ref, gain_ref, bias_ref, lm_ref, lb_ref, rm_ref, rb_ref, w_ref, shift_ref,
     lo_ref, hi_ref, left_all, turned_ref, rows_ref, sems) = refs[len(packs) + 1 :]
    seqs, residues, depth = x_ref.shape
    hidden = lm_ref.shape[0]
    per = LANES // hidden
    slots = LANES // seqs
    minor = hidden // slots
    groups = residues // per
    own = lax.axis_index("narrow")

    piece = seqs // pieces
    copies = [
        pltpu.make_async_copy(
            x_hbm.at[pl.ds(p * piece, piece)], x_ref.at[pl.ds(p * piece, piece)], sems.at[p]
        )
        for p in range(pieces)
    ]
    small = ((gain_hbm, gain_ref), (bias_hbm, bias_ref), (lm_hbm, lm_ref),
             (lb_hbm, lb_ref), (rm_hbm, rm_ref), (rb_hbm, rb_ref))
    rest = [pltpu.make_async_copy(a, b, sems.at[pieces + i]) for i, (a, b) in enumerate(small)]
    copies[0].start()
    for copy in rest:
        copy.start()
    for copy in copies[1:]:
        copy.start()
    late = [
        pltpu.make_async_copy(a, b, sems.at[pieces + len(small) + i])
        for i, (a, b) in enumerate(((w_hbm, w_ref), (shift_hbm, shift_ref)))
    ]
    for copy in late:
        copy.start()
    for copy in rest:
        copy.wait()

    column, row = iota((hidden, LANES), 1) % hidden, iota((hidden, LANES), 0)
    spread_l = (column == row).astype(jnp.float32)
    spread_r = (column == (row ^ (own * minor))).astype(jnp.float32)

    def widen(m, pick):
        return lax.dot_general(
            m, pick.astype(jnp.bfloat16), (((0,), (0,)), ((), ())),
            preferred_element_type=jnp.float32,
        )

    def widen_bias(b, pick):
        b = jnp.broadcast_to(b.reshape(1, hidden), (8, hidden))
        return jnp.dot(
            b, pick, precision=lax.Precision.HIGHEST, preferred_element_type=jnp.float32
        )[:1]

    weights = jnp.concatenate(
        [widen(lm_ref[...], spread_l), widen(rm_ref[...], spread_r)], axis=1
    )
    shift = jnp.concatenate(
        [widen_bias(lb_ref[...], spread_l), widen_bias(rb_ref[...], spread_r)], axis=1
    )
    place = iota((depth, 2 * LANES), 1) % LANES // hidden

    gain = gain_ref[...].reshape(1, depth)
    bias = bias_ref[...].reshape(1, depth)
    step = 4
    for s in range(0, seqs, step):
        if s % piece == 0:
            copies[s // piece].wait()
        x = x_ref[s : s + step].reshape(step * residues, depth).astype(jnp.float32)
        x = x - jnp.mean(x, axis=-1, keepdims=True)
        spread = jnp.mean(x * x, axis=-1, keepdims=True)
        x = x * lax.rsqrt(spread + 1e-05) * gain + bias
        rows = pl.ds(s * residues, step * residues)
        lo_ref[rows, :] = x[:, :LANES]
        hi_ref[rows, :] = x[:, LANES:]

    total = None
    for k in range(per):
        part = jnp.concatenate(
            [
                jnp.concatenate(
                    [half[pl.ds(g * per + k, seqs, stride=residues), :] for half in (lo_ref, hi_ref)],
                    axis=1,
                )
                for g in range(groups)
            ],
            axis=0,
        ).astype(jnp.bfloat16)
        placed = jnp.where(place == k, weights, 0.0).astype(jnp.bfloat16)
        term = jnp.dot(part, placed, preferred_element_type=jnp.float32)
        total = term if total is None else total + term
    total = total + shift
    left_all[...] = total[:, :LANES].astype(left_all.dtype).reshape(groups, seqs, LANES)
    mine = groups // parts

    slot = iota((minor, LANES), 1) // seqs
    for block in range(groups // slots):
        turned_ref[...] = total[block * LANES : (block + 1) * LANES, LANES:].T
        for k in range(per):
            parts_of = [turned_ref[pl.ds(k * hidden + q * minor, minor), :] for q in range(slots)]
            for g in range(slots):
                out = None
                for q in range(slots):
                    moved = parts_of[q]
                    if q != g:
                        moved = pltpu.roll(moved, (q - g) % slots * seqs, axis=1)
                    out = moved if out is None else jnp.where(slot == q, moved, out)
                j = (block * slots + g) * per + k
                rows_ref[pl.ds(j, minor, stride=residues), :] = out
    right = rows_ref[...].astype(jnp.bfloat16)
    for out, pack in zip(outs, packs):
        at = 0
        for item in pack:
            if item == RIGHT:
                rows = right
            else:
                rows = left_all[pl.ds((own ^ item) * mine, mine)].reshape(mine * seqs, LANES)
            out[at : at + rows.shape[0], :] = rows
            at += rows.shape[0]
    for copy in late:
        copy.wait()
    wf_ref[: w_ref.shape[0]] = w_ref[...].astype(jnp.float32)
    wf_ref[w_ref.shape[0] :] = jnp.broadcast_to(shift_ref[...].reshape(1, -1), (8, shift_ref.shape[0]))


def block_weights(wf_ref, wide_ref, *, parts, minor):
    cz = wf_ref.shape[1]
    hidden = parts * minor
    half = minor // 2
    rows_each = wide_ref.shape[0] // hidden // hidden
    own = lax.axis_index("narrow")
    wide_ref[...] = jnp.zeros_like(wide_ref)
    for e in range(hidden):
        rows = wf_ref[pl.ds(e ^ (own * minor), hidden, stride=hidden), :].astype(jnp.bfloat16)
        q, e2, t = e // minor, e % minor // half, e % half
        for k in range(rows_each):
            at = ((((q * half + t) * 2 + e2) * rows_each) + k) * hidden
            wide_ref[at : at + hidden, k * cz : (k + 1) * cz] = rows


def pack_kernel(*refs, count):
    out_ref, at = refs[-1], 0
    for ref in refs[:count]:
        out_ref[at : at + ref.shape[0]] = ref[...]
        at += ref.shape[0]


def pair_rows(left_of, right_of, wide_ref, shift, outer_ref, store, *, wides, parts, minor, seqs_total):
    cz = shift.shape[1]
    half = minor // 2
    seqs = LANES // parts
    groups = left_of(0).shape[0] // seqs
    residues = right_of(0, 0).shape[0] // minor
    cols = wides * residues
    slot = iota((minor * residues, LANES), 1) // seqs
    low = iota((seqs, LANES), 1) < LANES // 2
    zero = jnp.zeros((seqs, LANES), jnp.float32)

    lefts = []
    for m in range(parts):
        halves = []
        for g in range(groups):
            rows = left_of(m)[g * seqs : (g + 1) * seqs].astype(jnp.float32)
            turned = pltpu.roll(rows, LANES // 2, axis=1)
            for first, second in ((rows, turned), (turned, rows)):
                halves.append((jnp.where(low, first, zero), jnp.where(low, zero, second)))
        lefts.append(
            [jnp.concatenate([h[i] for h in halves], axis=1).astype(jnp.bfloat16) for i in range(2)]
        )
    for q in range(parts):
        left = jnp.concatenate([lefts[q ^ k][i] for i in range(2) for k in range(parts)], axis=0)
        for d in range(wides):
            right = None
            for k in range(parts):
                chunk = right_of(d, q ^ k)
                right = chunk if right is None else jnp.where(slot == k, chunk, right)
            right = jnp.concatenate([right[: half * residues], right[half * residues :]], axis=1)
            outer = jnp.dot(right, left, preferred_element_type=jnp.float32).astype(jnp.bfloat16)
            for t in range(half):
                for g in range(2 * groups):
                    outer_ref[
                        pl.ds(g * cols + d * residues, residues),
                        (q * half + t) * LANES : (q * half + t + 1) * LANES,
                    ] = outer[t * residues : (t + 1) * residues, g * LANES : (g + 1) * LANES]

    pairs = jnp.dot(outer_ref[...], wide_ref[...], preferred_element_type=jnp.float32)
    rows_each = wide_ref.shape[1] // cz
    for g in range(2 * groups):
        for k in range(rows_each):
            pair = pairs[g * cols : (g + 1) * cols, k * cz : (k + 1) * cz]
            store(g * rows_each + k, pair * (1.0 / seqs_total) + shift)


def pair_kernel(*refs, places, blocks, first, **sizes):
    operands = sizes.pop("operands")
    if first:
        out_hbm, wide_ref, shift_ref, outer_ref, done_ref, sems = refs[-6:]
    else:
        wide_ref, shift_ref = refs[operands : operands + 2]
        out_hbm, outer_ref, done_ref, sems = refs[-4:]
    parts, minor = sizes["parts"], sizes["minor"]
    own_rows, cols, _ = done_ref.shape
    residues = cols // len(blocks)
    left_count = own_rows * minor
    right_count = minor * residues

    def left_of(m):
        ref, at = places[m][:2]
        return refs[ref][at : at + left_count, :]

    def right_of(d, m):
        ref, at = places[m][2:]
        return refs[ref][at + d * right_count : at + (d + 1) * right_count, :]

    def store(row, pair):
        done_ref[row] = pair.astype(done_ref.dtype)

    if first:
        wf_ref = refs[operands]
        block_weights(wf_ref, wide_ref, parts=parts, minor=minor)
        shift_ref[...] = wf_ref[wf_ref.shape[0] - 8 :]
    pair_rows(left_of, right_of, wide_ref, shift_ref[:1], outer_ref, store, wides=len(blocks), **sizes)
    copies = []
    for d, block in enumerate(blocks):
        at = pl.multiple_of((lax.axis_index("wide") ^ block) * residues, 16)
        copies.append(
            pltpu.make_async_copy(
                done_ref.at[:, pl.ds(d * residues, residues), :],
                out_hbm.at[:, pl.ds(at, residues), :],
                sems.at[d],
            )
        )
        copies[-1].start()
    for copy in copies:
        copy.wait()


def pair_blocks_kernel(*refs, wides, parts, minor, **sizes):
    left_refs, (right_ref, wf_ref, out_ref, wide_ref, outer_ref) = refs[:parts], refs[parts:]

    @pl.when(pl.program_id(0) == 0)
    def _():
        block_weights(wf_ref, wide_ref, parts=parts, minor=minor)

    def store(row, pair):
        out_ref[row] = pair.astype(out_ref.dtype)

    pair_rows(
        lambda m: left_refs[m][...], lambda d, m: right_ref[d, m],
        wide_ref, wf_ref[wf_ref.shape[0] - 8 :][:1], outer_ref, store,
        wides=wides, parts=parts, minor=minor, **sizes,
    )


def on_device(wide, narrow, x, gain, bias, lm, lb, rm, rb, w, shift):
    seqs, residues, depth = x.shape
    hidden = lm.shape[1]
    cz = w.shape[1]
    per = LANES // hidden
    slots = LANES // seqs
    minor = hidden // slots
    own_rows = residues // narrow
    groups = own_rows // per
    pieces = 4
    hbm = pl.BlockSpec(memory_space=pltpu.HBM)
    vmem = pl.BlockSpec(memory_space=pltpu.VMEM)
    params = pltpu.CompilerParams(vmem_limit_bytes=VMEM_LIMIT)
    direct = wide == 4 and narrow == 4
    if direct:
        packs = ((0,), (RIGHT,), (1, RIGHT), (2, 3))
    else:
        packs = tuple((m,) for m in range(narrow)) + ((RIGHT,),)
    left_count, right_count = groups * seqs, minor * residues
    args = (x, gain, bias, lm.T, lb, rm.T, rb, w, shift)
    *made, w = pl.pallas_call(
        functools.partial(features_kernel, packs=packs, parts=narrow, pieces=pieces),
        out_shape=tuple(
            jax.ShapeDtypeStruct(
                (sum(right_count if i == RIGHT else left_count for i in pack), LANES), jnp.bfloat16
            )
            for pack in packs
        )
        + (jax.ShapeDtypeStruct((w.shape[0] + 8, cz), jnp.float32),),
        in_specs=[hbm] * len(args),
        out_specs=(vmem,) * (len(packs) + 1),
        scratch_shapes=[pltpu.VMEM(a.shape, a.dtype) for a in args]
        + [
            pltpu.VMEM((seqs * residues, LANES), jnp.float32),
            pltpu.VMEM((seqs * residues, LANES), jnp.float32),
            pltpu.VMEM((residues // per, seqs, LANES), jnp.bfloat16),
            pltpu.VMEM((LANES, LANES), jnp.float32),
            pltpu.VMEM((minor * residues, LANES), jnp.float32),
            pltpu.SemaphoreType.DMA((pieces + len(args) - 1,)),
        ],
        compiler_params=pltpu.CompilerParams(vmem_limit_bytes=VMEM_ALL),
        name="features",
    )(*args)

    def across(a, m):
        return lax.ppermute(a, "narrow", [(i, i ^ m) for i in range(narrow)])

    def along(a, d):
        return lax.ppermute(a, "wide", [(i, i ^ d) for i in range(wide)])

    sizes = dict(parts=narrow, minor=minor, seqs_total=seqs * narrow)
    out_shape = jax.ShapeDtypeStruct((own_rows, wide * residues, cz), jnp.bfloat16)
    if direct:
        return pairs_by_block(made, across, along, w, out_shape, residues, sizes, params)

    lefts = [made[0]] + [across(made[m], m) for m in range(1, narrow)]
    every = lax.all_gather(made[narrow], ("wide", "narrow"), axis=0, tiled=False)
    every = every.reshape(wide, narrow, right_count, LANES)
    every = jnp.take(every, lax.axis_index("narrow") ^ jnp.arange(narrow), axis=1)
    block = wide
    while block % 2 == 0 and block * residues > 192:
        block //= 2
    cols = block * residues
    return pl.pallas_call(
        functools.partial(pair_blocks_kernel, wides=block, **sizes),
        grid=(wide // block,),
        in_specs=[pl.BlockSpec((left_count, LANES), lambda b: (0, 0))] * narrow
        + [
            pl.BlockSpec((block, narrow, right_count, LANES), lambda b: (b, 0, 0, 0)),
            pl.BlockSpec(w.shape, lambda b: (0, 0)),
        ],
        out_specs=pl.BlockSpec((own_rows, cols, cz), lambda b: (0, b, 0)),
        out_shape=out_shape,
        scratch_shapes=[
            pltpu.VMEM((hidden * LANES // 2, 2 * cz), jnp.bfloat16),
            pltpu.VMEM((2 * groups * cols, hidden * LANES // 2), jnp.bfloat16),
        ],
        compiler_params=params,
        name="pairs",
    )(*lefts, every, w)


def pairs_by_block(made, across, along, w, out_shape, residues, sizes, params):
    left_own, right, to_core, to_chip = made
    left_count, right_count = left_own.shape[0], right.shape[0]
    hbm = pl.BlockSpec(memory_space=pltpu.HBM)
    vmem = pl.BlockSpec(memory_space=pltpu.VMEM)
    own_rows, _, cz = out_shape.shape
    hidden = sizes["parts"] * sizes["minor"]
    groups = own_rows * hidden // LANES

    def pack(*chunks, after):
        return pl.pallas_call(
            functools.partial(pack_kernel, count=len(chunks)),
            out_shape=jax.ShapeDtypeStruct((sum(c.shape[0] for c in chunks), LANES), jnp.bfloat16),
            in_specs=[vmem] * (len(chunks) + len(after)),
            out_specs=vmem,
            compiler_params=params,
            name="pack",
        )(*chunks, *after)

    def pairs(lefts, rights, blocks, *weights, out=None, after=()):
        operands = []
        places = []
        for (a, at), (b, bt) in zip(lefts, rights):
            places.append((len(operands), at, len(operands) + 1, bt))
            operands += [a, b]
        count = len(operands)
        operands += [*weights, *after]
        specs = [vmem] * len(operands)
        aliases, shapes, outs = {}, [out_shape], [hbm]
        cols = len(blocks) * residues
        scratch = [
            pltpu.VMEM((2 * groups * cols, hidden * LANES // 2), jnp.bfloat16),
            pltpu.VMEM((own_rows, cols, cz), jnp.bfloat16),
            pltpu.SemaphoreType.DMA((len(blocks),)),
        ]
        if out is None:
            shapes.append(jax.ShapeDtypeStruct((hidden * LANES // 2, 2 * cz), jnp.bfloat16))
            shapes.append(jax.ShapeDtypeStruct((8, cz), jnp.float32))
            outs += [vmem, vmem]
        else:
            aliases = {len(operands): 0}
            operands.append(out)
            specs.append(hbm)
        return pl.pallas_call(
            functools.partial(
                pair_kernel, places=places, blocks=blocks, operands=count, first=out is None, **sizes
            ),
            out_shape=shapes,
            in_specs=specs,
            out_specs=outs,
            input_output_aliases=aliases,
            scratch_shapes=scratch,
            compiler_params=params,
            cost_estimate=pl.CostEstimate(
                flops=1000, bytes_accessed=1000, transcendentals=0
            ),
            name=f"pairs_{blocks[0]}",
        )(*operands)

    far = along(right, 2)
    near = along(right, 1)
    last = along(far, 1)
    chip = across(right, 2)
    chip_left = across(to_chip, 2)
    core = across(to_core, 1)
    middle = pack(near, far, after=(chip, core))
    beside = across(middle, 1)
    both = across(pack(chip_left, chip, after=(last,)), 1)
    lefts = ((left_own, 0), (core, 0), (chip_left, 0), (both, left_count))
    own = ((right, 0), (core, left_count), (chip, 0), (both, 2 * left_count))
    out, *weights = pairs(lefts, own, (0,), w)

    other = across(middle, 2)
    onward = across(pack(other, after=weights[:1]), 1)
    middle = ((middle, 0), (beside, 0), (other, 0), (onward, 0))
    (out,) = pairs(lefts, middle, (1, 2), *weights, out=out)

    other = across(last, 2)
    both = across(pack(last, other, after=()), 1)
    (out,) = pairs(lefts, ((last, 0), (both, 0), (other, 0), (both, right_count)), (3,), *weights, out=out)
    return out


def solution(mesh):
    in_specs = (P(("groups", "narrow"), "wide", None), P(), P(), P(), P(), P(), P(), P(), P())
    out_specs = P(("groups", "wide", "narrow"), None, None)
    return jax.shard_map(
        functools.partial(on_device, mesh.shape["wide"], mesh.shape["narrow"]),
        mesh=mesh,
        in_specs=in_specs,
        out_specs=out_specs,
        check_vma=False,
    )
```

```python
import functools

import jax
import jax.numpy as jnp
from jax import lax
from jax.experimental import pallas as pl
from jax.experimental.pallas import tpu as pltpu
from jax.sharding import PartitionSpec as P

LANES = 128
RIGHT = -1
VMEM_LIMIT = 40 * 1024 * 1024
VMEM_ALL = 62 * 1024 * 1024


def iota(shape, dim):
    return lax.broadcasted_iota(jnp.int32, shape, dim)


def features_kernel(*refs, packs, parts, pieces):
    args, refs = refs[:9], refs[9:]
    outs, wf_hbm, refs = refs[: len(packs)], refs[len(packs)], refs[len(packs) + 1 :]
    held, (lo_ref, hi_ref, left_ref, turned_ref, rows_ref, right_ref, wf_ref, sems) = refs[:9], refs[9:]
    x_ref, gain_ref, bias_ref, lm_ref, lb_ref, rm_ref, rb_ref, w_ref, shift_ref = held
    seqs, residues, depth = x_ref.shape
    hidden = lm_ref.shape[0]
    per = LANES // hidden
    slots = LANES // seqs
    minor = hidden // slots
    groups = residues // per
    own = lax.axis_index("narrow")

    piece = seqs // pieces
    copies = [
        pltpu.make_async_copy(
            args[0].at[pl.ds(p * piece, piece)], x_ref.at[pl.ds(p * piece, piece)], sems.at[p]
        )
        for p in range(pieces)
    ]
    rest = [
        pltpu.make_async_copy(a, b, sems.at[pieces + i]) for i, (a, b) in enumerate(zip(args[1:], held[1:]))
    ]
    for copy in copies[:1] + rest[:2] + copies[1:] + rest[2:]:
        copy.start()
    free = pieces + len(rest)

    def norm(p):
        gain = gain_ref[...].reshape(1, depth)
        bias = bias_ref[...].reshape(1, depth)
        step = min(4, piece)
        for s in range(p * piece, (p + 1) * piece, step):
            x = x_ref[s : s + step].reshape(step * residues, depth).astype(jnp.float32)
            x = x - jnp.mean(x, axis=-1, keepdims=True)
            spread = jnp.mean(x * x, axis=-1, keepdims=True)
            x = x * lax.rsqrt(spread + 1e-05) * gain + bias
            rows = pl.ds(s * residues, step * residues)
            lo_ref[rows, :] = x[:, :LANES]
            hi_ref[rows, :] = x[:, LANES:]

    for copy in rest[:2]:
        copy.wait()
    for p in range(pieces - 1):
        copies[p].wait()
        norm(p)
    for copy in copies[-1:] + rest[2:]:
        copy.wait()
    count = w_ref.shape[0]
    wf_ref[:count] = w_ref[...].astype(jnp.float32)
    wf_ref[count:] = jnp.broadcast_to(shift_ref[...].reshape(1, -1), (8, shift_ref.shape[0]))
    norm(pieces - 1)

    column, row = iota((hidden, LANES), 1) % hidden, iota((hidden, LANES), 0)
    spread_l = (column == row).astype(jnp.float32)
    spread_r = (column == (row ^ (own * minor))).astype(jnp.float32)

    def widen(m, pick):
        return lax.dot_general(
            m, pick.astype(jnp.bfloat16), (((0,), (0,)), ((), ())),
            preferred_element_type=jnp.float32,
        )

    def widen_bias(b, pick):
        b = jnp.broadcast_to(b.reshape(1, hidden), (8, hidden))
        return jnp.dot(
            b, pick, precision=lax.Precision.HIGHEST, preferred_element_type=jnp.float32
        )[:1]

    weights = jnp.concatenate(
        [widen(lm_ref[...], spread_l), widen(rm_ref[...], spread_r)], axis=1
    )
    shift = jnp.concatenate(
        [widen_bias(lb_ref[...], spread_l), widen_bias(rb_ref[...], spread_r)], axis=1
    )
    place = iota((depth, 2 * LANES), 1) % LANES // hidden
    sends = [pltpu.make_async_copy(wf_ref, wf_hbm, sems.at[free])]
    sends[0].start()

    total = None
    for k in range(per):
        part = jnp.concatenate(
            [
                jnp.concatenate(
                    [half[pl.ds(g * per + k, seqs, stride=residues), :] for half in (lo_ref, hi_ref)],
                    axis=1,
                )
                for g in range(groups)
            ],
            axis=0,
        ).astype(jnp.bfloat16)
        placed = jnp.where(place == k, weights, 0.0).astype(jnp.bfloat16)
        term = jnp.dot(part, placed, preferred_element_type=jnp.float32)
        total = term if total is None else total + term
    total = total + shift
    left_ref[...] = total[:, :LANES].astype(left_ref.dtype)

    slot = iota((minor, LANES), 1) // seqs
    for block in range(groups // slots):
        turned_ref[...] = total[block * LANES : (block + 1) * LANES, LANES:].T
        for k in range(per):
            parts_of = [turned_ref[pl.ds(k * hidden + q * minor, minor), :] for q in range(slots)]
            for g in range(slots):
                out = None
                for q in range(slots):
                    moved = parts_of[q]
                    if q != g:
                        moved = pltpu.roll(moved, (q - g) % slots * seqs, axis=1)
                    out = moved if out is None else jnp.where(slot == q, moved, out)
                j = (block * slots + g) * per + k
                rows_ref[pl.ds(j, minor, stride=residues), :] = out
    right_ref[...] = rows_ref[...].astype(right_ref.dtype)

    mine = left_ref.shape[0] // parts
    for out, pack in zip(outs, packs):
        at = 0
        for item in pack:
            if item == RIGHT:
                rows = right_ref
            else:
                rows = left_ref.at[pl.ds(pl.multiple_of((own ^ item) * mine, 16), mine)]
            free += 1
            sends.append(
                pltpu.make_async_copy(rows, out.at[pl.ds(at, rows.shape[0])], sems.at[free])
            )
            sends[-1].start()
            at += rows.shape[0]
    for copy in sends:
        copy.wait()


def block_weights(wf_ref, wide_ref, *, parts, minor):
    cz = wf_ref.shape[1]
    hidden = parts * minor
    half = minor // 2
    rows_each = wide_ref.shape[0] // hidden // hidden
    own = lax.axis_index("narrow")
    wide_ref[...] = jnp.zeros_like(wide_ref)
    for e in range(hidden):
        rows = wf_ref[pl.ds(e ^ (own * minor), hidden, stride=hidden), :].astype(jnp.bfloat16)
        q, e2, t = e // minor, e % minor // half, e % half
        for k in range(rows_each):
            at = ((((q * half + t) * 2 + e2) * rows_each) + k) * hidden
            wide_ref[at : at + hidden, k * cz : (k + 1) * cz] = rows


def pack_kernel(*refs, count):
    out_ref, at = refs[-1], 0
    for ref in refs[:count]:
        out_ref[at : at + ref.shape[0]] = ref[...]
        at += ref.shape[0]


def spread_left(left_of, spread_ref, *, parts):
    seqs = LANES // parts
    low = iota((seqs, LANES), 1) < LANES // 2
    zero = jnp.zeros((seqs, LANES), jnp.float32)
    for m in range(parts):
        left = left_of(m)
        for g in range(left.shape[0] // seqs):
            rows = left[g * seqs : (g + 1) * seqs].astype(jnp.float32)
            turned = pltpu.roll(rows, LANES // 2, axis=1)
            for half, (first, second) in enumerate(((rows, turned), (turned, rows))):
                lanes = pl.ds((2 * g + half) * LANES, LANES)
                spread_ref[m, 0, :, lanes] = jnp.where(low, first, zero).astype(spread_ref.dtype)
                spread_ref[m, 1, :, lanes] = jnp.where(low, zero, second).astype(spread_ref.dtype)


def pair_rows(spread_ref, right_of, wide_ref, shift, outer_ref, store, *, wides, parts, minor, seqs_total):
    cz = shift.shape[1]
    half = minor // 2
    seqs = LANES // parts
    halves = spread_ref.shape[3] // LANES
    residues = right_of(0, 0).shape[0] // minor
    cols = wides * residues
    slot = iota((minor * residues, LANES), 1) // seqs
    for q in range(parts):
        left = jnp.concatenate([spread_ref[q ^ k, i] for i in range(2) for k in range(parts)], axis=0)
        for d in range(wides):
            right = None
            for k in range(parts):
                chunk = right_of(d, q ^ k)
                right = chunk if right is None else jnp.where(slot == k, chunk, right)
            right = jnp.concatenate([right[: half * residues], right[half * residues :]], axis=1)
            outer = jnp.dot(right, left, preferred_element_type=jnp.float32).astype(jnp.bfloat16)
            for t in range(half):
                for g in range(halves):
                    outer_ref[
                        pl.ds(g * cols + d * residues, residues),
                        (q * half + t) * LANES : (q * half + t + 1) * LANES,
                    ] = outer[t * residues : (t + 1) * residues, g * LANES : (g + 1) * LANES]

    pairs = jnp.dot(outer_ref[...], wide_ref[...], preferred_element_type=jnp.float32)
    rows_each = wide_ref.shape[1] // cz
    for g in range(halves):
        for k in range(rows_each):
            pair = pairs[g * cols : (g + 1) * cols, k * cz : (k + 1) * cz]
            store(g * rows_each + k, pair * (1.0 / seqs_total) + shift)


def pair_kernel(*refs, operands, rights, blocks, earlier, lefts=None, **sizes):
    parts, minor = sizes["parts"], sizes["minor"]
    inputs, refs = refs[:operands], refs[operands:]
    if lefts is not None:
        wf_ref, done_ref, spread_ref, wide_ref, shift_ref, outer_ref = refs
        own_rows = done_ref.shape[0]
        block_weights(wf_ref, wide_ref, parts=parts, minor=minor)
        shift_ref[...] = wf_ref[wf_ref.shape[0] - 8 :]
        count = own_rows * minor
        spread_left(lambda m: inputs[lefts[m][0]][lefts[m][1] : lefts[m][1] + count, :], spread_ref, parts=parts)
    elif not earlier:
        spread_ref, wide_ref, shift_ref, done_ref, outer_ref = refs
    else:
        spread_ref, wide_ref, shift_ref = refs[:3]
        before, (out_hbm, outer_ref, done_ref, sems) = refs[3 : 3 + len(earlier)], refs[3 + len(earlier) :]
    residues = done_ref.shape[1] // len(blocks)
    copies = []

    def write(ref, places):
        for d, block in enumerate(places):
            at = pl.multiple_of((lax.axis_index("wide") ^ block) * residues, 16)
            copies.append(
                pltpu.make_async_copy(
                    ref.at[:, pl.ds(d * residues, residues), :],
                    out_hbm.at[:, pl.ds(at, residues), :],
                    sems.at[len(copies)],
                )
            )
            copies[-1].start()

    if earlier:
        for ref, places in zip(before, earlier):
            write(ref, places)

    def right_of(d, m):
        ref, at = rights[m]
        at += d * minor * residues
        return inputs[ref][at : at + minor * residues, :]

    def store(row, pair):
        done_ref[row] = pair.astype(done_ref.dtype)

    pair_rows(spread_ref, right_of, wide_ref, shift_ref[:1], outer_ref, store, wides=len(blocks), **sizes)
    if earlier:
        write(done_ref, blocks)
        for copy in copies:
            copy.wait()


def pair_blocks_kernel(*refs, wides, parts, minor, **sizes):
    left_refs, (right_ref, wf_ref, out_ref, spread_ref, wide_ref, outer_ref) = refs[:parts], refs[parts:]

    @pl.when(pl.program_id(0) == 0)
    def _():
        block_weights(wf_ref, wide_ref, parts=parts, minor=minor)
        spread_left(lambda m: left_refs[m][...], spread_ref, parts=parts)

    def store(row, pair):
        out_ref[row] = pair.astype(out_ref.dtype)

    pair_rows(
        spread_ref, lambda d, m: right_ref[d, m],
        wide_ref, wf_ref[wf_ref.shape[0] - 8 :][:1], outer_ref, store,
        wides=wides, parts=parts, minor=minor, **sizes,
    )


def on_device(wide, narrow, x, gain, bias, lm, lb, rm, rb, w, shift):
    seqs, residues, depth = x.shape
    hidden = lm.shape[1]
    cz = w.shape[1]
    per = LANES // hidden
    slots = LANES // seqs
    minor = hidden // slots
    own_rows = residues // narrow
    groups = own_rows // per
    pieces = 4
    hbm = pl.BlockSpec(memory_space=pltpu.HBM)
    vmem = pl.BlockSpec(memory_space=pltpu.VMEM)
    params = pltpu.CompilerParams(vmem_limit_bytes=VMEM_LIMIT)
    direct = wide == 4 and narrow == 4
    if direct:
        packs = ((0,), (RIGHT,), (1, RIGHT), (2, 3, RIGHT))
    else:
        packs = tuple((m,) for m in range(narrow)) + ((RIGHT,),)
    left_count, right_count = groups * seqs, minor * residues
    args = (x, gain, bias, lm.T, lb, rm.T, rb, w, shift)
    *made, w = pl.pallas_call(
        functools.partial(features_kernel, packs=packs, parts=narrow, pieces=pieces),
        out_shape=tuple(
            jax.ShapeDtypeStruct(
                (sum(right_count if i == RIGHT else left_count for i in pack), LANES), jnp.bfloat16
            )
            for pack in packs
        )
        + (jax.ShapeDtypeStruct((w.shape[0] + 8, cz), jnp.float32),),
        in_specs=[hbm] * len(args),
        out_specs=(hbm,) * (len(packs) + 1),
        scratch_shapes=[pltpu.VMEM(a.shape, a.dtype) for a in args]
        + [
            pltpu.VMEM((seqs * residues, LANES), jnp.float32),
            pltpu.VMEM((seqs * residues, LANES), jnp.float32),
            pltpu.VMEM((residues // per * seqs, LANES), jnp.bfloat16),
            pltpu.VMEM((LANES, LANES), jnp.float32),
            pltpu.VMEM((minor * residues, LANES), jnp.float32),
            pltpu.VMEM((minor * residues, LANES), jnp.bfloat16),
            pltpu.VMEM((w.shape[0] + 8, cz), jnp.float32),
            pltpu.SemaphoreType.DMA((pieces + len(args) + sum(len(pack) for pack in packs),)),
        ],
        compiler_params=pltpu.CompilerParams(vmem_limit_bytes=VMEM_ALL),
        name="features",
    )(*args)

    def across(a, m):
        return lax.ppermute(a, "narrow", [(i, i ^ m) for i in range(narrow)])

    def along(a, d):
        return lax.ppermute(a, "wide", [(i, i ^ d) for i in range(wide)])

    sizes = dict(parts=narrow, minor=minor, seqs_total=seqs * narrow)
    out_shape = jax.ShapeDtypeStruct((own_rows, wide * residues, cz), jnp.bfloat16)
    if direct:
        return pairs_by_block(made, across, along, w, out_shape, residues, sizes, params)

    lefts = [made[0]] + [across(made[m], m) for m in range(1, narrow)]
    every = lax.all_gather(made[narrow], ("wide", "narrow"), axis=0, tiled=False)
    every = every.reshape(wide, narrow, right_count, LANES)
    every = jnp.take(every, lax.axis_index("narrow") ^ jnp.arange(narrow), axis=1)
    block = wide
    while block % 2 == 0 and block * residues > 192:
        block //= 2
    cols = block * residues
    return pl.pallas_call(
        functools.partial(pair_blocks_kernel, wides=block, **sizes),
        grid=(wide // block,),
        in_specs=[pl.BlockSpec((left_count, LANES), lambda b: (0, 0))] * narrow
        + [
            pl.BlockSpec((block, narrow, right_count, LANES), lambda b: (b, 0, 0, 0)),
            pl.BlockSpec(w.shape, lambda b: (0, 0)),
        ],
        out_specs=pl.BlockSpec((own_rows, cols, cz), lambda b: (0, b, 0)),
        out_shape=out_shape,
        scratch_shapes=[
            pltpu.VMEM((narrow, 2, seqs, 2 * groups * LANES), jnp.bfloat16),
            pltpu.VMEM((hidden * LANES // 2, 2 * cz), jnp.bfloat16),
            pltpu.VMEM((2 * groups * cols, hidden * LANES // 2), jnp.bfloat16),
        ],
        compiler_params=params,
        name="pairs",
    )(*lefts, every, w)


def pairs_by_block(made, across, along, w, out_shape, residues, sizes, params):
    left_own, right, to_core, to_chip = made
    left_count, right_count = left_own.shape[0], right.shape[0]
    hbm = pl.BlockSpec(memory_space=pltpu.HBM)
    vmem = pl.BlockSpec(memory_space=pltpu.VMEM)
    own_rows, _, cz = out_shape.shape
    narrow = sizes["parts"]
    hidden = narrow * sizes["minor"]
    groups = own_rows * hidden // LANES

    def pack(*chunks, after):
        return pl.pallas_call(
            functools.partial(pack_kernel, count=len(chunks)),
            out_shape=jax.ShapeDtypeStruct((sum(c.shape[0] for c in chunks), LANES), jnp.bfloat16),
            in_specs=[vmem] * (len(chunks) + len(after)),
            out_specs=vmem,
            compiler_params=params,
            name="pack",
        )(*chunks, *after)

    def pairs(rights, blocks, *shared, lefts=None, earlier=()):
        operands, places = [], []
        for chunks in (rights, lefts or ()):
            places.append([])
            for chunk, at in chunks:
                places[-1].append((len(operands), at))
                operands.append(chunk)
        count = len(operands)
        operands += shared
        cols = len(blocks) * residues
        done = jax.ShapeDtypeStruct((own_rows, cols, cz), jnp.bfloat16)
        shapes, outs = [done], [vmem]
        scratch = [pltpu.VMEM((2 * groups * cols, hidden * LANES // 2), jnp.bfloat16)]
        if lefts is not None:
            shapes += [
                jax.ShapeDtypeStruct((narrow, 2, LANES // narrow, 2 * groups * LANES), jnp.bfloat16),
                jax.ShapeDtypeStruct((hidden * LANES // 2, 2 * cz), jnp.bfloat16),
                jax.ShapeDtypeStruct((8, cz), jnp.float32),
            ]
            outs += [vmem] * 3
        if earlier:
            operands += [ref for ref, _ in earlier]
            shapes, outs = [out_shape], [hbm]
            scratch += [
                pltpu.VMEM(done.shape, done.dtype),
                pltpu.SemaphoreType.DMA((len(blocks) + sum(len(b) for _, b in earlier),)),
            ]
        return pl.pallas_call(
            functools.partial(
                pair_kernel, operands=count, rights=places[0], blocks=blocks,
                earlier=[b for _, b in earlier], lefts=lefts and places[1], **sizes,
            ),
            out_shape=shapes,
            in_specs=[vmem] * len(operands),
            out_specs=outs,
            scratch_shapes=scratch,
            compiler_params=params,
            cost_estimate=pl.CostEstimate(flops=1000, bytes_accessed=1000, transcendentals=0),
            name=f"pairs_{blocks[0]}",
        )(*operands)

    far = along(right, 2)
    near = along(right, 1)
    last = along(far, 1)
    chip = across(to_chip, 2)
    core = across(to_core, 1)
    middle = pack(near, far, after=(chip, core))
    beside = across(middle, 1)
    both = across(pack(chip, after=(last,)), 1)
    lefts = ((left_own, 0), (core, 0), (chip, 0), (both, left_count))
    own = ((right, 0), (core, left_count), (chip, 2 * left_count), (both, 2 * left_count))
    first, *shared = pairs(own, (0,), w, lefts=lefts)

    other = across(middle, 2)
    onward = across(pack(other, after=shared[1:2]), 1)
    (second,) = pairs(((middle, 0), (beside, 0), (other, 0), (onward, 0)), (1, 2), *shared)

    other = across(last, 2)
    both = across(pack(last, other, after=()), 1)
    (out,) = pairs(
        ((last, 0), (both, 0), (other, 0), (both, right_count)), (3,), *shared,
        earlier=((first, (0,)), (second, (1, 2))),
    )
    return out


def solution(mesh):
    in_specs = (P(("groups", "narrow"), "wide", None), P(), P(), P(), P(), P(), P(), P(), P())
    out_specs = P(("groups", "wide", "narrow"), None, None)
    return jax.shard_map(
        functools.partial(on_device, mesh.shape["wide"], mesh.shape["narrow"]),
        mesh=mesh,
        in_specs=in_specs,
        out_specs=out_specs,
        check_vma=False,
    )
```

```python
import functools

import jax
import jax.numpy as jnp
from jax import lax
from jax.experimental import pallas as pl
from jax.experimental.pallas import tpu as pltpu
from jax.sharding import PartitionSpec as P

LANES = 128
RIGHT = -1
VMEM_LIMIT = 40 * 1024 * 1024
VMEM_ALL = 62 * 1024 * 1024


def iota(shape, dim):
    return lax.broadcasted_iota(jnp.int32, shape, dim)


def features_kernel(*refs, packs, parts, pieces):
    args, refs = refs[:9], refs[9:]
    outs, wf_hbm, refs = refs[: len(packs)], refs[len(packs)], refs[len(packs) + 1 :]
    held, (lo_ref, hi_ref, left_ref, turned_ref, rows_ref, right_ref, wf_ref, sems) = refs[:9], refs[9:]
    x_ref, gain_ref, bias_ref, lm_ref, lb_ref, rm_ref, rb_ref, w_ref, shift_ref = held
    seqs, residues, depth = x_ref.shape
    hidden = lm_ref.shape[0]
    per = LANES // hidden
    slots = LANES // seqs
    minor = hidden // slots
    groups = residues // per
    own = lax.axis_index("narrow")

    piece = seqs // pieces
    copies = [
        pltpu.make_async_copy(
            args[0].at[pl.ds(p * piece, piece)], x_ref.at[pl.ds(p * piece, piece)], sems.at[p]
        )
        for p in range(pieces)
    ]
    rest = [
        pltpu.make_async_copy(a, b, sems.at[pieces + i]) for i, (a, b) in enumerate(zip(args[1:], held[1:]))
    ]
    for copy in copies[:1] + rest[:2] + copies[1:] + rest[2:]:
        copy.start()
    free = pieces + len(rest)

    def norm(p):
        gain = gain_ref[...].reshape(1, depth)
        bias = bias_ref[...].reshape(1, depth)
        step = min(4, piece)
        for s in range(p * piece, (p + 1) * piece, step):
            x = x_ref[s : s + step].reshape(step * residues, depth).astype(jnp.float32)
            x = x - jnp.mean(x, axis=-1, keepdims=True)
            spread = jnp.mean(x * x, axis=-1, keepdims=True)
            x = x * lax.rsqrt(spread + 1e-05) * gain + bias
            rows = pl.ds(s * residues, step * residues)
            lo_ref[rows, :] = x[:, :LANES]
            hi_ref[rows, :] = x[:, LANES:]

    for copy in rest[:2]:
        copy.wait()
    for p in range(pieces - 1):
        copies[p].wait()
        norm(p)
    for copy in copies[-1:] + rest[2:]:
        copy.wait()
    count = w_ref.shape[0]
    wf_ref[:count] = w_ref[...].astype(jnp.float32)
    wf_ref[count:] = jnp.broadcast_to(shift_ref[...].reshape(1, -1), (8, shift_ref.shape[0]))
    norm(pieces - 1)

    column, row = iota((hidden, LANES), 1) % hidden, iota((hidden, LANES), 0)
    spread_l = (column == row).astype(jnp.float32)
    spread_r = (column == (row ^ (own * minor))).astype(jnp.float32)

    def widen(m, pick):
        return lax.dot_general(
            m, pick.astype(jnp.bfloat16), (((0,), (0,)), ((), ())),
            preferred_element_type=jnp.float32,
        )

    def widen_bias(b, pick):
        b = jnp.broadcast_to(b.reshape(1, hidden), (8, hidden))
        return jnp.dot(
            b, pick, precision=lax.Precision.HIGHEST, preferred_element_type=jnp.float32
        )[:1]

    weights = jnp.concatenate(
        [widen(lm_ref[...], spread_l), widen(rm_ref[...], spread_r)], axis=1
    )
    shift = jnp.concatenate(
        [widen_bias(lb_ref[...], spread_l), widen_bias(rb_ref[...], spread_r)], axis=1
    )
    place = iota((depth, 2 * LANES), 1) % LANES // hidden
    sends = [pltpu.make_async_copy(wf_ref, wf_hbm, sems.at[free])]
    sends[0].start()

    total = None
    for k in range(per):
        part = jnp.concatenate(
            [
                jnp.concatenate(
                    [half[pl.ds(g * per + k, seqs, stride=residues), :] for half in (lo_ref, hi_ref)],
                    axis=1,
                )
                for g in range(groups)
            ],
            axis=0,
        ).astype(jnp.bfloat16)
        placed = jnp.where(place == k, weights, 0.0).astype(jnp.bfloat16)
        term = jnp.dot(part, placed, preferred_element_type=jnp.float32)
        total = term if total is None else total + term
    total = total + shift
    left_ref[...] = total[:, :LANES].astype(left_ref.dtype)

    slot = iota((minor, LANES), 1) // seqs
    for block in range(groups // slots):
        turned_ref[...] = total[block * LANES : (block + 1) * LANES, LANES:].T
        for k in range(per):
            parts_of = [turned_ref[pl.ds(k * hidden + q * minor, minor), :] for q in range(slots)]
            for g in range(slots):
                out = None
                for q in range(slots):
                    moved = parts_of[q]
                    if q != g:
                        moved = pltpu.roll(moved, (q - g) % slots * seqs, axis=1)
                    out = moved if out is None else jnp.where(slot == q, moved, out)
                j = (block * slots + g) * per + k
                rows_ref[pl.ds(j, minor, stride=residues), :] = out
    right_ref[...] = rows_ref[...].astype(right_ref.dtype)

    mine = left_ref.shape[0] // parts
    for out, pack in zip(outs, packs):
        at = 0
        for item in pack:
            if item == RIGHT:
                rows = right_ref
            else:
                rows = left_ref.at[pl.ds(pl.multiple_of((own ^ item) * mine, 16), mine)]
            free += 1
            sends.append(
                pltpu.make_async_copy(rows, out.at[pl.ds(at, rows.shape[0])], sems.at[free])
            )
            sends[-1].start()
            at += rows.shape[0]
    for copy in sends:
        copy.wait()


def block_weights(wf_ref, wide_ref, *, parts, minor):
    cz = wf_ref.shape[1]
    hidden = parts * minor
    half = minor // 2
    rows_each = wide_ref.shape[0] // hidden // hidden
    own = lax.axis_index("narrow")
    wide_ref[...] = jnp.zeros_like(wide_ref)
    for e in range(hidden):
        rows = wf_ref[pl.ds(e ^ (own * minor), hidden, stride=hidden), :].astype(jnp.bfloat16)
        q, e2, t = e // minor, e % minor // half, e % half
        for k in range(rows_each):
            at = ((((q * half + t) * 2 + e2) * rows_each) + k) * hidden
            wide_ref[at : at + hidden, k * cz : (k + 1) * cz] = rows


def pack_kernel(*refs, count):
    out_ref, at = refs[-1], 0
    for ref in refs[:count]:
        out_ref[at : at + ref.shape[0]] = ref[...]
        at += ref.shape[0]


def spread_left(left_of, spread_ref, *, parts):
    seqs = LANES // parts
    low = iota((seqs, LANES), 1) < LANES // 2
    zero = jnp.zeros((seqs, LANES), jnp.float32)
    for m in range(parts):
        left = left_of(m)
        for g in range(left.shape[0] // seqs):
            rows = left[g * seqs : (g + 1) * seqs].astype(jnp.float32)
            turned = pltpu.roll(rows, LANES // 2, axis=1)
            for half, (first, second) in enumerate(((rows, turned), (turned, rows))):
                lanes = pl.ds((2 * g + half) * LANES, LANES)
                spread_ref[m, 0, :, lanes] = jnp.where(low, first, zero).astype(spread_ref.dtype)
                spread_ref[m, 1, :, lanes] = jnp.where(low, zero, second).astype(spread_ref.dtype)


def pair_rows(spread_ref, right_of, wide_ref, shift, outer_ref, store, *, wides, parts, minor, seqs_total):
    cz = shift.shape[1]
    half = minor // 2
    seqs = LANES // parts
    halves = spread_ref.shape[3] // LANES
    residues = right_of(0, 0).shape[0] // minor
    cols = wides * residues
    slot = iota((minor * residues, LANES), 1) // seqs
    for q in range(parts):
        left = jnp.concatenate([spread_ref[q ^ k, i] for i in range(2) for k in range(parts)], axis=0)
        for d in range(wides):
            right = None
            for k in range(parts):
                chunk = right_of(d, q ^ k)
                right = chunk if right is None else jnp.where(slot == k, chunk, right)
            right = jnp.concatenate([right[: half * residues], right[half * residues :]], axis=1)
            outer = jnp.dot(right, left, preferred_element_type=jnp.float32).astype(jnp.bfloat16)
            for t in range(half):
                for g in range(halves):
                    outer_ref[
                        pl.ds(g * cols + d * residues, residues),
                        (q * half + t) * LANES : (q * half + t + 1) * LANES,
                    ] = outer[t * residues : (t + 1) * residues, g * LANES : (g + 1) * LANES]

    pairs = jnp.dot(outer_ref[...], wide_ref[...], preferred_element_type=jnp.float32)
    rows_each = wide_ref.shape[1] // cz
    for g in range(halves):
        for k in range(rows_each):
            pair = pairs[g * cols : (g + 1) * cols, k * cz : (k + 1) * cz]
            store(g * rows_each + k, pair * (1.0 / seqs_total) + shift)


def pair_kernel(*refs, operands, rights, blocks, earlier, lefts=None, **sizes):
    parts, minor = sizes["parts"], sizes["minor"]
    inputs, refs = refs[:operands], refs[operands:]
    if lefts is not None:
        wf_ref, done_ref, spread_ref, wide_ref, shift_ref, outer_ref = refs
        own_rows = done_ref.shape[0]
        block_weights(wf_ref, wide_ref, parts=parts, minor=minor)
        shift_ref[...] = wf_ref[wf_ref.shape[0] - 8 :]
        count = own_rows * minor
        spread_left(lambda m: inputs[lefts[m][0]][lefts[m][1] : lefts[m][1] + count, :], spread_ref, parts=parts)
    elif not earlier:
        spread_ref, wide_ref, shift_ref, done_ref, outer_ref = refs
    else:
        spread_ref, wide_ref, shift_ref = refs[:3]
        before, (out_hbm, outer_ref, done_ref, sems) = refs[3 : 3 + len(earlier)], refs[3 + len(earlier) :]
    residues = done_ref.shape[1] // len(blocks)
    copies = []

    def write(ref, places):
        for d, block in enumerate(places):
            at = pl.multiple_of((lax.axis_index("wide") ^ block) * residues, 16)
            copies.append(
                pltpu.make_async_copy(
                    ref.at[:, pl.ds(d * residues, residues), :],
                    out_hbm.at[:, pl.ds(at, residues), :],
                    sems.at[len(copies)],
                )
            )
            copies[-1].start()

    if earlier:
        for ref, places in zip(before, earlier):
            write(ref, places)

    def right_of(d, m):
        ref, at = rights[m]
        at += d * minor * residues
        return inputs[ref][at : at + minor * residues, :]

    def store(row, pair):
        done_ref[row] = pair.astype(done_ref.dtype)

    pair_rows(spread_ref, right_of, wide_ref, shift_ref[:1], outer_ref, store, wides=len(blocks), **sizes)
    if earlier:
        write(done_ref, blocks)
        for copy in copies:
            copy.wait()


def pair_blocks_kernel(*refs, wides, parts, minor, **sizes):
    left_refs, (right_ref, wf_ref, out_ref, spread_ref, wide_ref, outer_ref) = refs[:parts], refs[parts:]

    @pl.when(pl.program_id(0) == 0)
    def _():
        block_weights(wf_ref, wide_ref, parts=parts, minor=minor)
        spread_left(lambda m: left_refs[m][...], spread_ref, parts=parts)

    def store(row, pair):
        out_ref[row] = pair.astype(out_ref.dtype)

    pair_rows(
        spread_ref, lambda d, m: right_ref[d, m],
        wide_ref, wf_ref[wf_ref.shape[0] - 8 :][:1], outer_ref, store,
        wides=wides, parts=parts, minor=minor, **sizes,
    )


def on_device(wide, narrow, x, gain, bias, lm, lb, rm, rb, w, shift):
    seqs, residues, depth = x.shape
    hidden = lm.shape[1]
    cz = w.shape[1]
    per = LANES // hidden
    slots = LANES // seqs
    minor = hidden // slots
    own_rows = residues // narrow
    groups = own_rows // per
    pieces = 4
    hbm = pl.BlockSpec(memory_space=pltpu.HBM)
    vmem = pl.BlockSpec(memory_space=pltpu.VMEM)
    params = pltpu.CompilerParams(vmem_limit_bytes=VMEM_LIMIT)
    direct = wide == 4 and narrow == 4
    if direct:
        packs = ((0,), (RIGHT,), (1, RIGHT), (2, 3, RIGHT))
    else:
        packs = tuple((m,) for m in range(narrow)) + ((RIGHT,),)
    left_count, right_count = groups * seqs, minor * residues
    args = (x, gain, bias, lm.T, lb, rm.T, rb, w, shift)
    *made, w = pl.pallas_call(
        functools.partial(features_kernel, packs=packs, parts=narrow, pieces=pieces),
        out_shape=tuple(
            jax.ShapeDtypeStruct(
                (sum(right_count if i == RIGHT else left_count for i in pack), LANES), jnp.bfloat16
            )
            for pack in packs
        )
        + (jax.ShapeDtypeStruct((w.shape[0] + 8, cz), jnp.float32),),
        in_specs=[hbm] * len(args),
        out_specs=(hbm,) * (len(packs) + 1),
        scratch_shapes=[pltpu.VMEM(a.shape, a.dtype) for a in args]
        + [
            pltpu.VMEM((seqs * residues, LANES), jnp.float32),
            pltpu.VMEM((seqs * residues, LANES), jnp.float32),
            pltpu.VMEM((residues // per * seqs, LANES), jnp.bfloat16),
            pltpu.VMEM((LANES, LANES), jnp.float32),
            pltpu.VMEM((minor * residues, LANES), jnp.float32),
            pltpu.VMEM((minor * residues, LANES), jnp.bfloat16),
            pltpu.VMEM((w.shape[0] + 8, cz), jnp.float32),
            pltpu.SemaphoreType.DMA((pieces + len(args) + sum(len(pack) for pack in packs),)),
        ],
        compiler_params=pltpu.CompilerParams(vmem_limit_bytes=VMEM_ALL),
        name="features",
    )(*args)

    def across(a, m):
        return lax.ppermute(a, "narrow", [(i, i ^ m) for i in range(narrow)])

    def along(a, d):
        return lax.ppermute(a, "wide", [(i, i ^ d) for i in range(wide)])

    sizes = dict(parts=narrow, minor=minor, seqs_total=seqs * narrow)
    out_shape = jax.ShapeDtypeStruct((own_rows, wide * residues, cz), jnp.bfloat16)
    if direct:
        return pairs_by_block(made, across, along, w, out_shape, residues, sizes, params)

    lefts = [made[0]] + [across(made[m], m) for m in range(1, narrow)]
    every = lax.all_gather(made[narrow], ("wide", "narrow"), axis=0, tiled=False)
    every = every.reshape(wide, narrow, right_count, LANES)
    every = jnp.take(every, lax.axis_index("narrow") ^ jnp.arange(narrow), axis=1)
    block = wide
    while block % 2 == 0 and block * residues > 192:
        block //= 2
    cols = block * residues
    return pl.pallas_call(
        functools.partial(pair_blocks_kernel, wides=block, **sizes),
        grid=(wide // block,),
        in_specs=[pl.BlockSpec((left_count, LANES), lambda b: (0, 0))] * narrow
        + [
            pl.BlockSpec((block, narrow, right_count, LANES), lambda b: (b, 0, 0, 0)),
            pl.BlockSpec(w.shape, lambda b: (0, 0)),
        ],
        out_specs=pl.BlockSpec((own_rows, cols, cz), lambda b: (0, b, 0)),
        out_shape=out_shape,
        scratch_shapes=[
            pltpu.VMEM((narrow, 2, seqs, 2 * groups * LANES), jnp.bfloat16),
            pltpu.VMEM((hidden * LANES // 2, 2 * cz), jnp.bfloat16),
            pltpu.VMEM((2 * groups * cols, hidden * LANES // 2), jnp.bfloat16),
        ],
        compiler_params=params,
        name="pairs",
    )(*lefts, every, w)


def pairs_by_block(made, across, along, w, out_shape, residues, sizes, params):
    left_own, right, to_core, to_chip = made
    left_count, right_count = left_own.shape[0], right.shape[0]
    hbm = pl.BlockSpec(memory_space=pltpu.HBM)
    vmem = pl.BlockSpec(memory_space=pltpu.VMEM)
    own_rows, _, cz = out_shape.shape
    narrow = sizes["parts"]
    hidden = narrow * sizes["minor"]
    groups = own_rows * hidden // LANES

    def pack(*chunks, after):
        return pl.pallas_call(
            functools.partial(pack_kernel, count=len(chunks)),
            out_shape=jax.ShapeDtypeStruct((sum(c.shape[0] for c in chunks), LANES), jnp.bfloat16),
            in_specs=[vmem] * (len(chunks) + len(after)),
            out_specs=vmem,
            compiler_params=params,
            name="pack",
        )(*chunks, *after)

    def pairs(rights, blocks, *shared, lefts=None, earlier=()):
        operands, places = [], []
        for chunks in (rights, lefts or ()):
            places.append([])
            for chunk, at in chunks:
                places[-1].append((len(operands), at))
                operands.append(chunk)
        count = len(operands)
        operands += shared
        cols = len(blocks) * residues
        done = jax.ShapeDtypeStruct((own_rows, cols, cz), jnp.bfloat16)
        shapes, outs = [done], [vmem]
        scratch = [pltpu.VMEM((2 * groups * cols, hidden * LANES // 2), jnp.bfloat16)]
        if lefts is not None:
            shapes += [
                jax.ShapeDtypeStruct((narrow, 2, LANES // narrow, 2 * groups * LANES), jnp.bfloat16),
                jax.ShapeDtypeStruct((hidden * LANES // 2, 2 * cz), jnp.bfloat16),
                jax.ShapeDtypeStruct((8, cz), jnp.float32),
            ]
            outs += [vmem] * 3
        if earlier:
            operands += [ref for ref, _ in earlier]
            shapes, outs = [out_shape], [hbm]
            scratch += [
                pltpu.VMEM(done.shape, done.dtype),
                pltpu.SemaphoreType.DMA((len(blocks) + sum(len(b) for _, b in earlier),)),
            ]
        return pl.pallas_call(
            functools.partial(
                pair_kernel, operands=count, rights=places[0], blocks=blocks,
                earlier=[b for _, b in earlier], lefts=lefts and places[1], **sizes,
            ),
            out_shape=shapes,
            in_specs=[vmem] * len(operands),
            out_specs=outs,
            scratch_shapes=scratch,
            compiler_params=params,
            cost_estimate=pl.CostEstimate(flops=1000, bytes_accessed=1000, transcendentals=0),
            name=f"pairs_{blocks[0]}",
        )(*operands)

    near = along(right, 1)
    core = across(to_core, 1)
    far = pack(along(right, 2), after=(near,))
    last = along(far, 1)
    chip = across(to_chip, 2)
    middle = pack(near, far, after=(core,))
    beside = across(middle, 1)
    both = across(pack(chip, after=(last,)), 1)
    lefts = ((left_own, 0), (core, 0), (chip, 0), (both, left_count))
    own = ((right, 0), (core, left_count), (chip, 2 * left_count), (both, 2 * left_count))
    first, *shared = pairs(own, (0,), w, lefts=lefts)

    other = across(middle, 2)
    onward = across(pack(other, after=(shared[1],)), 1)
    (second,) = pairs(((middle, 0), (beside, 0), (other, 0), (onward, 0)), (1, 2), *shared)

    other = across(last, 2)
    both = across(pack(last, other, after=()), 1)
    (out,) = pairs(
        ((last, 0), (both, 0), (other, 0), (both, right_count)), (3,), *shared,
        earlier=((first, (0,)), (second, (1, 2))),
    )
    return out


def solution(mesh):
    in_specs = (P(("groups", "narrow"), "wide", None), P(), P(), P(), P(), P(), P(), P(), P())
    out_specs = P(("groups", "wide", "narrow"), None, None)
    return jax.shard_map(
        functools.partial(on_device, mesh.shape["wide"], mesh.shape["narrow"]),
        mesh=mesh,
        in_specs=in_specs,
        out_specs=out_specs,
        check_vma=False,
    )
```

```python
import functools

import jax
import jax.numpy as jnp
from jax import lax
from jax.experimental import pallas as pl
from jax.experimental.pallas import tpu as pltpu
from jax.sharding import PartitionSpec as P

LANES = 128
RIGHT = -1
VMEM_LIMIT = 40 * 1024 * 1024
VMEM_ALL = 62 * 1024 * 1024


def iota(shape, dim):
    return lax.broadcasted_iota(jnp.int32, shape, dim)


def features_kernel(*refs, packs, parts, pieces):
    args, refs = refs[:9], refs[9:]
    outs, wf_hbm, refs = refs[: len(packs)], refs[len(packs)], refs[len(packs) + 1 :]
    held, (left_ref, turned_ref, rows_ref, right_ref, wf_ref, sems) = refs[:9], refs[9:]
    x_ref, gain_ref, bias_ref, lm_ref, lb_ref, rm_ref, rb_ref, w_ref, shift_ref = held
    seqs, residues, depth = x_ref.shape
    hidden = lm_ref.shape[0]
    per = LANES // hidden
    slots = LANES // seqs
    minor = hidden // slots
    groups = residues // per
    own = lax.axis_index("narrow")

    piece = seqs // pieces
    copies = [
        pltpu.make_async_copy(
            args[0].at[pl.ds(p * piece, piece)], x_ref.at[pl.ds(p * piece, piece)], sems.at[p]
        )
        for p in range(pieces)
    ]
    rest = [
        pltpu.make_async_copy(a, b, sems.at[pieces + i]) for i, (a, b) in enumerate(zip(args[1:], held[1:]))
    ]
    for copy in copies[:1] + rest[:2] + copies[1:] + rest[2:]:
        copy.start()
    free = pieces + len(rest)

    for copy in rest[:-2]:
        copy.wait()

    column, row = iota((hidden, LANES), 1) % hidden, iota((hidden, LANES), 0)
    spread_l = (column == row).astype(jnp.float32)
    spread_r = (column == (row ^ (own * minor))).astype(jnp.float32)

    def widen(m, pick):
        return lax.dot_general(
            m, pick.astype(jnp.bfloat16), (((0,), (0,)), ((), ())),
            preferred_element_type=jnp.float32,
        )

    def widen_bias(b, pick):
        b = jnp.broadcast_to(b.reshape(1, hidden), (8, hidden))
        return jnp.dot(
            b, pick, precision=lax.Precision.HIGHEST, preferred_element_type=jnp.float32
        )[:1]

    weights = jnp.concatenate(
        [widen(lm_ref[...], spread_l), widen(rm_ref[...], spread_r)], axis=1
    ).astype(jnp.bfloat16)
    shift = jnp.concatenate(
        [widen_bias(lb_ref[...], spread_l), widen_bias(rb_ref[...], spread_r)], axis=1
    )
    gain = gain_ref[...].reshape(1, depth)
    bias = bias_ref[...].reshape(1, depth)
    average = jnp.full((depth, LANES), 1.0 / depth, jnp.bfloat16)

    cols = LANES // piece
    out_row, in_row = iota((LANES // per, LANES), 0), iota((LANES // per, LANES), 1)
    gather = (in_row // cols == out_row % piece) & (in_row % cols // per == out_row // piece)
    gather = gather.astype(jnp.bfloat16)
    rows = piece * residues
    mine = iota((rows, 2 * LANES), 0) % per == iota((rows, 2 * LANES), 1) % LANES // hidden

    grouped = [[] for _ in range(groups)]
    for p in range(pieces):
        copies[p].wait()
        x = x_ref[p * piece : (p + 1) * piece].reshape(rows, depth)
        center = jnp.dot(x, average, preferred_element_type=jnp.float32)
        x = x.astype(jnp.float32)
        x = [x[:, h * LANES : (h + 1) * LANES] - center for h in range(depth // LANES)]
        spread = sum(h * h for h in x)
        scale = lax.rsqrt(jnp.sum(spread, axis=-1, keepdims=True) * (1.0 / depth) + 1e-05)
        x = jnp.concatenate([h * scale for h in x], axis=1) * gain + bias
        y = jnp.dot(x.astype(jnp.bfloat16), weights, preferred_element_type=jnp.float32) + shift
        y = jnp.where(mine, y, 0.0).astype(jnp.bfloat16).reshape(piece, residues, 2 * LANES)
        for b in range(residues // cols):
            block = y[:, b * cols : (b + 1) * cols].reshape(LANES, 2 * LANES)
            block = jnp.dot(gather, block, preferred_element_type=jnp.float32)
            for g in range(cols // per):
                grouped[b * (cols // per) + g].append(block[g * piece : (g + 1) * piece])
    total = jnp.concatenate([rows for group in grouped for rows in group], axis=0)

    for copy in rest[-2:]:
        copy.wait()
    count = w_ref.shape[0]
    wf_ref[:count] = w_ref[...].astype(jnp.float32)
    wf_ref[count:] = jnp.broadcast_to(shift_ref[...].reshape(1, -1), (8, shift_ref.shape[0]))
    sends = [pltpu.make_async_copy(wf_ref, wf_hbm, sems.at[free])]
    sends[0].start()
    left_ref[...] = total[:, :LANES].astype(left_ref.dtype)

    slot = iota((minor, LANES), 1) // seqs
    for block in range(groups // slots):
        turned_ref[...] = total[block * LANES : (block + 1) * LANES, LANES:].T
        for k in range(per):
            parts_of = [turned_ref[pl.ds(k * hidden + q * minor, minor), :] for q in range(slots)]
            for g in range(slots):
                out = None
                for q in range(slots):
                    moved = parts_of[q]
                    if q != g:
                        moved = pltpu.roll(moved, (q - g) % slots * seqs, axis=1)
                    out = moved if out is None else jnp.where(slot == q, moved, out)
                j = (block * slots + g) * per + k
                rows_ref[pl.ds(j * minor, minor), :] = out
    cols = LANES // minor
    out_row, in_row = iota((LANES, LANES), 0), iota((LANES, LANES), 1)
    turn = (in_row // minor == out_row % cols) & (in_row % minor == out_row // cols)
    turn = turn.astype(jnp.bfloat16)
    for b in range(residues // cols):
        block = rows_ref[b * LANES : (b + 1) * LANES].astype(jnp.bfloat16)
        block = jnp.dot(turn, block, preferred_element_type=jnp.float32).astype(right_ref.dtype)
        for e in range(minor):
            at = e * residues + b * cols
            right_ref[at : at + cols] = block[e * cols : (e + 1) * cols]

    mine = left_ref.shape[0] // parts
    for out, pack in zip(outs, packs):
        at = 0
        for item in pack:
            if item == RIGHT:
                rows = right_ref
            else:
                rows = left_ref.at[pl.ds(pl.multiple_of((own ^ item) * mine, 16), mine)]
            free += 1
            sends.append(
                pltpu.make_async_copy(rows, out.at[pl.ds(at, rows.shape[0])], sems.at[free])
            )
            sends[-1].start()
            at += rows.shape[0]
    for copy in sends:
        copy.wait()


def block_weights(wf_ref, wide_ref, *, parts, minor):
    cz = wf_ref.shape[1]
    hidden = parts * minor
    half = minor // 2
    rows_each = wide_ref.shape[0] // hidden // hidden
    own = lax.axis_index("narrow")
    wide_ref[...] = jnp.zeros_like(wide_ref)
    for e in range(hidden):
        rows = wf_ref[pl.ds(e ^ (own * minor), hidden, stride=hidden), :].astype(jnp.bfloat16)
        q, e2, t = e // minor, e % minor // half, e % half
        for k in range(rows_each):
            at = ((((q * half + t) * 2 + e2) * rows_each) + k) * hidden
            wide_ref[at : at + hidden, k * cz : (k + 1) * cz] = rows


def pack_kernel(*refs, count):
    out_ref, at = refs[-1], 0
    for ref in refs[:count]:
        out_ref[at : at + ref.shape[0]] = ref[...]
        at += ref.shape[0]


def spread_left(left_of, spread_ref, *, parts):
    seqs = LANES // parts
    low = iota((seqs, LANES), 1) < LANES // 2
    zero = jnp.zeros((seqs, LANES), jnp.float32)
    for m in range(parts):
        left = left_of(m)
        for g in range(left.shape[0] // seqs):
            rows = left[g * seqs : (g + 1) * seqs].astype(jnp.float32)
            turned = pltpu.roll(rows, LANES // 2, axis=1)
            for half, (first, second) in enumerate(((rows, turned), (turned, rows))):
                lanes = pl.ds((2 * g + half) * LANES, LANES)
                spread_ref[m, 0, :, lanes] = jnp.where(low, first, zero).astype(spread_ref.dtype)
                spread_ref[m, 1, :, lanes] = jnp.where(low, zero, second).astype(spread_ref.dtype)


def pair_rows(spread_ref, right_of, wide_ref, shift, outer_ref, store, *, wides, parts, minor, seqs_total):
    cz = shift.shape[1]
    half = minor // 2
    seqs = LANES // parts
    halves = spread_ref.shape[3] // LANES
    residues = right_of(0, 0).shape[0] // minor
    cols = wides * residues
    slot = iota((minor * residues, LANES), 1) // seqs
    for q in range(parts):
        left = jnp.concatenate([spread_ref[q ^ k, i] for i in range(2) for k in range(parts)], axis=0)
        for d in range(wides):
            right = None
            for k in range(parts):
                chunk = right_of(d, q ^ k)
                right = chunk if right is None else jnp.where(slot == k, chunk, right)
            right = jnp.concatenate([right[: half * residues], right[half * residues :]], axis=1)
            outer = jnp.dot(right, left, preferred_element_type=jnp.float32).astype(jnp.bfloat16)
            for t in range(half):
                for g in range(halves):
                    outer_ref[
                        pl.ds(g * cols + d * residues, residues),
                        (q * half + t) * LANES : (q * half + t + 1) * LANES,
                    ] = outer[t * residues : (t + 1) * residues, g * LANES : (g + 1) * LANES]

    pairs = jnp.dot(outer_ref[...], wide_ref[...], preferred_element_type=jnp.float32)
    rows_each = wide_ref.shape[1] // cz
    for g in range(halves):
        for k in range(rows_each):
            pair = pairs[g * cols : (g + 1) * cols, k * cz : (k + 1) * cz]
            store(g * rows_each + k, pair * (1.0 / seqs_total) + shift)


def pair_kernel(*refs, operands, rights, blocks, earlier, lefts=None, **sizes):
    parts, minor = sizes["parts"], sizes["minor"]
    inputs, refs = refs[:operands], refs[operands:]
    if lefts is not None:
        wf_ref, done_ref, spread_ref, wide_ref, shift_ref, outer_ref = refs
        own_rows = done_ref.shape[0]
        block_weights(wf_ref, wide_ref, parts=parts, minor=minor)
        shift_ref[...] = wf_ref[wf_ref.shape[0] - 8 :]
        count = own_rows * minor
        spread_left(lambda m: inputs[lefts[m][0]][lefts[m][1] : lefts[m][1] + count, :], spread_ref, parts=parts)
    elif not earlier:
        spread_ref, wide_ref, shift_ref, done_ref, outer_ref = refs
    else:
        spread_ref, wide_ref, shift_ref = refs[:3]
        before, (out_hbm, outer_ref, done_ref, sems) = refs[3 : 3 + len(earlier)], refs[3 + len(earlier) :]
    residues = done_ref.shape[1] // len(blocks)
    copies = []

    def write(ref, places):
        for d, block in enumerate(places):
            at = pl.multiple_of((lax.axis_index("wide") ^ block) * residues, 16)
            copies.append(
                pltpu.make_async_copy(
                    ref.at[:, pl.ds(d * residues, residues), :],
                    out_hbm.at[:, pl.ds(at, residues), :],
                    sems.at[len(copies)],
                )
            )
            copies[-1].start()

    if earlier:
        for ref, places in zip(before, earlier):
            write(ref, places)

    def right_of(d, m):
        ref, at = rights[m]
        at += d * minor * residues
        return inputs[ref][at : at + minor * residues, :]

    def store(row, pair):
        done_ref[row] = pair.astype(done_ref.dtype)

    pair_rows(spread_ref, right_of, wide_ref, shift_ref[:1], outer_ref, store, wides=len(blocks), **sizes)
    if earlier:
        write(done_ref, blocks)
        for copy in copies:
            copy.wait()


def pair_blocks_kernel(*refs, wides, parts, minor, **sizes):
    left_refs, (right_ref, wf_ref, out_ref, spread_ref, wide_ref, outer_ref) = refs[:parts], refs[parts:]

    @pl.when(pl.program_id(0) == 0)
    def _():
        block_weights(wf_ref, wide_ref, parts=parts, minor=minor)
        spread_left(lambda m: left_refs[m][...], spread_ref, parts=parts)

    def store(row, pair):
        out_ref[row] = pair.astype(out_ref.dtype)

    pair_rows(
        spread_ref, lambda d, m: right_ref[d, m],
        wide_ref, wf_ref[wf_ref.shape[0] - 8 :][:1], outer_ref, store,
        wides=wides, parts=parts, minor=minor, **sizes,
    )


def on_device(wide, narrow, x, gain, bias, lm, lb, rm, rb, w, shift):
    seqs, residues, depth = x.shape
    hidden = lm.shape[1]
    cz = w.shape[1]
    per = LANES // hidden
    slots = LANES // seqs
    minor = hidden // slots
    own_rows = residues // narrow
    groups = own_rows // per
    pieces = seqs // 8
    hbm = pl.BlockSpec(memory_space=pltpu.HBM)
    vmem = pl.BlockSpec(memory_space=pltpu.VMEM)
    params = pltpu.CompilerParams(vmem_limit_bytes=VMEM_LIMIT)
    direct = wide == 4 and narrow == 4
    if direct:
        packs = ((0,), (RIGHT,), (1, RIGHT), (2, 3, RIGHT))
    else:
        packs = tuple((m,) for m in range(narrow)) + ((RIGHT,),)
    left_count, right_count = groups * seqs, minor * residues
    args = (x, gain, bias, lm.T, lb, rm.T, rb, w, shift)
    *made, w = pl.pallas_call(
        functools.partial(features_kernel, packs=packs, parts=narrow, pieces=pieces),
        out_shape=tuple(
            jax.ShapeDtypeStruct(
                (sum(right_count if i == RIGHT else left_count for i in pack), LANES), jnp.bfloat16
            )
            for pack in packs
        )
        + (jax.ShapeDtypeStruct((w.shape[0] + 8, cz), jnp.float32),),
        in_specs=[hbm] * len(args),
        out_specs=(hbm,) * (len(packs) + 1),
        scratch_shapes=[pltpu.VMEM(a.shape, a.dtype) for a in args]
        + [
            pltpu.VMEM((residues // per * seqs, LANES), jnp.bfloat16),
            pltpu.VMEM((LANES, LANES), jnp.float32),
            pltpu.VMEM((minor * residues, LANES), jnp.float32),
            pltpu.VMEM((minor * residues, LANES), jnp.bfloat16),
            pltpu.VMEM((w.shape[0] + 8, cz), jnp.float32),
            pltpu.SemaphoreType.DMA((pieces + len(args) + sum(len(pack) for pack in packs),)),
        ],
        compiler_params=pltpu.CompilerParams(vmem_limit_bytes=VMEM_ALL),
        name="features",
    )(*args)

    def across(a, m):
        return lax.ppermute(a, "narrow", [(i, i ^ m) for i in range(narrow)])

    def along(a, d):
        return lax.ppermute(a, "wide", [(i, i ^ d) for i in range(wide)])

    sizes = dict(parts=narrow, minor=minor, seqs_total=seqs * narrow)
    out_shape = jax.ShapeDtypeStruct((own_rows, wide * residues, cz), jnp.bfloat16)
    if direct:
        return pairs_by_block(made, across, along, w, out_shape, residues, sizes, params)

    lefts = [made[0]] + [across(made[m], m) for m in range(1, narrow)]
    every = lax.all_gather(made[narrow], ("wide", "narrow"), axis=0, tiled=False)
    every = every.reshape(wide, narrow, right_count, LANES)
    every = jnp.take(every, lax.axis_index("narrow") ^ jnp.arange(narrow), axis=1)
    block = wide
    while block % 2 == 0 and block * residues > 192:
        block //= 2
    cols = block * residues
    return pl.pallas_call(
        functools.partial(pair_blocks_kernel, wides=block, **sizes),
        grid=(wide // block,),
        in_specs=[pl.BlockSpec((left_count, LANES), lambda b: (0, 0))] * narrow
        + [
            pl.BlockSpec((block, narrow, right_count, LANES), lambda b: (b, 0, 0, 0)),
            pl.BlockSpec(w.shape, lambda b: (0, 0)),
        ],
        out_specs=pl.BlockSpec((own_rows, cols, cz), lambda b: (0, b, 0)),
        out_shape=out_shape,
        scratch_shapes=[
            pltpu.VMEM((narrow, 2, seqs, 2 * groups * LANES), jnp.bfloat16),
            pltpu.VMEM((hidden * LANES // 2, 2 * cz), jnp.bfloat16),
            pltpu.VMEM((2 * groups * cols, hidden * LANES // 2), jnp.bfloat16),
        ],
        compiler_params=params,
        name="pairs",
    )(*lefts, every, w)


def pairs_by_block(made, across, along, w, out_shape, residues, sizes, params):
    left_own, right, to_core, to_chip = made
    left_count, right_count = left_own.shape[0], right.shape[0]
    hbm = pl.BlockSpec(memory_space=pltpu.HBM)
    vmem = pl.BlockSpec(memory_space=pltpu.VMEM)
    own_rows, _, cz = out_shape.shape
    narrow = sizes["parts"]
    hidden = narrow * sizes["minor"]
    groups = own_rows * hidden // LANES

    def pack(*chunks, after):
        return pl.pallas_call(
            functools.partial(pack_kernel, count=len(chunks)),
            out_shape=jax.ShapeDtypeStruct((sum(c.shape[0] for c in chunks), LANES), jnp.bfloat16),
            in_specs=[vmem] * (len(chunks) + len(after)),
            out_specs=vmem,
            compiler_params=params,
            name="pack",
        )(*chunks, *after)

    def pairs(rights, blocks, *shared, lefts=None, earlier=()):
        operands, places = [], []
        for chunks in (rights, lefts or ()):
            places.append([])
            for chunk, at in chunks:
                places[-1].append((len(operands), at))
                operands.append(chunk)
        count = len(operands)
        operands += shared
        cols = len(blocks) * residues
        done = jax.ShapeDtypeStruct((own_rows, cols, cz), jnp.bfloat16)
        shapes, outs = [done], [vmem]
        scratch = [pltpu.VMEM((2 * groups * cols, hidden * LANES // 2), jnp.bfloat16)]
        if lefts is not None:
            shapes += [
                jax.ShapeDtypeStruct((narrow, 2, LANES // narrow, 2 * groups * LANES), jnp.bfloat16),
                jax.ShapeDtypeStruct((hidden * LANES // 2, 2 * cz), jnp.bfloat16),
                jax.ShapeDtypeStruct((8, cz), jnp.float32),
            ]
            outs += [vmem] * 3
        if earlier:
            operands += [ref for ref, _ in earlier]
            shapes, outs = [out_shape], [hbm]
            scratch += [
                pltpu.VMEM(done.shape, done.dtype),
                pltpu.SemaphoreType.DMA((len(blocks) + sum(len(b) for _, b in earlier),)),
            ]
        return pl.pallas_call(
            functools.partial(
                pair_kernel, operands=count, rights=places[0], blocks=blocks,
                earlier=[b for _, b in earlier], lefts=lefts and places[1], **sizes,
            ),
            out_shape=shapes,
            in_specs=[vmem] * len(operands),
            out_specs=outs,
            scratch_shapes=scratch,
            compiler_params=params,
            cost_estimate=pl.CostEstimate(flops=1000, bytes_accessed=1000, transcendentals=0),
            name=f"pairs_{blocks[0]}",
        )(*operands)

    far = along(right, 2)
    near = along(right, 1)
    last = along(far, 1)
    chip = across(to_chip, 2)
    core = across(to_core, 1)
    middle = pack(near, far, after=(chip, core))
    beside = across(middle, 1)
    both = across(pack(chip, after=(last,)), 1)
    lefts = ((left_own, 0), (core, 0), (chip, 0), (both, left_count))
    own = ((right, 0), (core, left_count), (chip, 2 * left_count), (both, 2 * left_count))
    first, *shared = pairs(own, (0,), w, lefts=lefts)

    other = across(middle, 2)
    onward = across(pack(other, after=shared[1:2]), 1)
    (second,) = pairs(((middle, 0), (beside, 0), (other, 0), (onward, 0)), (1, 2), *shared)

    other = across(last, 2)
    both = across(pack(last, other, after=()), 1)
    (out,) = pairs(
        ((last, 0), (both, 0), (other, 0), (both, right_count)), (3,), *shared,
        earlier=((first, (0,)), (second, (1, 2))),
    )
    return out


def solution(mesh):
    in_specs = (P(("groups", "narrow"), "wide", None), P(), P(), P(), P(), P(), P(), P(), P())
    out_specs = P(("groups", "wide", "narrow"), None, None)
    return jax.shard_map(
        functools.partial(on_device, mesh.shape["wide"], mesh.shape["narrow"]),
        mesh=mesh,
        in_specs=in_specs,
        out_specs=out_specs,
        check_vma=False,
    )
```

```python
import functools

import jax
import jax.numpy as jnp
from jax import lax
from jax.experimental import pallas as pl
from jax.experimental.pallas import tpu as pltpu
from jax.sharding import PartitionSpec as P

LANES = 128
RIGHT = -1
VMEM_LIMIT = 40 * 1024 * 1024
VMEM_ALL = 62 * 1024 * 1024


def iota(shape, dim):
    return lax.broadcasted_iota(jnp.int32, shape, dim)


def features_kernel(*refs, packs, parts, pieces):
    args, passed, refs = refs[:7], refs[7:9], refs[9:]
    outs, refs = refs[: len(packs) + 2], refs[len(packs) + 2 :]
    held, (lo_ref, hi_ref, left_ref, turned_ref, rows_ref, right_ref, sems) = refs[:7], refs[7:]
    x_ref, gain_ref, bias_ref, lm_ref, lb_ref, rm_ref, rb_ref = held
    seqs, residues, depth = x_ref.shape
    hidden = lm_ref.shape[0]
    per = LANES // hidden
    slots = LANES // seqs
    minor = hidden // slots
    groups = residues // per
    own = lax.axis_index("narrow")

    piece = seqs // pieces
    copies = [
        pltpu.make_async_copy(
            args[0].at[pl.ds(p * piece, piece)], x_ref.at[pl.ds(p * piece, piece)], sems.at[p]
        )
        for p in range(pieces)
    ]
    rest = [
        pltpu.make_async_copy(a, b, sems.at[pieces + i]) for i, (a, b) in enumerate(zip(args[1:], held[1:]))
    ]
    free = pieces + len(rest)
    sends = [pltpu.make_async_copy(a, b, sems.at[free + i]) for i, (a, b) in enumerate(zip(passed, outs[-2:]))]
    free += len(sends)
    for copy in copies + rest + sends:
        copy.start()
    for copy in copies + rest:
        copy.wait()

    column, row = iota((hidden, LANES), 1) % hidden, iota((hidden, LANES), 0)
    spread_l = (column == row).astype(jnp.float32)
    spread_r = (column == (row ^ (own * minor))).astype(jnp.float32)

    def widen(m, pick):
        return lax.dot_general(
            m, pick.astype(jnp.bfloat16), (((0,), (0,)), ((), ())),
            preferred_element_type=jnp.float32,
        )

    def widen_bias(b, pick):
        b = jnp.broadcast_to(b.reshape(1, hidden), (8, hidden))
        return jnp.dot(
            b, pick, precision=lax.Precision.HIGHEST, preferred_element_type=jnp.float32
        )[:1]

    weights = jnp.concatenate(
        [widen(lm_ref[...], spread_l), widen(rm_ref[...], spread_r)], axis=1
    )
    shift = jnp.concatenate(
        [widen_bias(lb_ref[...], spread_l), widen_bias(rb_ref[...], spread_r)], axis=1
    )
    place = iota((depth, 2 * LANES), 1) % LANES // hidden

    gain = gain_ref[...].reshape(1, depth)
    bias = bias_ref[...].reshape(1, depth)
    step = 4
    for s in range(0, seqs, step):
        x = x_ref[s : s + step].reshape(step * residues, depth).astype(jnp.float32)
        x = x - jnp.mean(x, axis=-1, keepdims=True)
        spread = jnp.mean(x * x, axis=-1, keepdims=True)
        x = x * lax.rsqrt(spread + 1e-05) * gain + bias
        rows = pl.ds(s * residues, step * residues)
        lo_ref[rows, :] = x[:, :LANES]
        hi_ref[rows, :] = x[:, LANES:]

    total = None
    for k in range(per):
        part = jnp.concatenate(
            [
                jnp.concatenate(
                    [half[pl.ds(g * per + k, seqs, stride=residues), :] for half in (lo_ref, hi_ref)],
                    axis=1,
                )
                for g in range(groups)
            ],
            axis=0,
        ).astype(jnp.bfloat16)
        placed = jnp.where(place == k, weights, 0.0).astype(jnp.bfloat16)
        term = jnp.dot(part, placed, preferred_element_type=jnp.float32)
        total = term if total is None else total + term
    total = total + shift
    left_ref[...] = total[:, :LANES].astype(left_ref.dtype)

    slot = iota((minor, LANES), 1) // seqs
    for block in range(groups // slots):
        turned_ref[...] = total[block * LANES : (block + 1) * LANES, LANES:].T
        for k in range(per):
            parts_of = [turned_ref[pl.ds(k * hidden + q * minor, minor), :] for q in range(slots)]
            for g in range(slots):
                out = None
                for q in range(slots):
                    moved = parts_of[q]
                    if q != g:
                        moved = pltpu.roll(moved, (q - g) % slots * seqs, axis=1)
                    out = moved if out is None else jnp.where(slot == q, moved, out)
                j = (block * slots + g) * per + k
                rows_ref[pl.ds(j, minor, stride=residues), :] = out
    right_ref[...] = rows_ref[...].astype(right_ref.dtype)

    mine = left_ref.shape[0] // parts
    for out, pack in zip(outs, packs):
        at = 0
        for item in pack:
            if item == RIGHT:
                rows = right_ref
            else:
                rows = left_ref.at[pl.ds(pl.multiple_of((own ^ item) * mine, 16), mine)]
            sends.append(
                pltpu.make_async_copy(rows, out.at[pl.ds(at, rows.shape[0])], sems.at[free])
            )
            free += 1
            sends[-1].start()
            at += rows.shape[0]
    for copy in sends:
        copy.wait()


def block_weights(w_ref, wide_ref, wf_ref, *, parts, minor):
    cz = wf_ref.shape[1]
    hidden = parts * minor
    half = minor // 2
    rows_each = wide_ref.shape[0] // hidden // hidden
    own = lax.axis_index("narrow")
    wide_ref[...] = jnp.zeros_like(wide_ref)
    wf_ref[...] = w_ref[...].astype(jnp.float32)
    for e in range(hidden):
        rows = wf_ref[pl.ds(e ^ (own * minor), hidden, stride=hidden), :].astype(jnp.bfloat16)
        q, e2, t = e // minor, e % minor // half, e % half
        for k in range(rows_each):
            at = ((((q * half + t) * 2 + e2) * rows_each) + k) * hidden
            wide_ref[at : at + hidden, k * cz : (k + 1) * cz] = rows


def pack_kernel(*refs, count):
    out_ref, at = refs[-1], 0
    for ref in refs[:count]:
        out_ref[at : at + ref.shape[0]] = ref[...]
        at += ref.shape[0]


def spread_left(left_of, spread_ref, *, parts):
    seqs = LANES // parts
    low = iota((seqs, LANES), 1) < LANES // 2
    zero = jnp.zeros((seqs, LANES), jnp.float32)
    for m in range(parts):
        left = left_of(m)
        for g in range(left.shape[0] // seqs):
            rows = left[g * seqs : (g + 1) * seqs].astype(jnp.float32)
            turned = pltpu.roll(rows, LANES // 2, axis=1)
            for half, (first, second) in enumerate(((rows, turned), (turned, rows))):
                lanes = pl.ds((2 * g + half) * LANES, LANES)
                spread_ref[m, 0, :, lanes] = jnp.where(low, first, zero).astype(spread_ref.dtype)
                spread_ref[m, 1, :, lanes] = jnp.where(low, zero, second).astype(spread_ref.dtype)


def pair_rows(spread_ref, right_of, wide_ref, shift, outer_ref, store, *, wides, parts, minor, seqs_total):
    cz = shift.shape[1]
    half = minor // 2
    seqs = LANES // parts
    halves = spread_ref.shape[3] // LANES
    residues = right_of(0, 0).shape[0] // minor
    cols = wides * residues
    slot = iota((minor * residues, LANES), 1) // seqs
    for q in range(parts):
        left = jnp.concatenate([spread_ref[q ^ k, i] for i in range(2) for k in range(parts)], axis=0)
        for d in range(wides):
            right = None
            for k in range(parts):
                chunk = right_of(d, q ^ k)
                right = chunk if right is None else jnp.where(slot == k, chunk, right)
            right = jnp.concatenate([right[: half * residues], right[half * residues :]], axis=1)
            outer = jnp.dot(right, left, preferred_element_type=jnp.float32).astype(jnp.bfloat16)
            for t in range(half):
                for g in range(halves):
                    outer_ref[
                        pl.ds(g * cols + d * residues, residues),
                        (q * half + t) * LANES : (q * half + t + 1) * LANES,
                    ] = outer[t * residues : (t + 1) * residues, g * LANES : (g + 1) * LANES]

    pairs = jnp.dot(outer_ref[...], wide_ref[...], preferred_element_type=jnp.float32)
    rows_each = wide_ref.shape[1] // cz
    for g in range(halves):
        for k in range(rows_each):
            pair = pairs[g * cols : (g + 1) * cols, k * cz : (k + 1) * cz]
            store(g * rows_each + k, pair * (1.0 / seqs_total) + shift)


def pair_kernel(*refs, operands, rights, blocks, earlier, lefts=None, **sizes):
    parts, minor = sizes["parts"], sizes["minor"]
    inputs, refs = refs[:operands], refs[operands:]
    if lefts is not None:
        w_ref, shift_ref, done_ref, spread_ref, wide_ref, outer_ref, wf_ref = refs
        own_rows = done_ref.shape[0]
        block_weights(w_ref, wide_ref, wf_ref, parts=parts, minor=minor)
        count = own_rows * minor
        spread_left(lambda m: inputs[lefts[m][0]][lefts[m][1] : lefts[m][1] + count, :], spread_ref, parts=parts)
    elif not earlier:
        spread_ref, wide_ref, shift_ref, done_ref, outer_ref = refs
    else:
        spread_ref, wide_ref, shift_ref = refs[:3]
        before, (out_hbm, outer_ref, done_ref, sems) = refs[3 : 3 + len(earlier)], refs[3 + len(earlier) :]
    residues = done_ref.shape[1] // len(blocks)
    copies = []

    def write(ref, places):
        for d, block in enumerate(places):
            at = pl.multiple_of((lax.axis_index("wide") ^ block) * residues, 16)
            copies.append(
                pltpu.make_async_copy(
                    ref.at[:, pl.ds(d * residues, residues), :],
                    out_hbm.at[:, pl.ds(at, residues), :],
                    sems.at[len(copies)],
                )
            )
            copies[-1].start()

    if earlier:
        for ref, places in zip(before, earlier):
            write(ref, places)

    def right_of(d, m):
        ref, at = rights[m]
        at += d * minor * residues
        return inputs[ref][at : at + minor * residues, :]

    def store(row, pair):
        done_ref[row] = pair.astype(done_ref.dtype)

    shift = shift_ref[...].reshape(1, -1)
    pair_rows(spread_ref, right_of, wide_ref, shift, outer_ref, store, wides=len(blocks), **sizes)
    if earlier:
        write(done_ref, blocks)
        for copy in copies:
            copy.wait()


def pair_blocks_kernel(*refs, wides, parts, minor, **sizes):
    left_refs, refs = refs[:parts], refs[parts:]
    right_ref, w_ref, shift_ref, out_ref, spread_ref, wide_ref, outer_ref, wf_ref = refs

    @pl.when(pl.program_id(0) == 0)
    def _():
        block_weights(w_ref, wide_ref, wf_ref, parts=parts, minor=minor)
        spread_left(lambda m: left_refs[m][...], spread_ref, parts=parts)

    def store(row, pair):
        out_ref[row] = pair.astype(out_ref.dtype)

    pair_rows(
        spread_ref, lambda d, m: right_ref[d, m],
        wide_ref, shift_ref[...].reshape(1, -1), outer_ref, store,
        wides=wides, parts=parts, minor=minor, **sizes,
    )


def on_device(wide, narrow, x, gain, bias, lm, lb, rm, rb, w, shift):
    seqs, residues, depth = x.shape
    hidden = lm.shape[1]
    cz = w.shape[1]
    per = LANES // hidden
    slots = LANES // seqs
    minor = hidden // slots
    own_rows = residues // narrow
    groups = own_rows // per
    pieces = 4
    hbm = pl.BlockSpec(memory_space=pltpu.HBM)
    vmem = pl.BlockSpec(memory_space=pltpu.VMEM)
    params = pltpu.CompilerParams(vmem_limit_bytes=VMEM_LIMIT)
    direct = wide == 4 and narrow == 4
    if direct:
        packs = ((0,), (RIGHT,), (1, RIGHT), (2, 3, RIGHT))
    else:
        packs = tuple((m,) for m in range(narrow)) + ((RIGHT,),)
    left_count, right_count = groups * seqs, minor * residues
    args = (x, gain, bias, lm.T, lb, rm.T, rb, w, shift)
    *made, w, shift = pl.pallas_call(
        functools.partial(features_kernel, packs=packs, parts=narrow, pieces=pieces),
        out_shape=tuple(
            jax.ShapeDtypeStruct(
                (sum(right_count if i == RIGHT else left_count for i in pack), LANES), jnp.bfloat16
            )
            for pack in packs
        )
        + (jax.ShapeDtypeStruct(w.shape, w.dtype), jax.ShapeDtypeStruct(shift.shape, shift.dtype)),
        in_specs=[hbm] * len(args),
        out_specs=(hbm,) * (len(packs) + 2),
        scratch_shapes=[pltpu.VMEM(a.shape, a.dtype) for a in args[:7]]
        + [
            pltpu.VMEM((seqs * residues, LANES), jnp.float32),
            pltpu.VMEM((seqs * residues, LANES), jnp.float32),
            pltpu.VMEM((residues // per * seqs, LANES), jnp.bfloat16),
            pltpu.VMEM((LANES, LANES), jnp.float32),
            pltpu.VMEM((minor * residues, LANES), jnp.float32),
            pltpu.VMEM((minor * residues, LANES), jnp.bfloat16),
            pltpu.SemaphoreType.DMA((pieces + len(args) + sum(len(pack) for pack in packs),)),
        ],
        compiler_params=pltpu.CompilerParams(vmem_limit_bytes=VMEM_ALL),
        name="features",
    )(*args)

    def across(a, m):
        return lax.ppermute(a, "narrow", [(i, i ^ m) for i in range(narrow)])

    def along(a, d):
        return lax.ppermute(a, "wide", [(i, i ^ d) for i in range(wide)])

    sizes = dict(parts=narrow, minor=minor, seqs_total=seqs * narrow)
    out_shape = jax.ShapeDtypeStruct((own_rows, wide * residues, cz), jnp.bfloat16)
    if direct:
        return pairs_by_block(made, across, along, w, shift, out_shape, residues, sizes, params)

    lefts = [made[0]] + [across(made[m], m) for m in range(1, narrow)]
    every = lax.all_gather(made[narrow], ("wide", "narrow"), axis=0, tiled=False)
    every = every.reshape(wide, narrow, right_count, LANES)
    every = jnp.take(every, lax.axis_index("narrow") ^ jnp.arange(narrow), axis=1)
    block = wide
    while block % 2 == 0 and block * residues > 192:
        block //= 2
    cols = block * residues
    return pl.pallas_call(
        functools.partial(pair_blocks_kernel, wides=block, **sizes),
        grid=(wide // block,),
        in_specs=[pl.BlockSpec((left_count, LANES), lambda b: (0, 0))] * narrow
        + [
            pl.BlockSpec((block, narrow, right_count, LANES), lambda b: (b, 0, 0, 0)),
            pl.BlockSpec(w.shape, lambda b: (0, 0)),
            pl.BlockSpec(shift.shape, lambda b: (0,)),
        ],
        out_specs=pl.BlockSpec((own_rows, cols, cz), lambda b: (0, b, 0)),
        out_shape=out_shape,
        scratch_shapes=[
            pltpu.VMEM((narrow, 2, seqs, 2 * groups * LANES), jnp.bfloat16),
            pltpu.VMEM((hidden * LANES // 2, 2 * cz), jnp.bfloat16),
            pltpu.VMEM((2 * groups * cols, hidden * LANES // 2), jnp.bfloat16),
            pltpu.VMEM(w.shape, jnp.float32),
        ],
        compiler_params=params,
        name="pairs",
    )(*lefts, every, w, shift)


def pairs_by_block(made, across, along, w, shift, out_shape, residues, sizes, params):
    left_own, right, to_core, to_chip = made
    left_count, right_count = left_own.shape[0], right.shape[0]
    hbm = pl.BlockSpec(memory_space=pltpu.HBM)
    vmem = pl.BlockSpec(memory_space=pltpu.VMEM)
    own_rows, _, cz = out_shape.shape
    narrow = sizes["parts"]
    hidden = narrow * sizes["minor"]
    groups = own_rows * hidden // LANES

    def pack(*chunks, after):
        return pl.pallas_call(
            functools.partial(pack_kernel, count=len(chunks)),
            out_shape=jax.ShapeDtypeStruct((sum(c.shape[0] for c in chunks), LANES), jnp.bfloat16),
            in_specs=[vmem] * (len(chunks) + len(after)),
            out_specs=vmem,
            compiler_params=params,
            name="pack",
        )(*chunks, *after)

    def pairs(rights, blocks, *shared, lefts=None, earlier=()):
        operands, places = [], []
        for chunks in (rights, lefts or ()):
            places.append([])
            for chunk, at in chunks:
                places[-1].append((len(operands), at))
                operands.append(chunk)
        count = len(operands)
        operands += shared
        cols = len(blocks) * residues
        done = jax.ShapeDtypeStruct((own_rows, cols, cz), jnp.bfloat16)
        shapes, outs = [done], [vmem]
        scratch = [pltpu.VMEM((2 * groups * cols, hidden * LANES // 2), jnp.bfloat16)]
        if lefts is not None:
            shapes += [
                jax.ShapeDtypeStruct((narrow, 2, LANES // narrow, 2 * groups * LANES), jnp.bfloat16),
                jax.ShapeDtypeStruct((hidden * LANES // 2, 2 * cz), jnp.bfloat16),
            ]
            outs += [vmem] * 2
            scratch.append(pltpu.VMEM(w.shape, jnp.float32))
        if earlier:
            operands += [ref for ref, _ in earlier]
            shapes, outs = [out_shape], [hbm]
            scratch += [
                pltpu.VMEM(done.shape, done.dtype),
                pltpu.SemaphoreType.DMA((len(blocks) + sum(len(b) for _, b in earlier),)),
            ]
        return pl.pallas_call(
            functools.partial(
                pair_kernel, operands=count, rights=places[0], blocks=blocks,
                earlier=[b for _, b in earlier], lefts=lefts and places[1], **sizes,
            ),
            out_shape=shapes,
            in_specs=[vmem] * len(operands),
            out_specs=outs,
            scratch_shapes=scratch,
            compiler_params=params,
            cost_estimate=pl.CostEstimate(flops=1000, bytes_accessed=1000, transcendentals=0),
            name=f"pairs_{blocks[0]}",
        )(*operands)

    far = along(right, 2)
    near = along(right, 1)
    last = along(far, 1)
    chip = across(to_chip, 2)
    core = across(to_core, 1)
    middle = pack(near, far, after=(chip, core))
    beside = across(middle, 1)
    both = across(pack(chip, after=(last,)), 1)
    lefts = ((left_own, 0), (core, 0), (chip, 0), (both, left_count))
    own = ((right, 0), (core, left_count), (chip, 2 * left_count), (both, 2 * left_count))
    first, *shared = pairs(own, (0,), w, shift, lefts=lefts)
    shared.append(shift)

    other = across(middle, 2)
    onward = across(pack(other, after=shared[1:2]), 1)
    (second,) = pairs(((middle, 0), (beside, 0), (other, 0), (onward, 0)), (1, 2), *shared)

    other = across(last, 2)
    both = across(pack(last, other, after=()), 1)
    (out,) = pairs(
        ((last, 0), (both, 0), (other, 0), (both, right_count)), (3,), *shared,
        earlier=((first, (0,)), (second, (1, 2))),
    )
    return out


def solution(mesh):
    in_specs = (P(("groups", "narrow"), "wide", None), P(), P(), P(), P(), P(), P(), P(), P())
    out_specs = P(("groups", "wide", "narrow"), None, None)
    return jax.shard_map(
        functools.partial(on_device, mesh.shape["wide"], mesh.shape["narrow"]),
        mesh=mesh,
        in_specs=in_specs,
        out_specs=out_specs,
        check_vma=False,
    )
```

```python
import functools

import jax
import jax.numpy as jnp
from jax import lax
from jax.experimental import pallas as pl
from jax.experimental.pallas import tpu as pltpu
from jax.sharding import PartitionSpec as P

LANES = 128
RIGHT = -1
VMEM_LIMIT = 40 * 1024 * 1024
VMEM_ALL = 62 * 1024 * 1024


def iota(shape, dim):
    return lax.broadcasted_iota(jnp.int32, shape, dim)


def features_kernel(*refs, packs, parts, pieces):
    args, refs = refs[:9], refs[9:]
    outs, wf_hbm, refs = refs[: len(packs)], refs[len(packs)], refs[len(packs) + 1 :]
    held, (lo_ref, hi_ref, left_ref, turned_ref, rows_ref, right_ref, wf_ref, sems) = refs[:9], refs[9:]
    x_ref, gain_ref, bias_ref, lm_ref, lb_ref, rm_ref, rb_ref, w_ref, shift_ref = held
    seqs, residues, depth = x_ref.shape
    hidden = lm_ref.shape[0]
    per = LANES // hidden
    slots = LANES // seqs
    minor = hidden // slots
    groups = residues // per
    own = lax.axis_index("narrow")

    piece = seqs // pieces
    copies = [
        pltpu.make_async_copy(
            args[0].at[pl.ds(p * piece, piece)], x_ref.at[pl.ds(p * piece, piece)], sems.at[p]
        )
        for p in range(pieces)
    ]
    rest = [
        pltpu.make_async_copy(a, b, sems.at[pieces + i]) for i, (a, b) in enumerate(zip(args[1:], held[1:]))
    ]
    for copy in copies[:1] + rest[:2] + copies[1:] + rest[2:]:
        copy.start()
    free = pieces + len(rest)

    def norm(p):
        gain = gain_ref[...].reshape(1, depth)
        bias = bias_ref[...].reshape(1, depth)
        step = min(4, piece)
        for s in range(p * piece, (p + 1) * piece, step):
            x = x_ref[s : s + step].reshape(step * residues, depth).astype(jnp.float32)
            x = x - jnp.mean(x, axis=-1, keepdims=True)
            spread = jnp.mean(x * x, axis=-1, keepdims=True)
            x = x * lax.rsqrt(spread + 1e-05) * gain + bias
            rows = pl.ds(s * residues, step * residues)
            lo_ref[rows, :] = x[:, :LANES]
            hi_ref[rows, :] = x[:, LANES:]

    for copy in rest[:2]:
        copy.wait()
    for p in range(pieces - 1):
        copies[p].wait()
        norm(p)
    for copy in copies[-1:] + rest[2:]:
        copy.wait()
    count = w_ref.shape[0]
    wf_ref[:count] = w_ref[...].astype(jnp.float32)
    wf_ref[count:] = jnp.broadcast_to(shift_ref[...].reshape(1, -1), (8, shift_ref.shape[0]))
    norm(pieces - 1)

    column, row = iota((hidden, LANES), 1) % hidden, iota((hidden, LANES), 0)
    spread_l = (column == row).astype(jnp.float32)
    spread_r = (column == (row ^ (own * minor))).astype(jnp.float32)

    def widen(m, pick):
        return lax.dot_general(
            m, pick.astype(jnp.bfloat16), (((0,), (0,)), ((), ())),
            preferred_element_type=jnp.float32,
        )

    def widen_bias(b, pick):
        b = jnp.broadcast_to(b.reshape(1, hidden), (8, hidden))
        return jnp.dot(
            b, pick, precision=lax.Precision.HIGHEST, preferred_element_type=jnp.float32
        )[:1]

    weights = jnp.concatenate(
        [widen(lm_ref[...], spread_l), widen(rm_ref[...], spread_r)], axis=1
    )
    shift = jnp.concatenate(
        [widen_bias(lb_ref[...], spread_l), widen_bias(rb_ref[...], spread_r)], axis=1
    )
    place = iota((depth, 2 * LANES), 1) % LANES // hidden
    sends = [pltpu.make_async_copy(wf_ref, wf_hbm, sems.at[free])]
    sends[0].start()

    total = None
    for k in range(per):
        part = jnp.concatenate(
            [
                jnp.concatenate(
                    [half[pl.ds(g * per + k, seqs, stride=residues), :] for half in (lo_ref, hi_ref)],
                    axis=1,
                )
                for g in range(groups)
            ],
            axis=0,
        ).astype(jnp.bfloat16)
        placed = jnp.where(place == k, weights, 0.0).astype(jnp.bfloat16)
        term = jnp.dot(part, placed, preferred_element_type=jnp.float32)
        total = term if total is None else total + term
    total = total + shift
    left_ref[...] = total[:, :LANES].astype(left_ref.dtype)

    slot = iota((minor, LANES), 1) // seqs
    for block in range(groups // slots):
        turned_ref[...] = total[block * LANES : (block + 1) * LANES, LANES:].T
        for k in range(per):
            parts_of = [turned_ref[pl.ds(k * hidden + q * minor, minor), :] for q in range(slots)]
            for g in range(slots):
                out = None
                for q in range(slots):
                    moved = parts_of[q]
                    if q != g:
                        moved = pltpu.roll(moved, (q - g) % slots * seqs, axis=1)
                    out = moved if out is None else jnp.where(slot == q, moved, out)
                j = (block * slots + g) * per + k
                rows_ref[pl.ds(j, minor, stride=residues), :] = out
    right_ref[...] = rows_ref[...].astype(right_ref.dtype)

    mine = left_ref.shape[0] // parts
    for out, pack in zip(outs, packs):
        at = 0
        for item in pack:
            if item == RIGHT:
                rows = right_ref
            else:
                rows = left_ref.at[pl.ds(pl.multiple_of((own ^ item) * mine, 16), mine)]
            free += 1
            sends.append(
                pltpu.make_async_copy(rows, out.at[pl.ds(at, rows.shape[0])], sems.at[free])
            )
            sends[-1].start()
            at += rows.shape[0]
    for copy in sends:
        copy.wait()


def block_weights(wf_ref, wide_ref, *, parts, minor):
    cz = wf_ref.shape[1]
    hidden = parts * minor
    half = minor // 2
    rows_each = wide_ref.shape[0] // hidden // hidden
    own = lax.axis_index("narrow")
    wide_ref[...] = jnp.zeros_like(wide_ref)
    for e in range(hidden):
        rows = wf_ref[pl.ds(e ^ (own * minor), hidden, stride=hidden), :].astype(jnp.bfloat16)
        q, e2, t = e // minor, e % minor // half, e % half
        for k in range(rows_each):
            at = ((((q * half + t) * 2 + e2) * rows_each) + k) * hidden
            wide_ref[at : at + hidden, k * cz : (k + 1) * cz] = rows


def pack_kernel(*refs, count):
    out_ref, at = refs[-1], 0
    for ref in refs[:count]:
        out_ref[at : at + ref.shape[0]] = ref[...]
        at += ref.shape[0]


def spread_left(left_of, spread_ref, *, parts):
    seqs = LANES // parts
    low = iota((seqs, LANES), 1) < LANES // 2
    zero = jnp.zeros((seqs, LANES), jnp.float32)
    for m in range(parts):
        left = left_of(m)
        for g in range(left.shape[0] // seqs):
            rows = left[g * seqs : (g + 1) * seqs].astype(jnp.float32)
            turned = pltpu.roll(rows, LANES // 2, axis=1)
            for half, (first, second) in enumerate(((rows, turned), (turned, rows))):
                lanes = pl.ds((2 * g + half) * LANES, LANES)
                spread_ref[m, 0, :, lanes] = jnp.where(low, first, zero).astype(spread_ref.dtype)
                spread_ref[m, 1, :, lanes] = jnp.where(low, zero, second).astype(spread_ref.dtype)


def pair_rows(spread_ref, right_of, wide_ref, shift, outer_ref, store, *, wides, parts, minor, seqs_total):
    cz = shift.shape[1]
    half = minor // 2
    seqs = LANES // parts
    halves = spread_ref.shape[3] // LANES
    residues = right_of(0, 0).shape[0] // minor
    cols = wides * residues
    slot = iota((minor * residues, LANES), 1) // seqs
    for q in range(parts):
        left = jnp.concatenate([spread_ref[q ^ k, i] for i in range(2) for k in range(parts)], axis=0)
        for d in range(wides):
            right = None
            for k in range(parts):
                chunk = right_of(d, q ^ k)
                right = chunk if right is None else jnp.where(slot == k, chunk, right)
            right = jnp.concatenate([right[: half * residues], right[half * residues :]], axis=1)
            outer = jnp.dot(right, left, preferred_element_type=jnp.float32).astype(jnp.bfloat16)
            for t in range(half):
                for g in range(halves):
                    outer_ref[
                        pl.ds(g * cols + d * residues, residues),
                        (q * half + t) * LANES : (q * half + t + 1) * LANES,
                    ] = outer[t * residues : (t + 1) * residues, g * LANES : (g + 1) * LANES]

    pairs = jnp.dot(outer_ref[...], wide_ref[...], preferred_element_type=jnp.float32)
    rows_each = wide_ref.shape[1] // cz
    for g in range(halves):
        for k in range(rows_each):
            pair = pairs[g * cols : (g + 1) * cols, k * cz : (k + 1) * cz]
            store(g * rows_each + k, pair * (1.0 / seqs_total) + shift)


def pair_kernel(*refs, operands, rights, blocks, earlier, lefts=None, **sizes):
    parts, minor = sizes["parts"], sizes["minor"]
    inputs, refs = refs[:operands], refs[operands:]
    if lefts is not None:
        wf_ref, done_ref, spread_ref, wide_ref, shift_ref, outer_ref = refs
        own_rows = done_ref.shape[0]
        block_weights(wf_ref, wide_ref, parts=parts, minor=minor)
        shift_ref[...] = wf_ref[wf_ref.shape[0] - 8 :]
        count = own_rows * minor
        spread_left(lambda m: inputs[lefts[m][0]][lefts[m][1] : lefts[m][1] + count, :], spread_ref, parts=parts)
    elif not earlier:
        spread_ref, wide_ref, shift_ref, done_ref, outer_ref = refs
    else:
        spread_ref, wide_ref, shift_ref = refs[:3]
        before, (out_hbm, outer_ref, done_ref, sems) = refs[3 : 3 + len(earlier)], refs[3 + len(earlier) :]
    residues = done_ref.shape[1] // len(blocks)
    copies = []

    def write(ref, places):
        for d, block in enumerate(places):
            at = pl.multiple_of((lax.axis_index("wide") ^ block) * residues, 16)
            copies.append(
                pltpu.make_async_copy(
                    ref.at[:, pl.ds(d * residues, residues), :],
                    out_hbm.at[:, pl.ds(at, residues), :],
                    sems.at[len(copies)],
                )
            )
            copies[-1].start()

    if earlier:
        for ref, places in zip(before, earlier):
            write(ref, places)

    def right_of(d, m):
        ref, at = rights[m]
        at += d * minor * residues
        return inputs[ref][at : at + minor * residues, :]

    def store(row, pair):
        done_ref[row] = pair.astype(done_ref.dtype)

    pair_rows(spread_ref, right_of, wide_ref, shift_ref[:1], outer_ref, store, wides=len(blocks), **sizes)
    if earlier:
        write(done_ref, blocks)
        for copy in copies:
            copy.wait()


def pair_blocks_kernel(*refs, wides, parts, minor, **sizes):
    left_refs, (right_ref, wf_ref, out_ref, spread_ref, wide_ref, outer_ref) = refs[:parts], refs[parts:]

    @pl.when(pl.program_id(0) == 0)
    def _():
        block_weights(wf_ref, wide_ref, parts=parts, minor=minor)
        spread_left(lambda m: left_refs[m][...], spread_ref, parts=parts)

    def store(row, pair):
        out_ref[row] = pair.astype(out_ref.dtype)

    pair_rows(
        spread_ref, lambda d, m: right_ref[d, m],
        wide_ref, wf_ref[wf_ref.shape[0] - 8 :][:1], outer_ref, store,
        wides=wides, parts=parts, minor=minor, **sizes,
    )


def on_device(wide, narrow, x, gain, bias, lm, lb, rm, rb, w, shift):
    seqs, residues, depth = x.shape
    hidden = lm.shape[1]
    cz = w.shape[1]
    per = LANES // hidden
    slots = LANES // seqs
    minor = hidden // slots
    own_rows = residues // narrow
    groups = own_rows // per
    pieces = 4
    hbm = pl.BlockSpec(memory_space=pltpu.HBM)
    vmem = pl.BlockSpec(memory_space=pltpu.VMEM)
    params = pltpu.CompilerParams(vmem_limit_bytes=VMEM_LIMIT)
    direct = wide == 4 and narrow == 4
    if direct:
        packs = ((0,), (RIGHT,), (1, RIGHT), (2, 3, RIGHT))
    else:
        packs = tuple((m,) for m in range(narrow)) + ((RIGHT,),)
    left_count, right_count = groups * seqs, minor * residues
    args = (x, gain, bias, lm.T, lb, rm.T, rb, w, shift)
    *made, w = pl.pallas_call(
        functools.partial(features_kernel, packs=packs, parts=narrow, pieces=pieces),
        out_shape=tuple(
            jax.ShapeDtypeStruct(
                (sum(right_count if i == RIGHT else left_count for i in pack), LANES), jnp.bfloat16
            )
            for pack in packs
        )
        + (jax.ShapeDtypeStruct((w.shape[0] + 8, cz), jnp.float32),),
        in_specs=[hbm] * len(args),
        out_specs=(hbm,) * (len(packs) + 1),
        scratch_shapes=[pltpu.VMEM(a.shape, a.dtype) for a in args]
        + [
            pltpu.VMEM((seqs * residues, LANES), jnp.float32),
            pltpu.VMEM((seqs * residues, LANES), jnp.float32),
            pltpu.VMEM((residues // per * seqs, LANES), jnp.bfloat16),
            pltpu.VMEM((LANES, LANES), jnp.float32),
            pltpu.VMEM((minor * residues, LANES), jnp.float32),
            pltpu.VMEM((minor * residues, LANES), jnp.bfloat16),
            pltpu.VMEM((w.shape[0] + 8, cz), jnp.float32),
            pltpu.SemaphoreType.DMA((pieces + len(args) + sum(len(pack) for pack in packs),)),
        ],
        compiler_params=pltpu.CompilerParams(vmem_limit_bytes=VMEM_ALL),
        name="features",
    )(*args)

    def across(a, m):
        return lax.ppermute(a, "narrow", [(i, i ^ m) for i in range(narrow)])

    def along(a, d):
        return lax.ppermute(a, "wide", [(i, i ^ d) for i in range(wide)])

    sizes = dict(parts=narrow, minor=minor, seqs_total=seqs * narrow)
    out_shape = jax.ShapeDtypeStruct((own_rows, wide * residues, cz), jnp.bfloat16)
    if direct:
        return pairs_by_block(made, across, along, w, out_shape, residues, sizes, params)

    lefts = [made[0]] + [across(made[m], m) for m in range(1, narrow)]
    every = lax.all_gather(made[narrow], ("wide", "narrow"), axis=0, tiled=False)
    every = every.reshape(wide, narrow, right_count, LANES)
    every = jnp.take(every, lax.axis_index("narrow") ^ jnp.arange(narrow), axis=1)
    block = wide
    while block % 2 == 0 and block * residues > 192:
        block //= 2
    cols = block * residues
    return pl.pallas_call(
        functools.partial(pair_blocks_kernel, wides=block, **sizes),
        grid=(wide // block,),
        in_specs=[pl.BlockSpec((left_count, LANES), lambda b: (0, 0))] * narrow
        + [
            pl.BlockSpec((block, narrow, right_count, LANES), lambda b: (b, 0, 0, 0)),
            pl.BlockSpec(w.shape, lambda b: (0, 0)),
        ],
        out_specs=pl.BlockSpec((own_rows, cols, cz), lambda b: (0, b, 0)),
        out_shape=out_shape,
        scratch_shapes=[
            pltpu.VMEM((narrow, 2, seqs, 2 * groups * LANES), jnp.bfloat16),
            pltpu.VMEM((hidden * LANES // 2, 2 * cz), jnp.bfloat16),
            pltpu.VMEM((2 * groups * cols, hidden * LANES // 2), jnp.bfloat16),
        ],
        compiler_params=params,
        name="pairs",
    )(*lefts, every, w)


def pairs_by_block(made, across, along, w, out_shape, residues, sizes, params):
    left_own, right, to_core, to_chip = made
    left_count, right_count = left_own.shape[0], right.shape[0]
    hbm = pl.BlockSpec(memory_space=pltpu.HBM)
    vmem = pl.BlockSpec(memory_space=pltpu.VMEM)
    own_rows, _, cz = out_shape.shape
    narrow = sizes["parts"]
    hidden = narrow * sizes["minor"]
    groups = own_rows * hidden // LANES

    def pack(*chunks, after, weight=1):
        return pl.pallas_call(
            functools.partial(pack_kernel, count=len(chunks)),
            out_shape=jax.ShapeDtypeStruct((sum(c.shape[0] for c in chunks), LANES), jnp.bfloat16),
            in_specs=[vmem] * (len(chunks) + len(after)),
            out_specs=vmem,
            compiler_params=params,
            cost_estimate=pl.CostEstimate(flops=weight, bytes_accessed=1000, transcendentals=0),
            name="pack",
        )(*chunks, *after)

    def pairs(rights, blocks, *shared, lefts=None, earlier=()):
        operands, places = [], []
        for chunks in (rights, lefts or ()):
            places.append([])
            for chunk, at in chunks:
                places[-1].append((len(operands), at))
                operands.append(chunk)
        count = len(operands)
        operands += shared
        cols = len(blocks) * residues
        done = jax.ShapeDtypeStruct((own_rows, cols, cz), jnp.bfloat16)
        shapes, outs = [done], [vmem]
        scratch = [pltpu.VMEM((2 * groups * cols, hidden * LANES // 2), jnp.bfloat16)]
        if lefts is not None:
            shapes += [
                jax.ShapeDtypeStruct((narrow, 2, LANES // narrow, 2 * groups * LANES), jnp.bfloat16),
                jax.ShapeDtypeStruct((hidden * LANES // 2, 2 * cz), jnp.bfloat16),
                jax.ShapeDtypeStruct((8, cz), jnp.float32),
            ]
            outs += [vmem] * 3
        if earlier:
            operands += [ref for ref, _ in earlier]
            shapes, outs = [out_shape], [hbm]
            scratch += [
                pltpu.VMEM(done.shape, done.dtype),
                pltpu.SemaphoreType.DMA((len(blocks) + sum(len(b) for _, b in earlier),)),
            ]
        return pl.pallas_call(
            functools.partial(
                pair_kernel, operands=count, rights=places[0], blocks=blocks,
                earlier=[b for _, b in earlier], lefts=lefts and places[1], **sizes,
            ),
            out_shape=shapes,
            in_specs=[vmem] * len(operands),
            out_specs=outs,
            scratch_shapes=scratch,
            compiler_params=params,
            cost_estimate=pl.CostEstimate(flops=1000, bytes_accessed=1000, transcendentals=0),
            name=f"pairs_{blocks[0]}",
        )(*operands)

    far = along(right, 2)
    near = along(right, 1)
    last = along(far, 1)
    chip = across(to_chip, 2)
    core = across(to_core, 1)
    middle = pack(near, far, after=(), weight=4_000_000_000)
    beside = across(middle, 1)
    both = across(pack(chip, after=(last, core)), 1)
    lefts = ((left_own, 0), (core, 0), (chip, 0), (both, left_count))
    own = ((right, 0), (core, left_count), (chip, 2 * left_count), (both, 2 * left_count))
    first, *shared = pairs(own, (0,), w, lefts=lefts)

    other = across(middle, 2)
    onward = across(pack(other, after=(shared[1],)), 1)
    (second,) = pairs(((middle, 0), (beside, 0), (other, 0), (onward, 0)), (1, 2), *shared)

    other = across(last, 2)
    both = across(pack(last, other, after=()), 1)
    (out,) = pairs(
        ((last, 0), (both, 0), (other, 0), (both, right_count)), (3,), *shared,
        earlier=((first, (0,)), (second, (1, 2))),
    )
    return out


def solution(mesh):
    in_specs = (P(("groups", "narrow"), "wide", None), P(), P(), P(), P(), P(), P(), P(), P())
    out_specs = P(("groups", "wide", "narrow"), None, None)
    return jax.shard_map(
        functools.partial(on_device, mesh.shape["wide"], mesh.shape["narrow"]),
        mesh=mesh,
        in_specs=in_specs,
        out_specs=out_specs,
        check_vma=False,
    )
```

```python
import functools

import jax
import jax.numpy as jnp
from jax import lax
from jax.experimental import pallas as pl
from jax.experimental.pallas import tpu as pltpu
from jax.sharding import PartitionSpec as P

LANES = 128
RIGHT = -1
VMEM_LIMIT = 40 * 1024 * 1024
VMEM_ALL = 62 * 1024 * 1024


def iota(shape, dim):
    return lax.broadcasted_iota(jnp.int32, shape, dim)


def features_kernel(*refs, packs, parts, pieces):
    args, refs = refs[:9], refs[9:]
    outs, wf_hbm, refs = refs[: len(packs)], refs[len(packs)], refs[len(packs) + 1 :]
    held, (lo_ref, hi_ref, left_ref, turned_ref, rows_ref, right_ref, wf_ref, sems) = refs[:9], refs[9:]
    x_ref, gain_ref, bias_ref, lm_ref, lb_ref, rm_ref, rb_ref, w_ref, shift_ref = held
    seqs, residues, depth = x_ref.shape
    hidden = lm_ref.shape[0]
    per = LANES // hidden
    slots = LANES // seqs
    minor = hidden // slots
    groups = residues // per
    own = lax.axis_index("narrow")

    piece = seqs // pieces
    copies = [
        pltpu.make_async_copy(
            args[0].at[pl.ds(p * piece, piece)], x_ref.at[pl.ds(p * piece, piece)], sems.at[p]
        )
        for p in range(pieces)
    ]
    rest = [
        pltpu.make_async_copy(a, b, sems.at[pieces + i]) for i, (a, b) in enumerate(zip(args[1:], held[1:]))
    ]
    for copy in copies[:1] + rest[:2] + copies[1:] + rest[2:]:
        copy.start()
    free = pieces + len(rest)

    def norm(p):
        gain = gain_ref[...].reshape(1, depth)
        bias = bias_ref[...].reshape(1, depth)
        step = min(4, piece)
        for s in range(p * piece, (p + 1) * piece, step):
            x = x_ref[s : s + step].reshape(step * residues, depth).astype(jnp.float32)
            x = x - jnp.mean(x, axis=-1, keepdims=True)
            spread = jnp.mean(x * x, axis=-1, keepdims=True)
            x = x * lax.rsqrt(spread + 1e-05) * gain + bias
            rows = pl.ds(s * residues, step * residues)
            lo_ref[rows, :] = x[:, :LANES]
            hi_ref[rows, :] = x[:, LANES:]

    for copy in rest[:2]:
        copy.wait()
    for p in range(pieces - 1):
        copies[p].wait()
        norm(p)
    for copy in copies[-1:] + rest[2:]:
        copy.wait()
    count = w_ref.shape[0]
    wf_ref[:count] = w_ref[...].astype(jnp.float32)
    wf_ref[count:] = jnp.broadcast_to(shift_ref[...].reshape(1, -1), (8, shift_ref.shape[0]))
    norm(pieces - 1)

    column, row = iota((hidden, LANES), 1) % hidden, iota((hidden, LANES), 0)
    spread_l = (column == row).astype(jnp.float32)
    spread_r = (column == (row ^ (own * minor))).astype(jnp.float32)

    def widen(m, pick):
        return lax.dot_general(
            m, pick.astype(jnp.bfloat16), (((0,), (0,)), ((), ())),
            preferred_element_type=jnp.float32,
        )

    def widen_bias(b, pick):
        b = jnp.broadcast_to(b.reshape(1, hidden), (8, hidden))
        return jnp.dot(
            b, pick, precision=lax.Precision.HIGHEST, preferred_element_type=jnp.float32
        )[:1]

    weights = jnp.concatenate(
        [widen(lm_ref[...], spread_l), widen(rm_ref[...], spread_r)], axis=1
    )
    shift = jnp.concatenate(
        [widen_bias(lb_ref[...], spread_l), widen_bias(rb_ref[...], spread_r)], axis=1
    )
    place = iota((depth, 2 * LANES), 1) % LANES // hidden
    sends = [pltpu.make_async_copy(wf_ref, wf_hbm, sems.at[free])]
    sends[0].start()

    total = None
    for k in range(per):
        part = jnp.concatenate(
            [
                jnp.concatenate(
                    [half[pl.ds(g * per + k, seqs, stride=residues), :] for half in (lo_ref, hi_ref)],
                    axis=1,
                )
                for g in range(groups)
            ],
            axis=0,
        ).astype(jnp.bfloat16)
        placed = jnp.where(place == k, weights, 0.0).astype(jnp.bfloat16)
        term = jnp.dot(part, placed, preferred_element_type=jnp.float32)
        total = term if total is None else total + term
    total = total + shift
    left_ref[...] = total[:, :LANES].astype(left_ref.dtype)

    slot = iota((minor, LANES), 1) // seqs
    for block in range(groups // slots):
        turned_ref[...] = total[block * LANES : (block + 1) * LANES, LANES:].T
        for k in range(per):
            parts_of = [turned_ref[pl.ds(k * hidden + q * minor, minor), :] for q in range(slots)]
            for g in range(slots):
                out = None
                for q in range(slots):
                    moved = parts_of[q]
                    if q != g:
                        moved = pltpu.roll(moved, (q - g) % slots * seqs, axis=1)
                    out = moved if out is None else jnp.where(slot == q, moved, out)
                j = (block * slots + g) * per + k
                rows_ref[pl.ds(j, minor, stride=residues), :] = out
    right_ref[...] = rows_ref[...].astype(right_ref.dtype)

    mine = left_ref.shape[0] // parts
    for out, pack in zip(outs, packs):
        at = 0
        for item in pack:
            if item == RIGHT:
                rows = right_ref
            else:
                rows = left_ref.at[pl.ds(pl.multiple_of((own ^ item) * mine, 16), mine)]
            free += 1
            sends.append(
                pltpu.make_async_copy(rows, out.at[pl.ds(at, rows.shape[0])], sems.at[free])
            )
            sends[-1].start()
            at += rows.shape[0]
    for copy in sends:
        copy.wait()


def block_weights(wf_ref, wide_ref, *, parts, minor):
    cz = wf_ref.shape[1]
    hidden = parts * minor
    half = minor // 2
    rows_each = wide_ref.shape[0] // hidden // hidden
    own = lax.axis_index("narrow")
    wide_ref[...] = jnp.zeros_like(wide_ref)
    for e in range(hidden):
        rows = wf_ref[pl.ds(e ^ (own * minor), hidden, stride=hidden), :].astype(jnp.bfloat16)
        q, e2, t = e // minor, e % minor // half, e % half
        for k in range(rows_each):
            at = ((((q * half + t) * 2 + e2) * rows_each) + k) * hidden
            wide_ref[at : at + hidden, k * cz : (k + 1) * cz] = rows


def pack_kernel(*refs, count):
    out_ref, at = refs[-1], 0
    for ref in refs[:count]:
        out_ref[at : at + ref.shape[0]] = ref[...]
        at += ref.shape[0]


def spread_left(left_of, spread_ref, *, parts):
    seqs = LANES // parts
    low = iota((seqs, LANES), 1) < LANES // 2
    zero = jnp.zeros((seqs, LANES), jnp.float32)
    for m in range(parts):
        left = left_of(m)
        for g in range(left.shape[0] // seqs):
            rows = left[g * seqs : (g + 1) * seqs].astype(jnp.float32)
            turned = pltpu.roll(rows, LANES // 2, axis=1)
            for half, (first, second) in enumerate(((rows, turned), (turned, rows))):
                lanes = pl.ds((2 * g + half) * LANES, LANES)
                spread_ref[m, 0, :, lanes] = jnp.where(low, first, zero).astype(spread_ref.dtype)
                spread_ref[m, 1, :, lanes] = jnp.where(low, zero, second).astype(spread_ref.dtype)


def pair_rows(spread_ref, right_of, wide_ref, shift, outer_ref, store, *, wides, parts, minor, seqs_total):
    cz = shift.shape[1]
    half = minor // 2
    seqs = LANES // parts
    halves = spread_ref.shape[3] // LANES
    residues = right_of(0, 0).shape[0] // minor
    cols = wides * residues
    slot = iota((minor * residues, LANES), 1) // seqs
    width = half * LANES

    def outer_of(q):
        left = jnp.concatenate([spread_ref[q ^ k, i] for i in range(2) for k in range(parts)], axis=0)
        for d in range(wides):
            right = None
            for k in range(parts):
                chunk = right_of(d, q ^ k)
                right = chunk if right is None else jnp.where(slot == k, chunk, right)
            right = jnp.concatenate([right[: half * residues], right[half * residues :]], axis=1)
            outer = jnp.dot(right, left, preferred_element_type=jnp.float32).astype(jnp.bfloat16)
            for t in range(half):
                for g in range(halves):
                    outer_ref[
                        pl.ds(g * cols + d * residues, residues),
                        q * width + t * LANES : q * width + (t + 1) * LANES,
                    ] = outer[t * residues : (t + 1) * residues, g * LANES : (g + 1) * LANES]

    def share_of(q):
        lanes = slice(q * width, (q + 1) * width)
        return jnp.dot(outer_ref[:, lanes], wide_ref[lanes], preferred_element_type=jnp.float32)

    outer_of(0)
    pairs = None
    for q in range(1, parts + 1):
        if q < parts:
            outer_of(q)
        share = share_of(q - 1)
        pairs = share if pairs is None else pairs + share
    rows_each = wide_ref.shape[1] // cz
    for g in range(halves):
        for k in range(rows_each):
            pair = pairs[g * cols : (g + 1) * cols, k * cz : (k + 1) * cz]
            store(g * rows_each + k, pair * (1.0 / seqs_total) + shift)


def pair_kernel(*refs, operands, rights, blocks, earlier, lefts=None, **sizes):
    parts, minor = sizes["parts"], sizes["minor"]
    inputs, refs = refs[:operands], refs[operands:]
    if lefts is not None:
        wf_ref, done_ref, spread_ref, wide_ref, shift_ref, outer_ref = refs
        own_rows = done_ref.shape[0]
        block_weights(wf_ref, wide_ref, parts=parts, minor=minor)
        shift_ref[...] = wf_ref[wf_ref.shape[0] - 8 :]
        count = own_rows * minor
        spread_left(lambda m: inputs[lefts[m][0]][lefts[m][1] : lefts[m][1] + count, :], spread_ref, parts=parts)
    elif not earlier:
        spread_ref, wide_ref, shift_ref, done_ref, outer_ref = refs
    else:
        spread_ref, wide_ref, shift_ref = refs[:3]
        before, (out_hbm, outer_ref, done_ref, sems) = refs[3 : 3 + len(earlier)], refs[3 + len(earlier) :]
    residues = done_ref.shape[1] // len(blocks)
    copies = []

    def write(ref, places):
        for d, block in enumerate(places):
            at = pl.multiple_of((lax.axis_index("wide") ^ block) * residues, 16)
            copies.append(
                pltpu.make_async_copy(
                    ref.at[:, pl.ds(d * residues, residues), :],
                    out_hbm.at[:, pl.ds(at, residues), :],
                    sems.at[len(copies)],
                )
            )
            copies[-1].start()

    if earlier:
        for ref, places in zip(before, earlier):
            write(ref, places)

    def right_of(d, m):
        ref, at = rights[m]
        at += d * minor * residues
        return inputs[ref][at : at + minor * residues, :]

    def store(row, pair):
        done_ref[row] = pair.astype(done_ref.dtype)

    pair_rows(spread_ref, right_of, wide_ref, shift_ref[:1], outer_ref, store, wides=len(blocks), **sizes)
    if earlier:
        write(done_ref, blocks)
        for copy in copies:
            copy.wait()


def pair_blocks_kernel(*refs, wides, parts, minor, **sizes):
    left_refs, (right_ref, wf_ref, out_ref, spread_ref, wide_ref, outer_ref) = refs[:parts], refs[parts:]

    @pl.when(pl.program_id(0) == 0)
    def _():
        block_weights(wf_ref, wide_ref, parts=parts, minor=minor)
        spread_left(lambda m: left_refs[m][...], spread_ref, parts=parts)

    def store(row, pair):
        out_ref[row] = pair.astype(out_ref.dtype)

    pair_rows(
        spread_ref, lambda d, m: right_ref[d, m],
        wide_ref, wf_ref[wf_ref.shape[0] - 8 :][:1], outer_ref, store,
        wides=wides, parts=parts, minor=minor, **sizes,
    )


def on_device(wide, narrow, x, gain, bias, lm, lb, rm, rb, w, shift):
    seqs, residues, depth = x.shape
    hidden = lm.shape[1]
    cz = w.shape[1]
    per = LANES // hidden
    slots = LANES // seqs
    minor = hidden // slots
    own_rows = residues // narrow
    groups = own_rows // per
    pieces = 4
    hbm = pl.BlockSpec(memory_space=pltpu.HBM)
    vmem = pl.BlockSpec(memory_space=pltpu.VMEM)
    params = pltpu.CompilerParams(vmem_limit_bytes=VMEM_LIMIT)
    direct = wide == 4 and narrow == 4
    if direct:
        packs = ((0,), (RIGHT,), (1, RIGHT), (2, 3, RIGHT))
    else:
        packs = tuple((m,) for m in range(narrow)) + ((RIGHT,),)
    left_count, right_count = groups * seqs, minor * residues
    args = (x, gain, bias, lm.T, lb, rm.T, rb, w, shift)
    *made, w = pl.pallas_call(
        functools.partial(features_kernel, packs=packs, parts=narrow, pieces=pieces),
        out_shape=tuple(
            jax.ShapeDtypeStruct(
                (sum(right_count if i == RIGHT else left_count for i in pack), LANES), jnp.bfloat16
            )
            for pack in packs
        )
        + (jax.ShapeDtypeStruct((w.shape[0] + 8, cz), jnp.float32),),
        in_specs=[hbm] * len(args),
        out_specs=(hbm,) * (len(packs) + 1),
        scratch_shapes=[pltpu.VMEM(a.shape, a.dtype) for a in args]
        + [
            pltpu.VMEM((seqs * residues, LANES), jnp.float32),
            pltpu.VMEM((seqs * residues, LANES), jnp.float32),
            pltpu.VMEM((residues // per * seqs, LANES), jnp.bfloat16),
            pltpu.VMEM((LANES, LANES), jnp.float32),
            pltpu.VMEM((minor * residues, LANES), jnp.float32),
            pltpu.VMEM((minor * residues, LANES), jnp.bfloat16),
            pltpu.VMEM((w.shape[0] + 8, cz), jnp.float32),
            pltpu.SemaphoreType.DMA((pieces + len(args) + sum(len(pack) for pack in packs),)),
        ],
        compiler_params=pltpu.CompilerParams(vmem_limit_bytes=VMEM_ALL),
        name="features",
    )(*args)

    def across(a, m):
        return lax.ppermute(a, "narrow", [(i, i ^ m) for i in range(narrow)])

    def along(a, d):
        return lax.ppermute(a, "wide", [(i, i ^ d) for i in range(wide)])

    sizes = dict(parts=narrow, minor=minor, seqs_total=seqs * narrow)
    out_shape = jax.ShapeDtypeStruct((own_rows, wide * residues, cz), jnp.bfloat16)
    if direct:
        return pairs_by_block(made, across, along, w, out_shape, residues, sizes, params)

    lefts = [made[0]] + [across(made[m], m) for m in range(1, narrow)]
    every = lax.all_gather(made[narrow], ("wide", "narrow"), axis=0, tiled=False)
    every = every.reshape(wide, narrow, right_count, LANES)
    every = jnp.take(every, lax.axis_index("narrow") ^ jnp.arange(narrow), axis=1)
    block = wide
    while block % 2 == 0 and block * residues > 192:
        block //= 2
    cols = block * residues
    return pl.pallas_call(
        functools.partial(pair_blocks_kernel, wides=block, **sizes),
        grid=(wide // block,),
        in_specs=[pl.BlockSpec((left_count, LANES), lambda b: (0, 0))] * narrow
        + [
            pl.BlockSpec((block, narrow, right_count, LANES), lambda b: (b, 0, 0, 0)),
            pl.BlockSpec(w.shape, lambda b: (0, 0)),
        ],
        out_specs=pl.BlockSpec((own_rows, cols, cz), lambda b: (0, b, 0)),
        out_shape=out_shape,
        scratch_shapes=[
            pltpu.VMEM((narrow, 2, seqs, 2 * groups * LANES), jnp.bfloat16),
            pltpu.VMEM((hidden * LANES // 2, 2 * cz), jnp.bfloat16),
            pltpu.VMEM((2 * groups * cols, hidden * LANES // 2), jnp.bfloat16),
        ],
        compiler_params=params,
        name="pairs",
    )(*lefts, every, w)


def pairs_by_block(made, across, along, w, out_shape, residues, sizes, params):
    left_own, right, to_core, to_chip = made
    left_count, right_count = left_own.shape[0], right.shape[0]
    hbm = pl.BlockSpec(memory_space=pltpu.HBM)
    vmem = pl.BlockSpec(memory_space=pltpu.VMEM)
    own_rows, _, cz = out_shape.shape
    narrow = sizes["parts"]
    hidden = narrow * sizes["minor"]
    groups = own_rows * hidden // LANES

    def pack(*chunks, after, weight=1):
        return pl.pallas_call(
            functools.partial(pack_kernel, count=len(chunks)),
            out_shape=jax.ShapeDtypeStruct((sum(c.shape[0] for c in chunks), LANES), jnp.bfloat16),
            in_specs=[vmem] * (len(chunks) + len(after)),
            out_specs=vmem,
            compiler_params=params,
            cost_estimate=pl.CostEstimate(flops=weight, bytes_accessed=1000, transcendentals=0),
            name="pack",
        )(*chunks, *after)

    def pairs(rights, blocks, *shared, lefts=None, earlier=()):
        operands, places = [], []
        for chunks in (rights, lefts or ()):
            places.append([])
            for chunk, at in chunks:
                places[-1].append((len(operands), at))
                operands.append(chunk)
        count = len(operands)
        operands += shared
        cols = len(blocks) * residues
        done = jax.ShapeDtypeStruct((own_rows, cols, cz), jnp.bfloat16)
        shapes, outs = [done], [vmem]
        scratch = [pltpu.VMEM((2 * groups * cols, hidden * LANES // 2), jnp.bfloat16)]
        if lefts is not None:
            shapes += [
                jax.ShapeDtypeStruct((narrow, 2, LANES // narrow, 2 * groups * LANES), jnp.bfloat16),
                jax.ShapeDtypeStruct((hidden * LANES // 2, 2 * cz), jnp.bfloat16),
                jax.ShapeDtypeStruct((8, cz), jnp.float32),
            ]
            outs += [vmem] * 3
        if earlier:
            operands += [ref for ref, _ in earlier]
            shapes, outs = [out_shape], [hbm]
            scratch += [
                pltpu.VMEM(done.shape, done.dtype),
                pltpu.SemaphoreType.DMA((len(blocks) + sum(len(b) for _, b in earlier),)),
            ]
        return pl.pallas_call(
            functools.partial(
                pair_kernel, operands=count, rights=places[0], blocks=blocks,
                earlier=[b for _, b in earlier], lefts=lefts and places[1], **sizes,
            ),
            out_shape=shapes,
            in_specs=[vmem] * len(operands),
            out_specs=outs,
            scratch_shapes=scratch,
            compiler_params=params,
            cost_estimate=pl.CostEstimate(flops=1000, bytes_accessed=1000, transcendentals=0),
            name=f"pairs_{blocks[0]}",
        )(*operands)

    far = along(right, 2)
    near = along(right, 1)
    last = along(far, 1)
    chip = across(to_chip, 2)
    core = across(to_core, 1)
    middle = pack(near, far, after=(), weight=4_000_000_000)
    beside = across(middle, 1)
    both = across(pack(chip, after=(last, core)), 1)
    lefts = ((left_own, 0), (core, 0), (chip, 0), (both, left_count))
    own = ((right, 0), (core, left_count), (chip, 2 * left_count), (both, 2 * left_count))
    first, *shared = pairs(own, (0,), w, lefts=lefts)

    other = across(middle, 2)
    onward = across(pack(other, after=(shared[1],)), 1)
    (second,) = pairs(((middle, 0), (beside, 0), (other, 0), (onward, 0)), (1, 2), *shared)

    other = across(last, 2)
    both = across(pack(last, other, after=()), 1)
    (out,) = pairs(
        ((last, 0), (both, 0), (other, 0), (both, right_count)), (3,), *shared,
        earlier=((first, (0,)), (second, (1, 2))),
    )
    return out


def solution(mesh):
    in_specs = (P(("groups", "narrow"), "wide", None), P(), P(), P(), P(), P(), P(), P(), P())
    out_specs = P(("groups", "wide", "narrow"), None, None)
    return jax.shard_map(
        functools.partial(on_device, mesh.shape["wide"], mesh.shape["narrow"]),
        mesh=mesh,
        in_specs=in_specs,
        out_specs=out_specs,
        check_vma=False,
    )
```

```python
import functools

import jax
import jax.numpy as jnp
from jax import lax
from jax.experimental import pallas as pl
from jax.experimental.pallas import tpu as pltpu
from jax.sharding import PartitionSpec as P

LANES = 128
RIGHT = -1
VMEM_LIMIT = 40 * 1024 * 1024
VMEM_ALL = 62 * 1024 * 1024


def iota(shape, dim):
    return lax.broadcasted_iota(jnp.int32, shape, dim)


def features_kernel(*refs, packs, parts, pieces):
    args, refs = refs[:9], refs[9:]
    outs, wf_hbm, refs = refs[: len(packs)], refs[len(packs)], refs[len(packs) + 1 :]
    held, (lo_ref, hi_ref, left_ref, turned_ref, rows_ref, right_ref, wf_ref, sems) = refs[:9], refs[9:]
    x_ref, gain_ref, bias_ref, lm_ref, lb_ref, rm_ref, rb_ref, w_ref, shift_ref = held
    seqs, residues, depth = x_ref.shape
    hidden = lm_ref.shape[0]
    per = LANES // hidden
    slots = LANES // seqs
    minor = hidden // slots
    groups = residues // per
    own = lax.axis_index("narrow")

    piece = seqs // pieces
    copies = [
        pltpu.make_async_copy(
            args[0].at[pl.ds(p * piece, piece)], x_ref.at[pl.ds(p * piece, piece)], sems.at[p]
        )
        for p in range(pieces)
    ]
    rest = [
        pltpu.make_async_copy(a, b, sems.at[pieces + i]) for i, (a, b) in enumerate(zip(args[1:], held[1:]))
    ]
    for copy in copies[:1] + rest[:2] + copies[1:] + rest[2:]:
        copy.start()
    free = pieces + len(rest)

    for copy in copies + rest:
        copy.wait()

    gain = gain_ref[...].reshape(1, depth)
    bias = bias_ref[...].reshape(1, depth)
    average = jnp.full((depth, LANES), 1.0 / depth, jnp.bfloat16)
    span = piece * residues

    def centered(p, center):
        x = x_ref[p * piece : (p + 1) * piece].reshape(span, depth).astype(jnp.float32)
        return [x[:, h * LANES : (h + 1) * LANES] - center for h in range(depth // LANES)]

    centers = [
        jnp.dot(
            x_ref[p * piece : (p + 1) * piece].reshape(span, depth), average,
            preferred_element_type=jnp.float32,
        )
        for p in range(pieces)
    ]
    spreads = []
    for p in range(pieces):
        square = sum(h * h for h in centered(p, centers[p]))
        coarse = square.astype(jnp.bfloat16)
        fine = (square - coarse.astype(jnp.float32)).astype(jnp.bfloat16)
        spreads.append(
            jnp.dot(
                jnp.concatenate([coarse, fine], axis=1), average, preferred_element_type=jnp.float32
            )
        )
    for p in range(pieces):
        scale = lax.rsqrt(spreads[p] + 1e-05)
        for h, ref in zip(range(depth // LANES), (lo_ref, hi_ref)):
            lanes = slice(h * LANES, (h + 1) * LANES)
            ref[p * span : (p + 1) * span, :] = (
                centered(p, centers[p])[h] * scale * gain[:, lanes] + bias[:, lanes]
            )

    count = w_ref.shape[0]
    wf_ref[:count] = w_ref[...].astype(jnp.float32)
    wf_ref[count:] = jnp.broadcast_to(shift_ref[...].reshape(1, -1), (8, shift_ref.shape[0]))

    column, row = iota((hidden, LANES), 1) % hidden, iota((hidden, LANES), 0)
    spread_l = (column == row).astype(jnp.float32)
    spread_r = (column == (row ^ (own * minor))).astype(jnp.float32)

    def widen(m, pick):
        return lax.dot_general(
            m, pick.astype(jnp.bfloat16), (((0,), (0,)), ((), ())),
            preferred_element_type=jnp.float32,
        )

    def widen_bias(b, pick):
        b = jnp.broadcast_to(b.reshape(1, hidden), (8, hidden))
        return jnp.dot(
            b, pick, precision=lax.Precision.HIGHEST, preferred_element_type=jnp.float32
        )[:1]

    weights = jnp.concatenate(
        [widen(lm_ref[...], spread_l), widen(rm_ref[...], spread_r)], axis=1
    )
    shift = jnp.concatenate(
        [widen_bias(lb_ref[...], spread_l), widen_bias(rb_ref[...], spread_r)], axis=1
    )
    place = iota((depth, 2 * LANES), 1) % LANES // hidden
    sends = [pltpu.make_async_copy(wf_ref, wf_hbm, sems.at[free])]
    sends[0].start()

    total = None
    for k in range(per):
        part = jnp.concatenate(
            [
                jnp.concatenate(
                    [half[pl.ds(g * per + k, seqs, stride=residues), :] for half in (lo_ref, hi_ref)],
                    axis=1,
                )
                for g in range(groups)
            ],
            axis=0,
        ).astype(jnp.bfloat16)
        placed = jnp.where(place == k, weights, 0.0).astype(jnp.bfloat16)
        term = jnp.dot(part, placed, preferred_element_type=jnp.float32)
        total = term if total is None else total + term
    total = total + shift
    left_ref[...] = total[:, :LANES].astype(left_ref.dtype)

    slot = iota((minor, LANES), 1) // seqs
    for block in range(groups // slots):
        turned_ref[...] = total[block * LANES : (block + 1) * LANES, LANES:].T
        for k in range(per):
            parts_of = [turned_ref[pl.ds(k * hidden + q * minor, minor), :] for q in range(slots)]
            for g in range(slots):
                out = None
                for q in range(slots):
                    moved = parts_of[q]
                    if q != g:
                        moved = pltpu.roll(moved, (q - g) % slots * seqs, axis=1)
                    out = moved if out is None else jnp.where(slot == q, moved, out)
                j = (block * slots + g) * per + k
                rows_ref[pl.ds(j, minor, stride=residues), :] = out
    right_ref[...] = rows_ref[...].astype(right_ref.dtype)

    mine = left_ref.shape[0] // parts
    for out, pack in zip(outs, packs):
        at = 0
        for item in pack:
            if item == RIGHT:
                rows = right_ref
            else:
                rows = left_ref.at[pl.ds(pl.multiple_of((own ^ item) * mine, 16), mine)]
            free += 1
            sends.append(
                pltpu.make_async_copy(rows, out.at[pl.ds(at, rows.shape[0])], sems.at[free])
            )
            sends[-1].start()
            at += rows.shape[0]
    for copy in sends:
        copy.wait()


def block_weights(wf_ref, wide_ref, *, parts, minor):
    cz = wf_ref.shape[1]
    hidden = parts * minor
    half = minor // 2
    rows_each = wide_ref.shape[0] // hidden // hidden
    own = lax.axis_index("narrow")
    wide_ref[...] = jnp.zeros_like(wide_ref)
    for e in range(hidden):
        rows = wf_ref[pl.ds(e ^ (own * minor), hidden, stride=hidden), :].astype(jnp.bfloat16)
        q, e2, t = e // minor, e % minor // half, e % half
        for k in range(rows_each):
            at = ((((q * half + t) * 2 + e2) * rows_each) + k) * hidden
            wide_ref[at : at + hidden, k * cz : (k + 1) * cz] = rows


def pack_kernel(*refs, count):
    out_ref, at = refs[-1], 0
    for ref in refs[:count]:
        out_ref[at : at + ref.shape[0]] = ref[...]
        at += ref.shape[0]


def spread_left(left_of, spread_ref, *, parts):
    seqs = LANES // parts
    low = iota((seqs, LANES), 1) < LANES // 2
    zero = jnp.zeros((seqs, LANES), jnp.float32)
    for m in range(parts):
        left = left_of(m)
        for g in range(left.shape[0] // seqs):
            rows = left[g * seqs : (g + 1) * seqs].astype(jnp.float32)
            turned = pltpu.roll(rows, LANES // 2, axis=1)
            for half, (first, second) in enumerate(((rows, turned), (turned, rows))):
                lanes = pl.ds((2 * g + half) * LANES, LANES)
                spread_ref[m, 0, :, lanes] = jnp.where(low, first, zero).astype(spread_ref.dtype)
                spread_ref[m, 1, :, lanes] = jnp.where(low, zero, second).astype(spread_ref.dtype)


def pair_rows(spread_ref, right_of, wide_ref, shift, outer_ref, store, *, wides, parts, minor, seqs_total):
    cz = shift.shape[1]
    half = minor // 2
    seqs = LANES // parts
    halves = spread_ref.shape[3] // LANES
    residues = right_of(0, 0).shape[0] // minor
    cols = wides * residues
    slot = iota((minor * residues, LANES), 1) // seqs
    for q in range(parts):
        left = jnp.concatenate([spread_ref[q ^ k, i] for i in range(2) for k in range(parts)], axis=0)
        rights = []
        for d in range(wides):
            right = None
            for k in range(parts):
                chunk = right_of(d, q ^ k)
                right = chunk if right is None else jnp.where(slot == k, chunk, right)
            rights.append(jnp.concatenate([right[: half * residues], right[half * residues :]], axis=1))
        right = jnp.concatenate(rights, axis=0)
        outer = jnp.dot(right, left, preferred_element_type=jnp.float32).astype(jnp.bfloat16)
        for d in range(wides):
            for t in range(half):
                at = (d * half + t) * residues
                for g in range(halves):
                    outer_ref[
                        pl.ds(g * cols + d * residues, residues),
                        (q * half + t) * LANES : (q * half + t + 1) * LANES,
                    ] = outer[at : at + residues, g * LANES : (g + 1) * LANES]

    pairs = jnp.dot(outer_ref[...], wide_ref[...], preferred_element_type=jnp.float32)
    rows_each = wide_ref.shape[1] // cz
    for g in range(halves):
        for k in range(rows_each):
            pair = pairs[g * cols : (g + 1) * cols, k * cz : (k + 1) * cz]
            store(g * rows_each + k, pair * (1.0 / seqs_total) + shift)


def pair_kernel(*refs, operands, rights, blocks, earlier, lefts=None, **sizes):
    parts, minor = sizes["parts"], sizes["minor"]
    inputs, refs = refs[:operands], refs[operands:]
    if lefts is not None:
        wf_ref, done_ref, spread_ref, wide_ref, shift_ref, outer_ref = refs
        own_rows = done_ref.shape[0]
        block_weights(wf_ref, wide_ref, parts=parts, minor=minor)
        shift_ref[...] = wf_ref[wf_ref.shape[0] - 8 :]
        count = own_rows * minor
        spread_left(lambda m: inputs[lefts[m][0]][lefts[m][1] : lefts[m][1] + count, :], spread_ref, parts=parts)
    elif not earlier:
        spread_ref, wide_ref, shift_ref, done_ref, outer_ref = refs
    else:
        spread_ref, wide_ref, shift_ref = refs[:3]
        before, (out_hbm, outer_ref, done_ref, sems) = refs[3 : 3 + len(earlier)], refs[3 + len(earlier) :]
    residues = done_ref.shape[1] // len(blocks)
    copies = []

    def write(ref, places):
        for d, block in enumerate(places):
            at = pl.multiple_of((lax.axis_index("wide") ^ block) * residues, 16)
            copies.append(
                pltpu.make_async_copy(
                    ref.at[:, pl.ds(d * residues, residues), :],
                    out_hbm.at[:, pl.ds(at, residues), :],
                    sems.at[len(copies)],
                )
            )
            copies[-1].start()

    if earlier:
        for ref, places in zip(before, earlier):
            write(ref, places)

    def right_of(d, m):
        ref, at = rights[d][m]
        return inputs[ref][at : at + minor * residues, :]

    def store(row, pair):
        done_ref[row] = pair.astype(done_ref.dtype)

    pair_rows(spread_ref, right_of, wide_ref, shift_ref[:1], outer_ref, store, wides=len(blocks), **sizes)
    if earlier:
        write(done_ref, blocks)
        for copy in copies:
            copy.wait()


def pair_blocks_kernel(*refs, wides, parts, minor, **sizes):
    left_refs, (right_ref, wf_ref, out_ref, spread_ref, wide_ref, outer_ref) = refs[:parts], refs[parts:]

    @pl.when(pl.program_id(0) == 0)
    def _():
        block_weights(wf_ref, wide_ref, parts=parts, minor=minor)
        spread_left(lambda m: left_refs[m][...], spread_ref, parts=parts)

    def store(row, pair):
        out_ref[row] = pair.astype(out_ref.dtype)

    pair_rows(
        spread_ref, lambda d, m: right_ref[d, m],
        wide_ref, wf_ref[wf_ref.shape[0] - 8 :][:1], outer_ref, store,
        wides=wides, parts=parts, minor=minor, **sizes,
    )


def on_device(wide, narrow, x, gain, bias, lm, lb, rm, rb, w, shift):
    seqs, residues, depth = x.shape
    hidden = lm.shape[1]
    cz = w.shape[1]
    per = LANES // hidden
    slots = LANES // seqs
    minor = hidden // slots
    own_rows = residues // narrow
    groups = own_rows // per
    pieces = 4
    hbm = pl.BlockSpec(memory_space=pltpu.HBM)
    vmem = pl.BlockSpec(memory_space=pltpu.VMEM)
    params = pltpu.CompilerParams(vmem_limit_bytes=VMEM_LIMIT)
    direct = wide == 4 and narrow == 4
    if direct:
        packs = ((0,), (RIGHT,), (1, RIGHT), (2, 3, RIGHT))
    else:
        packs = tuple((m,) for m in range(narrow)) + ((RIGHT,),)
    left_count, right_count = groups * seqs, minor * residues
    args = (x, gain, bias, lm.T, lb, rm.T, rb, w, shift)
    *made, w = pl.pallas_call(
        functools.partial(features_kernel, packs=packs, parts=narrow, pieces=pieces),
        out_shape=tuple(
            jax.ShapeDtypeStruct(
                (sum(right_count if i == RIGHT else left_count for i in pack), LANES), jnp.bfloat16
            )
            for pack in packs
        )
        + (jax.ShapeDtypeStruct((w.shape[0] + 8, cz), jnp.float32),),
        in_specs=[hbm] * len(args),
        out_specs=(hbm,) * (len(packs) + 1),
        scratch_shapes=[pltpu.VMEM(a.shape, a.dtype) for a in args]
        + [
            pltpu.VMEM((seqs * residues, LANES), jnp.float32),
            pltpu.VMEM((seqs * residues, LANES), jnp.float32),
            pltpu.VMEM((residues // per * seqs, LANES), jnp.bfloat16),
            pltpu.VMEM((LANES, LANES), jnp.float32),
            pltpu.VMEM((minor * residues, LANES), jnp.float32),
            pltpu.VMEM((minor * residues, LANES), jnp.bfloat16),
            pltpu.VMEM((w.shape[0] + 8, cz), jnp.float32),
            pltpu.SemaphoreType.DMA((pieces + len(args) + sum(len(pack) for pack in packs),)),
        ],
        compiler_params=pltpu.CompilerParams(vmem_limit_bytes=VMEM_ALL),
        name="features",
    )(*args)

    def across(a, m):
        return lax.ppermute(a, "narrow", [(i, i ^ m) for i in range(narrow)])

    def along(a, d):
        return lax.ppermute(a, "wide", [(i, i ^ d) for i in range(wide)])

    sizes = dict(parts=narrow, minor=minor, seqs_total=seqs * narrow)
    out_shape = jax.ShapeDtypeStruct((own_rows, wide * residues, cz), jnp.bfloat16)
    if direct:
        return pairs_by_block(made, across, along, w, out_shape, residues, sizes, params)

    lefts = [made[0]] + [across(made[m], m) for m in range(1, narrow)]
    every = lax.all_gather(made[narrow], ("wide", "narrow"), axis=0, tiled=False)
    every = every.reshape(wide, narrow, right_count, LANES)
    every = jnp.take(every, lax.axis_index("narrow") ^ jnp.arange(narrow), axis=1)
    block = wide
    while block % 2 == 0 and block * residues > 192:
        block //= 2
    cols = block * residues
    return pl.pallas_call(
        functools.partial(pair_blocks_kernel, wides=block, **sizes),
        grid=(wide // block,),
        in_specs=[pl.BlockSpec((left_count, LANES), lambda b: (0, 0))] * narrow
        + [
            pl.BlockSpec((block, narrow, right_count, LANES), lambda b: (b, 0, 0, 0)),
            pl.BlockSpec(w.shape, lambda b: (0, 0)),
        ],
        out_specs=pl.BlockSpec((own_rows, cols, cz), lambda b: (0, b, 0)),
        out_shape=out_shape,
        scratch_shapes=[
            pltpu.VMEM((narrow, 2, seqs, 2 * groups * LANES), jnp.bfloat16),
            pltpu.VMEM((hidden * LANES // 2, 2 * cz), jnp.bfloat16),
            pltpu.VMEM((2 * groups * cols, hidden * LANES // 2), jnp.bfloat16),
        ],
        compiler_params=params,
        name="pairs",
    )(*lefts, every, w)


def pairs_by_block(made, across, along, w, out_shape, residues, sizes, params):
    left_own, right, to_core, to_chip = made
    left_count, right_count = left_own.shape[0], right.shape[0]
    hbm = pl.BlockSpec(memory_space=pltpu.HBM)
    vmem = pl.BlockSpec(memory_space=pltpu.VMEM)
    own_rows, _, cz = out_shape.shape
    narrow = sizes["parts"]
    hidden = narrow * sizes["minor"]
    groups = own_rows * hidden // LANES

    def pack(*chunks, after, weight=1):
        return pl.pallas_call(
            functools.partial(pack_kernel, count=len(chunks)),
            out_shape=jax.ShapeDtypeStruct((sum(c.shape[0] for c in chunks), LANES), jnp.bfloat16),
            in_specs=[vmem] * (len(chunks) + len(after)),
            out_specs=vmem,
            compiler_params=params,
            cost_estimate=pl.CostEstimate(flops=weight, bytes_accessed=1000, transcendentals=0),
            name="pack",
        )(*chunks, *after)

    def pairs(rights, blocks, *shared, lefts=None, earlier=()):
        operands = []

        def place(chunk, at):
            operands.append(chunk)
            return len(operands) - 1, at

        rights = [[place(*chunk) for chunk in block] for block in rights]
        lefts = lefts and [place(*chunk) for chunk in lefts]
        count = len(operands)
        operands += shared
        cols = len(blocks) * residues
        done = jax.ShapeDtypeStruct((own_rows, cols, cz), jnp.bfloat16)
        shapes, outs = [done], [vmem]
        scratch = [pltpu.VMEM((2 * groups * cols, hidden * LANES // 2), jnp.bfloat16)]
        if lefts is not None:
            shapes += [
                jax.ShapeDtypeStruct((narrow, 2, LANES // narrow, 2 * groups * LANES), jnp.bfloat16),
                jax.ShapeDtypeStruct((hidden * LANES // 2, 2 * cz), jnp.bfloat16),
                jax.ShapeDtypeStruct((8, cz), jnp.float32),
            ]
            outs += [vmem] * 3
        if earlier:
            operands += [ref for ref, _ in earlier]
            shapes, outs = [out_shape], [hbm]
            scratch += [
                pltpu.VMEM(done.shape, done.dtype),
                pltpu.SemaphoreType.DMA((len(blocks) + sum(len(b) for _, b in earlier),)),
            ]
        return pl.pallas_call(
            functools.partial(
                pair_kernel, operands=count, rights=rights, blocks=blocks,
                earlier=[b for _, b in earlier], lefts=lefts, **sizes,
            ),
            out_shape=shapes,
            in_specs=[vmem] * len(operands),
            out_specs=outs,
            scratch_shapes=scratch,
            compiler_params=params,
            cost_estimate=pl.CostEstimate(flops=1000, bytes_accessed=1000, transcendentals=0),
            name=f"pairs_{blocks[0]}",
        )(*operands)

    far = along(right, 2)
    near = along(right, 1)
    last = along(far, 1)
    chip = across(to_chip, 2)
    core = across(to_core, 1)
    middle = pack(near, far, after=(), weight=4_000_000_000)
    beside = across(middle, 1)
    both = across(pack(chip, after=(last, core)), 1)
    lefts = ((left_own, 0), (core, 0), (chip, 0), (both, left_count))
    own = ((right, 0), (core, left_count), (chip, 2 * left_count), (both, 2 * left_count))
    first, *shared = pairs((own,), (0,), w, lefts=lefts)

    other = across(middle, 2)
    onward = across(pack(other, after=(shared[1],)), 1)
    onward = ((onward, 0), (onward, right_count))
    blocks = [
        ((middle, at), (beside, at), (other, at), onward[i]) for i, at in enumerate((0, right_count))
    ]
    (second,) = pairs(blocks, (1, 2), *shared)

    other = across(last, 2)
    both = across(pack(last, other, after=()), 1)
    (out,) = pairs(
        (((last, 0), (both, 0), (other, 0), (both, right_count)),), (3,), *shared,
        earlier=((first, (0,)), (second, (1, 2))),
    )
    return out


def solution(mesh):
    in_specs = (P(("groups", "narrow"), "wide", None), P(), P(), P(), P(), P(), P(), P(), P())
    out_specs = P(("groups", "wide", "narrow"), None, None)
    return jax.shard_map(
        functools.partial(on_device, mesh.shape["wide"], mesh.shape["narrow"]),
        mesh=mesh,
        in_specs=in_specs,
        out_specs=out_specs,
        check_vma=False,
    )
```

```python
import functools

import jax
import jax.numpy as jnp
from jax import lax
from jax.experimental import pallas as pl
from jax.experimental.pallas import tpu as pltpu
from jax.sharding import PartitionSpec as P

LANES = 128
RIGHT = -1
VMEM_LIMIT = 40 * 1024 * 1024
VMEM_ALL = 62 * 1024 * 1024


def iota(shape, dim):
    return lax.broadcasted_iota(jnp.int32, shape, dim)


def features_kernel(*refs, packs, parts, pieces):
    args, refs = refs[:9], refs[9:]
    outs, wf_hbm, refs = refs[: len(packs)], refs[len(packs)], refs[len(packs) + 1 :]
    held, (lo_ref, hi_ref, left_ref, turned_ref, rows_ref, right_ref, wf_ref, sems) = refs[:9], refs[9:]
    x_ref, gain_ref, bias_ref, lm_ref, lb_ref, rm_ref, rb_ref, w_ref, shift_ref = held
    seqs, residues, depth = x_ref.shape
    hidden = lm_ref.shape[0]
    per = LANES // hidden
    slots = LANES // seqs
    minor = hidden // slots
    groups = residues // per
    own = lax.axis_index("narrow")

    piece = seqs // pieces
    copies = [
        pltpu.make_async_copy(
            args[0].at[pl.ds(p * piece, piece)], x_ref.at[pl.ds(p * piece, piece)], sems.at[p]
        )
        for p in range(pieces)
    ]
    rest = [
        pltpu.make_async_copy(a, b, sems.at[pieces + i]) for i, (a, b) in enumerate(zip(args[1:], held[1:]))
    ]
    for copy in copies[:1] + rest[:2] + copies[1:] + rest[2:]:
        copy.start()
    free = pieces + len(rest)

    def norm(p):
        gain = gain_ref[...].reshape(1, depth)
        bias = bias_ref[...].reshape(1, depth)
        step = min(4, piece)
        for s in range(p * piece, (p + 1) * piece, step):
            x = x_ref[s : s + step].reshape(step * residues, depth).astype(jnp.float32)
            x = x - jnp.mean(x, axis=-1, keepdims=True)
            spread = jnp.mean(x * x, axis=-1, keepdims=True)
            x = x * lax.rsqrt(spread + 1e-05) * gain + bias
            rows = pl.ds(s * residues, step * residues)
            lo_ref[rows, :] = x[:, :LANES]
            hi_ref[rows, :] = x[:, LANES:]

    for copy in rest[:2]:
        copy.wait()
    for p in range(pieces - 1):
        copies[p].wait()
        norm(p)
    for copy in copies[-1:] + rest[2:]:
        copy.wait()
    count = w_ref.shape[0]
    wf_ref[:count] = w_ref[...].astype(jnp.float32)
    wf_ref[count:] = jnp.broadcast_to(shift_ref[...].reshape(1, -1), (8, shift_ref.shape[0]))
    norm(pieces - 1)

    column, row = iota((hidden, LANES), 1) % hidden, iota((hidden, LANES), 0)
    spread_l = (column == row).astype(jnp.float32)
    spread_r = (column == (row ^ (own * minor))).astype(jnp.float32)

    def widen(m, pick):
        return lax.dot_general(
            m, pick.astype(jnp.bfloat16), (((0,), (0,)), ((), ())),
            preferred_element_type=jnp.float32,
        )

    lane = iota((8, LANES), 1)

    def widen_bias(b):
        b = jnp.concatenate([b.reshape(1, hidden)] * per, axis=1)
        return jnp.broadcast_to(b, (8, LANES))

    def swapped(b):
        bit = 1
        while bit < slots:
            step = bit * minor
            up, down = pltpu.roll(b, step, axis=1), pltpu.roll(b, LANES - step, axis=1)
            other = jnp.where(lane & step != 0, up, down)
            b = jnp.where(own & bit != 0, other, b)
            bit *= 2
        return b

    weights = jnp.concatenate(
        [widen(lm_ref[...], spread_l), widen(rm_ref[...], spread_r)], axis=1
    )
    shift = jnp.concatenate(
        [widen_bias(lb_ref[...]), swapped(widen_bias(rb_ref[...]))], axis=1
    )[:1]
    place = iota((depth, 2 * LANES), 1) % LANES // hidden
    sends = [pltpu.make_async_copy(wf_ref, wf_hbm, sems.at[free])]
    sends[0].start()

    total = None
    for k in range(per):
        part = jnp.concatenate(
            [
                jnp.concatenate(
                    [half[pl.ds(g * per + k, seqs, stride=residues), :] for half in (lo_ref, hi_ref)],
                    axis=1,
                )
                for g in range(groups)
            ],
            axis=0,
        ).astype(jnp.bfloat16)
        placed = jnp.where(place == k, weights, 0.0).astype(jnp.bfloat16)
        term = jnp.dot(part, placed, preferred_element_type=jnp.float32)
        total = term if total is None else total + term
    total = total + shift
    left_ref[...] = total[:, :LANES].astype(left_ref.dtype)

    slot = iota((minor, LANES), 1) // seqs
    for block in range(groups // slots):
        turned_ref[...] = total[block * LANES : (block + 1) * LANES, LANES:].T
        for k in range(per):
            parts_of = [turned_ref[pl.ds(k * hidden + q * minor, minor), :] for q in range(slots)]
            for g in range(slots):
                out = None
                for q in range(slots):
                    moved = parts_of[q]
                    if q != g:
                        moved = pltpu.roll(moved, (q - g) % slots * seqs, axis=1)
                    out = moved if out is None else jnp.where(slot == q, moved, out)
                j = (block * slots + g) * per + k
                rows_ref[pl.ds(j, minor, stride=residues), :] = out
    right_ref[...] = rows_ref[...].astype(right_ref.dtype)

    mine = left_ref.shape[0] // parts
    for out, pack in zip(outs, packs):
        at = 0
        for item in pack:
            if item == RIGHT:
                rows = right_ref
            else:
                rows = left_ref.at[pl.ds(pl.multiple_of((own ^ item) * mine, 16), mine)]
            free += 1
            sends.append(
                pltpu.make_async_copy(rows, out.at[pl.ds(at, rows.shape[0])], sems.at[free])
            )
            sends[-1].start()
            at += rows.shape[0]
    for copy in sends:
        copy.wait()


def block_weights(wf_ref, wide_ref, *, parts, minor):
    cz = wf_ref.shape[1]
    hidden = parts * minor
    half = minor // 2
    rows_each = wide_ref.shape[0] // hidden // hidden
    own = lax.axis_index("narrow")
    wide_ref[...] = jnp.zeros_like(wide_ref)
    for e in range(hidden):
        rows = wf_ref[pl.ds(e ^ (own * minor), hidden, stride=hidden), :].astype(jnp.bfloat16)
        q, e2, t = e // minor, e % minor // half, e % half
        for k in range(rows_each):
            at = ((((q * half + t) * 2 + e2) * rows_each) + k) * hidden
            wide_ref[at : at + hidden, k * cz : (k + 1) * cz] = rows


def pack_kernel(*refs, count):
    out_ref, at = refs[-1], 0
    for ref in refs[:count]:
        out_ref[at : at + ref.shape[0]] = ref[...]
        at += ref.shape[0]


def spread_left(left_of, spread_ref, *, parts):
    seqs = LANES // parts
    low = iota((seqs, LANES), 1) < LANES // 2
    zero = jnp.zeros((seqs, LANES), jnp.float32)
    for m in range(parts):
        left = left_of(m)
        for g in range(left.shape[0] // seqs):
            rows = left[g * seqs : (g + 1) * seqs].astype(jnp.float32)
            turned = pltpu.roll(rows, LANES // 2, axis=1)
            for half, (first, second) in enumerate(((rows, turned), (turned, rows))):
                lanes = pl.ds((2 * g + half) * LANES, LANES)
                spread_ref[m, 0, :, lanes] = jnp.where(low, first, zero).astype(spread_ref.dtype)
                spread_ref[m, 1, :, lanes] = jnp.where(low, zero, second).astype(spread_ref.dtype)


def pair_rows(spread_ref, right_of, wide_ref, shift, outer_ref, store, *, wides, parts, minor, seqs_total):
    cz = shift.shape[1]
    half = minor // 2
    seqs = LANES // parts
    halves = spread_ref.shape[3] // LANES
    residues = right_of(0, 0).shape[0] // minor
    cols = wides * residues
    slot = iota((minor * residues, LANES), 1) // seqs
    for q in range(parts):
        left = jnp.concatenate([spread_ref[q ^ k, i] for i in range(2) for k in range(parts)], axis=0)
        rights = []
        for d in range(wides):
            right = None
            for k in range(parts):
                chunk = right_of(d, q ^ k)
                right = chunk if right is None else jnp.where(slot == k, chunk, right)
            rights.append(jnp.concatenate([right[: half * residues], right[half * residues :]], axis=1))
        right = jnp.concatenate(rights, axis=0)
        outer = jnp.dot(right, left, preferred_element_type=jnp.float32).astype(jnp.bfloat16)
        for d in range(wides):
            for t in range(half):
                at = (d * half + t) * residues
                for g in range(halves):
                    outer_ref[
                        pl.ds(g * cols + d * residues, residues),
                        (q * half + t) * LANES : (q * half + t + 1) * LANES,
                    ] = outer[at : at + residues, g * LANES : (g + 1) * LANES]

    pairs = jnp.dot(outer_ref[...], wide_ref[...], preferred_element_type=jnp.float32)
    rows_each = wide_ref.shape[1] // cz
    for g in range(halves):
        for k in range(rows_each):
            pair = pairs[g * cols : (g + 1) * cols, k * cz : (k + 1) * cz]
            store(g * rows_each + k, pair * (1.0 / seqs_total) + shift)


def pair_kernel(*refs, operands, rights, blocks, earlier, lefts=None, **sizes):
    parts, minor = sizes["parts"], sizes["minor"]
    inputs, refs = refs[:operands], refs[operands:]
    if lefts is not None:
        wf_ref, done_ref, spread_ref, wide_ref, shift_ref, outer_ref = refs
        own_rows = done_ref.shape[0]
        block_weights(wf_ref, wide_ref, parts=parts, minor=minor)
        shift_ref[...] = wf_ref[wf_ref.shape[0] - 8 :]
        count = own_rows * minor
        spread_left(lambda m: inputs[lefts[m][0]][lefts[m][1] : lefts[m][1] + count, :], spread_ref, parts=parts)
    elif not earlier:
        spread_ref, wide_ref, shift_ref, done_ref, outer_ref = refs
    else:
        spread_ref, wide_ref, shift_ref = refs[:3]
        before, (out_hbm, outer_ref, done_ref, sems) = refs[3 : 3 + len(earlier)], refs[3 + len(earlier) :]
    residues = done_ref.shape[1] // len(blocks)
    copies = []

    def write(ref, places):
        for d, block in enumerate(places):
            at = pl.multiple_of((lax.axis_index("wide") ^ block) * residues, 16)
            copies.append(
                pltpu.make_async_copy(
                    ref.at[:, pl.ds(d * residues, residues), :],
                    out_hbm.at[:, pl.ds(at, residues), :],
                    sems.at[len(copies)],
                )
            )
            copies[-1].start()

    if earlier:
        for ref, places in zip(before, earlier):
            write(ref, places)

    def right_of(d, m):
        ref, at = rights[d][m]
        return inputs[ref][at : at + minor * residues, :]

    def store(row, pair):
        done_ref[row] = pair.astype(done_ref.dtype)

    pair_rows(spread_ref, right_of, wide_ref, shift_ref[:1], outer_ref, store, wides=len(blocks), **sizes)
    if earlier:
        write(done_ref, blocks)
        for copy in copies:
            copy.wait()


def pair_blocks_kernel(*refs, wides, parts, minor, **sizes):
    left_refs, (right_ref, wf_ref, out_ref, spread_ref, wide_ref, outer_ref) = refs[:parts], refs[parts:]

    @pl.when(pl.program_id(0) == 0)
    def _():
        block_weights(wf_ref, wide_ref, parts=parts, minor=minor)
        spread_left(lambda m: left_refs[m][...], spread_ref, parts=parts)

    def store(row, pair):
        out_ref[row] = pair.astype(out_ref.dtype)

    pair_rows(
        spread_ref, lambda d, m: right_ref[d, m],
        wide_ref, wf_ref[wf_ref.shape[0] - 8 :][:1], outer_ref, store,
        wides=wides, parts=parts, minor=minor, **sizes,
    )


def on_device(wide, narrow, x, gain, bias, lm, lb, rm, rb, w, shift):
    seqs, residues, depth = x.shape
    hidden = lm.shape[1]
    cz = w.shape[1]
    per = LANES // hidden
    slots = LANES // seqs
    minor = hidden // slots
    own_rows = residues // narrow
    groups = own_rows // per
    pieces = 4
    hbm = pl.BlockSpec(memory_space=pltpu.HBM)
    vmem = pl.BlockSpec(memory_space=pltpu.VMEM)
    params = pltpu.CompilerParams(vmem_limit_bytes=VMEM_LIMIT)
    direct = wide == 4 and narrow == 4
    if direct:
        packs = ((0,), (RIGHT,), (1, RIGHT), (2, 3, RIGHT))
    else:
        packs = tuple((m,) for m in range(narrow)) + ((RIGHT,),)
    left_count, right_count = groups * seqs, minor * residues
    args = (x, gain, bias, lm.T, lb, rm.T, rb, w, shift)
    *made, w = pl.pallas_call(
        functools.partial(features_kernel, packs=packs, parts=narrow, pieces=pieces),
        out_shape=tuple(
            jax.ShapeDtypeStruct(
                (sum(right_count if i == RIGHT else left_count for i in pack), LANES), jnp.bfloat16
            )
            for pack in packs
        )
        + (jax.ShapeDtypeStruct((w.shape[0] + 8, cz), jnp.float32),),
        in_specs=[hbm] * len(args),
        out_specs=(hbm,) * (len(packs) + 1),
        scratch_shapes=[pltpu.VMEM(a.shape, a.dtype) for a in args]
        + [
            pltpu.VMEM((seqs * residues, LANES), jnp.float32),
            pltpu.VMEM((seqs * residues, LANES), jnp.float32),
            pltpu.VMEM((residues // per * seqs, LANES), jnp.bfloat16),
            pltpu.VMEM((LANES, LANES), jnp.float32),
            pltpu.VMEM((minor * residues, LANES), jnp.float32),
            pltpu.VMEM((minor * residues, LANES), jnp.bfloat16),
            pltpu.VMEM((w.shape[0] + 8, cz), jnp.float32),
            pltpu.SemaphoreType.DMA((pieces + len(args) + sum(len(pack) for pack in packs),)),
        ],
        compiler_params=pltpu.CompilerParams(vmem_limit_bytes=VMEM_ALL),
        name="features",
    )(*args)

    def across(a, m):
        return lax.ppermute(a, "narrow", [(i, i ^ m) for i in range(narrow)])

    def along(a, d):
        return lax.ppermute(a, "wide", [(i, i ^ d) for i in range(wide)])

    sizes = dict(parts=narrow, minor=minor, seqs_total=seqs * narrow)
    out_shape = jax.ShapeDtypeStruct((own_rows, wide * residues, cz), jnp.bfloat16)
    if direct:
        return pairs_by_block(made, across, along, w, out_shape, residues, sizes, params)

    lefts = [made[0]] + [across(made[m], m) for m in range(1, narrow)]
    every = lax.all_gather(made[narrow], ("wide", "narrow"), axis=0, tiled=False)
    every = every.reshape(wide, narrow, right_count, LANES)
    every = jnp.take(every, lax.axis_index("narrow") ^ jnp.arange(narrow), axis=1)
    block = wide
    while block % 2 == 0 and block * residues > 192:
        block //= 2
    cols = block * residues
    return pl.pallas_call(
        functools.partial(pair_blocks_kernel, wides=block, **sizes),
        grid=(wide // block,),
        in_specs=[pl.BlockSpec((left_count, LANES), lambda b: (0, 0))] * narrow
        + [
            pl.BlockSpec((block, narrow, right_count, LANES), lambda b: (b, 0, 0, 0)),
            pl.BlockSpec(w.shape, lambda b: (0, 0)),
        ],
        out_specs=pl.BlockSpec((own_rows, cols, cz), lambda b: (0, b, 0)),
        out_shape=out_shape,
        scratch_shapes=[
            pltpu.VMEM((narrow, 2, seqs, 2 * groups * LANES), jnp.bfloat16),
            pltpu.VMEM((hidden * LANES // 2, 2 * cz), jnp.bfloat16),
            pltpu.VMEM((2 * groups * cols, hidden * LANES // 2), jnp.bfloat16),
        ],
        compiler_params=params,
        name="pairs",
    )(*lefts, every, w)


def pairs_by_block(made, across, along, w, out_shape, residues, sizes, params):
    left_own, right, to_core, to_chip = made
    left_count, right_count = left_own.shape[0], right.shape[0]
    hbm = pl.BlockSpec(memory_space=pltpu.HBM)
    vmem = pl.BlockSpec(memory_space=pltpu.VMEM)
    own_rows, _, cz = out_shape.shape
    narrow = sizes["parts"]
    hidden = narrow * sizes["minor"]
    groups = own_rows * hidden // LANES

    def pack(*chunks, after, weight=1):
        return pl.pallas_call(
            functools.partial(pack_kernel, count=len(chunks)),
            out_shape=jax.ShapeDtypeStruct((sum(c.shape[0] for c in chunks), LANES), jnp.bfloat16),
            in_specs=[vmem] * (len(chunks) + len(after)),
            out_specs=vmem,
            compiler_params=params,
            cost_estimate=pl.CostEstimate(flops=weight, bytes_accessed=1000, transcendentals=0),
            name="pack",
        )(*chunks, *after)

    def pairs(rights, blocks, *shared, lefts=None, earlier=()):
        operands = []

        def place(chunk, at):
            operands.append(chunk)
            return len(operands) - 1, at

        rights = [[place(*chunk) for chunk in block] for block in rights]
        lefts = lefts and [place(*chunk) for chunk in lefts]
        count = len(operands)
        operands += shared
        cols = len(blocks) * residues
        done = jax.ShapeDtypeStruct((own_rows, cols, cz), jnp.bfloat16)
        shapes, outs = [done], [vmem]
        scratch = [pltpu.VMEM((2 * groups * cols, hidden * LANES // 2), jnp.bfloat16)]
        if lefts is not None:
            shapes += [
                jax.ShapeDtypeStruct((narrow, 2, LANES // narrow, 2 * groups * LANES), jnp.bfloat16),
                jax.ShapeDtypeStruct((hidden * LANES // 2, 2 * cz), jnp.bfloat16),
                jax.ShapeDtypeStruct((8, cz), jnp.float32),
            ]
            outs += [vmem] * 3
        if earlier:
            operands += [ref for ref, _ in earlier]
            shapes, outs = [out_shape], [hbm]
            scratch += [
                pltpu.VMEM(done.shape, done.dtype),
                pltpu.SemaphoreType.DMA((len(blocks) + sum(len(b) for _, b in earlier),)),
            ]
        return pl.pallas_call(
            functools.partial(
                pair_kernel, operands=count, rights=rights, blocks=blocks,
                earlier=[b for _, b in earlier], lefts=lefts, **sizes,
            ),
            out_shape=shapes,
            in_specs=[vmem] * len(operands),
            out_specs=outs,
            scratch_shapes=scratch,
            compiler_params=params,
            cost_estimate=pl.CostEstimate(flops=1000, bytes_accessed=1000, transcendentals=0),
            name=f"pairs_{blocks[0]}",
        )(*operands)

    far = along(right, 2)
    near = along(right, 1)
    last = along(far, 1)
    chip = across(to_chip, 2)
    core = across(to_core, 1)
    middle = pack(near, far, after=(), weight=4_000_000_000)
    beside = across(middle, 1)
    both = across(pack(chip, after=(last, core)), 1)
    lefts = ((left_own, 0), (core, 0), (chip, 0), (both, left_count))
    own = ((right, 0), (core, left_count), (chip, 2 * left_count), (both, 2 * left_count))
    first, *shared = pairs((own,), (0,), w, lefts=lefts)

    other = across(middle, 2)
    onward = across(pack(other, after=(shared[1],)), 1)
    onward = ((onward, 0), (onward, right_count))
    blocks = [
        ((middle, at), (beside, at), (other, at), onward[i]) for i, at in enumerate((0, right_count))
    ]
    (second,) = pairs(blocks, (1, 2), *shared)

    other = across(last, 2)
    both = across(pack(last, other, after=()), 1)
    (out,) = pairs(
        (((last, 0), (both, 0), (other, 0), (both, right_count)),), (3,), *shared,
        earlier=((first, (0,)), (second, (1, 2))),
    )
    return out


def solution(mesh):
    in_specs = (P(("groups", "narrow"), "wide", None), P(), P(), P(), P(), P(), P(), P(), P())
    out_specs = P(("groups", "wide", "narrow"), None, None)
    return jax.shard_map(
        functools.partial(on_device, mesh.shape["wide"], mesh.shape["narrow"]),
        mesh=mesh,
        in_specs=in_specs,
        out_specs=out_specs,
        check_vma=False,
    )
```

```python
import functools

import jax
import jax.numpy as jnp
from jax import lax
from jax.experimental import pallas as pl
from jax.experimental.pallas import tpu as pltpu
from jax.sharding import PartitionSpec as P

LANES = 128
RIGHT = -1
VMEM_LIMIT = 40 * 1024 * 1024
VMEM_ALL = 62 * 1024 * 1024


def iota(shape, dim):
    return lax.broadcasted_iota(jnp.int32, shape, dim)


def features_kernel(*refs, packs, parts, pieces):
    args, refs = refs[:9], refs[9:]
    outs, wf_hbm, refs = refs[: len(packs)], refs[len(packs)], refs[len(packs) + 1 :]
    held, (lo_ref, hi_ref, left_ref, turned_ref, rows_ref, right_ref, wf_ref, sems) = refs[:9], refs[9:]
    x_ref, gain_ref, bias_ref, lm_ref, lb_ref, rm_ref, rb_ref, w_ref, shift_ref = held
    seqs, residues, depth = x_ref.shape
    hidden = lm_ref.shape[0]
    per = LANES // hidden
    slots = LANES // seqs
    minor = hidden // slots
    groups = residues // per
    own = lax.axis_index("narrow")

    piece = seqs // pieces
    copies = [
        pltpu.make_async_copy(
            args[0].at[pl.ds(p * piece, piece)], x_ref.at[pl.ds(p * piece, piece)], sems.at[p]
        )
        for p in range(pieces)
    ]
    rest = [
        pltpu.make_async_copy(a, b, sems.at[pieces + i]) for i, (a, b) in enumerate(zip(args[1:], held[1:]))
    ]
    for copy in copies[:1] + rest[:2] + copies[1:] + rest[2:]:
        copy.start()
    free = pieces + len(rest)

    def norm(p):
        gain = gain_ref[...].reshape(1, depth)
        bias = bias_ref[...].reshape(1, depth)
        step = min(4, piece)
        for s in range(p * piece, (p + 1) * piece, step):
            x = x_ref[s : s + step].reshape(step * residues, depth).astype(jnp.float32)
            x = x - jnp.mean(x, axis=-1, keepdims=True)
            spread = jnp.mean(x * x, axis=-1, keepdims=True)
            x = x * lax.rsqrt(spread + 1e-05) * gain + bias
            rows = pl.ds(s * residues, step * residues)
            lo_ref[rows, :] = x[:, :LANES]
            hi_ref[rows, :] = x[:, LANES:]

    for copy in rest[:2]:
        copy.wait()
    for p in range(pieces - 1):
        copies[p].wait()
        norm(p)
    for copy in copies[-1:] + rest[2:]:
        copy.wait()
    count = w_ref.shape[0]
    wf_ref[:count] = w_ref[...].astype(jnp.float32)
    wf_ref[count:] = jnp.broadcast_to(shift_ref[...].reshape(1, -1), (8, shift_ref.shape[0]))
    norm(pieces - 1)

    column, row = iota((hidden, LANES), 1) % hidden, iota((hidden, LANES), 0)
    spread_l = (column == row).astype(jnp.float32)
    spread_r = (column == (row ^ (own * minor))).astype(jnp.float32)

    def widen(m, pick):
        return lax.dot_general(
            m, pick.astype(jnp.bfloat16), (((0,), (0,)), ((), ())),
            preferred_element_type=jnp.float32,
        )

    lane = iota((8, LANES), 1)

    def widen_bias(b):
        b = jnp.concatenate([b.reshape(1, hidden)] * per, axis=1)
        return jnp.broadcast_to(b, (8, LANES))

    def swapped(b):
        bit = 1
        while bit < slots:
            step = bit * minor
            up, down = pltpu.roll(b, step, axis=1), pltpu.roll(b, LANES - step, axis=1)
            other = jnp.where(lane & step != 0, up, down)
            b = jnp.where(own & bit != 0, other, b)
            bit *= 2
        return b

    weights = jnp.concatenate(
        [widen(lm_ref[...], spread_l), widen(rm_ref[...], spread_r)], axis=1
    )
    shift = jnp.concatenate(
        [widen_bias(lb_ref[...]), swapped(widen_bias(rb_ref[...]))], axis=1
    )[:1]
    place = iota((depth, 2 * LANES), 1) % LANES // hidden
    sends = [pltpu.make_async_copy(wf_ref, wf_hbm, sems.at[free])]
    sends[0].start()

    total = None
    for k in range(per):
        part = jnp.concatenate(
            [
                jnp.concatenate(
                    [half[pl.ds(g * per + k, seqs, stride=residues), :] for half in (lo_ref, hi_ref)],
                    axis=1,
                )
                for g in range(groups)
            ],
            axis=0,
        ).astype(jnp.bfloat16)
        placed = jnp.where(place == k, weights, 0.0).astype(jnp.bfloat16)
        term = jnp.dot(part, placed, preferred_element_type=jnp.float32)
        total = term if total is None else total + term
    total = total + shift
    left_ref[...] = total[:, :LANES].astype(left_ref.dtype)

    mine = left_ref.shape[0] // parts

    def send(is_right):
        number = free
        for out, pack in zip(outs, packs):
            at = 0
            for item in pack:
                if item == RIGHT:
                    rows = right_ref
                else:
                    rows = left_ref.at[pl.ds(pl.multiple_of((own ^ item) * mine, 16), mine)]
                number += 1
                if (item == RIGHT) == is_right:
                    sends.append(
                        pltpu.make_async_copy(rows, out.at[pl.ds(at, rows.shape[0])], sems.at[number])
                    )
                    sends[-1].start()
                at += rows.shape[0]

    send(False)

    slot = iota((minor, LANES), 1) // seqs
    for block in range(groups // slots):
        turned_ref[...] = total[block * LANES : (block + 1) * LANES, LANES:].T
        for k in range(per):
            parts_of = [turned_ref[pl.ds(k * hidden + q * minor, minor), :] for q in range(slots)]
            for g in range(slots):
                out = None
                for q in range(slots):
                    moved = parts_of[q]
                    if q != g:
                        moved = pltpu.roll(moved, (q - g) % slots * seqs, axis=1)
                    out = moved if out is None else jnp.where(slot == q, moved, out)
                j = (block * slots + g) * per + k
                rows_ref[pl.ds(j, minor, stride=residues), :] = out
    right_ref[...] = rows_ref[...].astype(right_ref.dtype)

    send(True)
    for copy in sends:
        copy.wait()


def block_weights(wf_ref, wide_ref, *, parts, minor):
    cz = wf_ref.shape[1]
    hidden = parts * minor
    half = minor // 2
    rows_each = wide_ref.shape[0] // hidden // hidden
    own = lax.axis_index("narrow")
    wide_ref[...] = jnp.zeros_like(wide_ref)
    for e in range(hidden):
        rows = wf_ref[pl.ds(e ^ (own * minor), hidden, stride=hidden), :].astype(jnp.bfloat16)
        q, e2, t = e // minor, e % minor // half, e % half
        for k in range(rows_each):
            at = ((((q * half + t) * 2 + e2) * rows_each) + k) * hidden
            wide_ref[at : at + hidden, k * cz : (k + 1) * cz] = rows


def pack_kernel(*refs, count):
    out_ref, at = refs[-1], 0
    for ref in refs[:count]:
        out_ref[at : at + ref.shape[0]] = ref[...]
        at += ref.shape[0]


def spread_left(left_of, spread_ref, *, parts):
    seqs = LANES // parts
    low = iota((seqs, LANES), 1) < LANES // 2
    zero = jnp.zeros((seqs, LANES), jnp.float32)
    for m in range(parts):
        left = left_of(m)
        for g in range(left.shape[0] // seqs):
            rows = left[g * seqs : (g + 1) * seqs].astype(jnp.float32)
            turned = pltpu.roll(rows, LANES // 2, axis=1)
            for half, (first, second) in enumerate(((rows, turned), (turned, rows))):
                lanes = pl.ds((2 * g + half) * LANES, LANES)
                spread_ref[m, 0, :, lanes] = jnp.where(low, first, zero).astype(spread_ref.dtype)
                spread_ref[m, 1, :, lanes] = jnp.where(low, zero, second).astype(spread_ref.dtype)


def pair_rows(spread_ref, right_of, wide_ref, shift, outer_ref, store, *, wides, parts, minor, seqs_total):
    cz = shift.shape[1]
    half = minor // 2
    seqs = LANES // parts
    halves = spread_ref.shape[3] // LANES
    residues = right_of(0, 0).shape[0] // minor
    cols = wides * residues
    slot = iota((minor * residues, LANES), 1) // seqs
    for q in range(parts):
        left = jnp.concatenate([spread_ref[q ^ k, i] for i in range(2) for k in range(parts)], axis=0)
        rights = []
        for d in range(wides):
            right = None
            for k in range(parts):
                chunk = right_of(d, q ^ k)
                right = chunk if right is None else jnp.where(slot == k, chunk, right)
            rights.append(jnp.concatenate([right[: half * residues], right[half * residues :]], axis=1))
        right = jnp.concatenate(rights, axis=0)
        outer = jnp.dot(right, left, preferred_element_type=jnp.float32).astype(jnp.bfloat16)
        for d in range(wides):
            for t in range(half):
                at = (d * half + t) * residues
                for g in range(halves):
                    outer_ref[
                        pl.ds(g * cols + d * residues, residues),
                        (q * half + t) * LANES : (q * half + t + 1) * LANES,
                    ] = outer[at : at + residues, g * LANES : (g + 1) * LANES]

    pairs = jnp.dot(outer_ref[...], wide_ref[...], preferred_element_type=jnp.float32)
    rows_each = wide_ref.shape[1] // cz
    for g in range(halves):
        for k in range(rows_each):
            pair = pairs[g * cols : (g + 1) * cols, k * cz : (k + 1) * cz]
            store(g * rows_each + k, pair * (1.0 / seqs_total) + shift)


def pair_kernel(*refs, operands, rights, blocks, earlier, lefts=None, **sizes):
    parts, minor = sizes["parts"], sizes["minor"]
    inputs, refs = refs[:operands], refs[operands:]
    if lefts is not None:
        wf_ref, done_ref, spread_ref, wide_ref, shift_ref, outer_ref = refs
        own_rows = done_ref.shape[0]
        block_weights(wf_ref, wide_ref, parts=parts, minor=minor)
        shift_ref[...] = wf_ref[wf_ref.shape[0] - 8 :]
        count = own_rows * minor
        spread_left(lambda m: inputs[lefts[m][0]][lefts[m][1] : lefts[m][1] + count, :], spread_ref, parts=parts)
    elif not earlier:
        spread_ref, wide_ref, shift_ref, done_ref, outer_ref = refs
    else:
        spread_ref, wide_ref, shift_ref = refs[:3]
        before, (out_hbm, outer_ref, done_ref, sems) = refs[3 : 3 + len(earlier)], refs[3 + len(earlier) :]
    residues = done_ref.shape[1] // len(blocks)
    copies = []

    def write(ref, places):
        for d, block in enumerate(places):
            at = pl.multiple_of((lax.axis_index("wide") ^ block) * residues, 16)
            copies.append(
                pltpu.make_async_copy(
                    ref.at[:, pl.ds(d * residues, residues), :],
                    out_hbm.at[:, pl.ds(at, residues), :],
                    sems.at[len(copies)],
                )
            )
            copies[-1].start()

    if earlier:
        for ref, places in zip(before, earlier):
            write(ref, places)

    def right_of(d, m):
        ref, at = rights[d][m]
        return inputs[ref][at : at + minor * residues, :]

    def store(row, pair):
        done_ref[row] = pair.astype(done_ref.dtype)

    pair_rows(spread_ref, right_of, wide_ref, shift_ref[:1], outer_ref, store, wides=len(blocks), **sizes)
    if earlier:
        write(done_ref, blocks)
        for copy in copies:
            copy.wait()


def pair_blocks_kernel(*refs, wides, parts, minor, **sizes):
    left_refs, (right_ref, wf_ref, out_ref, spread_ref, wide_ref, outer_ref) = refs[:parts], refs[parts:]

    @pl.when(pl.program_id(0) == 0)
    def _():
        block_weights(wf_ref, wide_ref, parts=parts, minor=minor)
        spread_left(lambda m: left_refs[m][...], spread_ref, parts=parts)

    def store(row, pair):
        out_ref[row] = pair.astype(out_ref.dtype)

    pair_rows(
        spread_ref, lambda d, m: right_ref[d, m],
        wide_ref, wf_ref[wf_ref.shape[0] - 8 :][:1], outer_ref, store,
        wides=wides, parts=parts, minor=minor, **sizes,
    )


def on_device(wide, narrow, x, gain, bias, lm, lb, rm, rb, w, shift):
    seqs, residues, depth = x.shape
    hidden = lm.shape[1]
    cz = w.shape[1]
    per = LANES // hidden
    slots = LANES // seqs
    minor = hidden // slots
    own_rows = residues // narrow
    groups = own_rows // per
    pieces = 4
    hbm = pl.BlockSpec(memory_space=pltpu.HBM)
    vmem = pl.BlockSpec(memory_space=pltpu.VMEM)
    params = pltpu.CompilerParams(vmem_limit_bytes=VMEM_LIMIT)
    direct = wide == 4 and narrow == 4
    if direct:
        packs = ((0,), (RIGHT,), (1, RIGHT), (2, 3, RIGHT))
    else:
        packs = tuple((m,) for m in range(narrow)) + ((RIGHT,),)
    left_count, right_count = groups * seqs, minor * residues
    args = (x, gain, bias, lm.T, lb, rm.T, rb, w, shift)
    *made, w = pl.pallas_call(
        functools.partial(features_kernel, packs=packs, parts=narrow, pieces=pieces),
        out_shape=tuple(
            jax.ShapeDtypeStruct(
                (sum(right_count if i == RIGHT else left_count for i in pack), LANES), jnp.bfloat16
            )
            for pack in packs
        )
        + (jax.ShapeDtypeStruct((w.shape[0] + 8, cz), jnp.float32),),
        in_specs=[hbm] * len(args),
        out_specs=(hbm,) * (len(packs) + 1),
        scratch_shapes=[pltpu.VMEM(a.shape, a.dtype) for a in args]
        + [
            pltpu.VMEM((seqs * residues, LANES), jnp.float32),
            pltpu.VMEM((seqs * residues, LANES), jnp.float32),
            pltpu.VMEM((residues // per * seqs, LANES), jnp.bfloat16),
            pltpu.VMEM((LANES, LANES), jnp.float32),
            pltpu.VMEM((minor * residues, LANES), jnp.float32),
            pltpu.VMEM((minor * residues, LANES), jnp.bfloat16),
            pltpu.VMEM((w.shape[0] + 8, cz), jnp.float32),
            pltpu.SemaphoreType.DMA((pieces + len(args) + sum(len(pack) for pack in packs),)),
        ],
        compiler_params=pltpu.CompilerParams(vmem_limit_bytes=VMEM_ALL),
        name="features",
    )(*args)

    def across(a, m):
        return lax.ppermute(a, "narrow", [(i, i ^ m) for i in range(narrow)])

    def along(a, d):
        return lax.ppermute(a, "wide", [(i, i ^ d) for i in range(wide)])

    sizes = dict(parts=narrow, minor=minor, seqs_total=seqs * narrow)
    out_shape = jax.ShapeDtypeStruct((own_rows, wide * residues, cz), jnp.bfloat16)
    if direct:
        return pairs_by_block(made, across, along, w, out_shape, residues, sizes, params)

    lefts = [made[0]] + [across(made[m], m) for m in range(1, narrow)]
    every = lax.all_gather(made[narrow], ("wide", "narrow"), axis=0, tiled=False)
    every = every.reshape(wide, narrow, right_count, LANES)
    every = jnp.take(every, lax.axis_index("narrow") ^ jnp.arange(narrow), axis=1)
    block = wide
    while block % 2 == 0 and block * residues > 192:
        block //= 2
    cols = block * residues
    return pl.pallas_call(
        functools.partial(pair_blocks_kernel, wides=block, **sizes),
        grid=(wide // block,),
        in_specs=[pl.BlockSpec((left_count, LANES), lambda b: (0, 0))] * narrow
        + [
            pl.BlockSpec((block, narrow, right_count, LANES), lambda b: (b, 0, 0, 0)),
            pl.BlockSpec(w.shape, lambda b: (0, 0)),
        ],
        out_specs=pl.BlockSpec((own_rows, cols, cz), lambda b: (0, b, 0)),
        out_shape=out_shape,
        scratch_shapes=[
            pltpu.VMEM((narrow, 2, seqs, 2 * groups * LANES), jnp.bfloat16),
            pltpu.VMEM((hidden * LANES // 2, 2 * cz), jnp.bfloat16),
            pltpu.VMEM((2 * groups * cols, hidden * LANES // 2), jnp.bfloat16),
        ],
        compiler_params=params,
        name="pairs",
    )(*lefts, every, w)


def pairs_by_block(made, across, along, w, out_shape, residues, sizes, params):
    left_own, right, to_core, to_chip = made
    left_count, right_count = left_own.shape[0], right.shape[0]
    hbm = pl.BlockSpec(memory_space=pltpu.HBM)
    vmem = pl.BlockSpec(memory_space=pltpu.VMEM)
    own_rows, _, cz = out_shape.shape
    narrow = sizes["parts"]
    hidden = narrow * sizes["minor"]
    groups = own_rows * hidden // LANES

    def pack(*chunks, after, weight=1):
        return pl.pallas_call(
            functools.partial(pack_kernel, count=len(chunks)),
            out_shape=jax.ShapeDtypeStruct((sum(c.shape[0] for c in chunks), LANES), jnp.bfloat16),
            in_specs=[vmem] * (len(chunks) + len(after)),
            out_specs=vmem,
            compiler_params=params,
            cost_estimate=pl.CostEstimate(flops=weight, bytes_accessed=1000, transcendentals=0),
            name="pack",
        )(*chunks, *after)

    def pairs(rights, blocks, *shared, lefts=None, earlier=()):
        operands = []

        def place(chunk, at):
            operands.append(chunk)
            return len(operands) - 1, at

        rights = [[place(*chunk) for chunk in block] for block in rights]
        lefts = lefts and [place(*chunk) for chunk in lefts]
        count = len(operands)
        operands += shared
        cols = len(blocks) * residues
        done = jax.ShapeDtypeStruct((own_rows, cols, cz), jnp.bfloat16)
        shapes, outs = [done], [vmem]
        scratch = [pltpu.VMEM((2 * groups * cols, hidden * LANES // 2), jnp.bfloat16)]
        if lefts is not None:
            shapes += [
                jax.ShapeDtypeStruct((narrow, 2, LANES // narrow, 2 * groups * LANES), jnp.bfloat16),
                jax.ShapeDtypeStruct((hidden * LANES // 2, 2 * cz), jnp.bfloat16),
                jax.ShapeDtypeStruct((8, cz), jnp.float32),
            ]
            outs += [vmem] * 3
        if earlier:
            operands += [ref for ref, _ in earlier]
            shapes, outs = [out_shape], [hbm]
            scratch += [
                pltpu.VMEM(done.shape, done.dtype),
                pltpu.SemaphoreType.DMA((len(blocks) + sum(len(b) for _, b in earlier),)),
            ]
        return pl.pallas_call(
            functools.partial(
                pair_kernel, operands=count, rights=rights, blocks=blocks,
                earlier=[b for _, b in earlier], lefts=lefts, **sizes,
            ),
            out_shape=shapes,
            in_specs=[vmem] * len(operands),
            out_specs=outs,
            scratch_shapes=scratch,
            compiler_params=params,
            cost_estimate=pl.CostEstimate(flops=1000, bytes_accessed=1000, transcendentals=0),
            name=f"pairs_{blocks[0]}",
        )(*operands)

    far = along(right, 2)
    near = along(right, 1)
    last = along(far, 1)
    chip = across(to_chip, 2)
    core = across(to_core, 1)
    middle = pack(near, far, after=(), weight=4_000_000_000)
    beside = across(middle, 1)
    both = across(pack(chip, after=(last, core)), 1)
    lefts = ((left_own, 0), (core, 0), (chip, 0), (both, left_count))
    own = ((right, 0), (core, left_count), (chip, 2 * left_count), (both, 2 * left_count))
    first, *shared = pairs((own,), (0,), w, lefts=lefts)

    other = across(middle, 2)
    onward = across(pack(other, after=(shared[1],)), 1)
    onward = ((onward, 0), (onward, right_count))
    blocks = [
        ((middle, at), (beside, at), (other, at), onward[i]) for i, at in enumerate((0, right_count))
    ]
    (second,) = pairs(blocks, (1, 2), *shared)

    other = across(last, 2)
    both = across(pack(last, other, after=()), 1)
    (out,) = pairs(
        (((last, 0), (both, 0), (other, 0), (both, right_count)),), (3,), *shared,
        earlier=((first, (0,)), (second, (1, 2))),
    )
    return out


def solution(mesh):
    in_specs = (P(("groups", "narrow"), "wide", None), P(), P(), P(), P(), P(), P(), P(), P())
    out_specs = P(("groups", "wide", "narrow"), None, None)
    return jax.shard_map(
        functools.partial(on_device, mesh.shape["wide"], mesh.shape["narrow"]),
        mesh=mesh,
        in_specs=in_specs,
        out_specs=out_specs,
        check_vma=False,
    )
```

```python
import functools

import jax
import jax.numpy as jnp
from jax import lax
from jax.experimental import pallas as pl
from jax.experimental.pallas import tpu as pltpu
from jax.sharding import PartitionSpec as P

LANES = 128
RIGHT = -1
VMEM_LIMIT = 40 * 1024 * 1024
VMEM_ALL = 62 * 1024 * 1024


def iota(shape, dim):
    return lax.broadcasted_iota(jnp.int32, shape, dim)


def features_kernel(*refs, packs, parts, pieces):
    args, refs = refs[:9], refs[9:]
    outs, wf_hbm, refs = refs[: len(packs)], refs[len(packs)], refs[len(packs) + 1 :]
    held, (lo_ref, hi_ref, left_ref, turned_ref, rows_ref, right_ref, wf_ref, sems) = refs[:9], refs[9:]
    x_ref, gain_ref, bias_ref, lm_ref, lb_ref, rm_ref, rb_ref, w_ref, shift_ref = held
    seqs, residues, depth = x_ref.shape
    hidden = lm_ref.shape[0]
    per = LANES // hidden
    slots = LANES // seqs
    minor = hidden // slots
    groups = residues // per
    own = lax.axis_index("narrow")

    piece = seqs // pieces
    copies = [
        pltpu.make_async_copy(
            args[0].at[pl.ds(p * piece, piece)], x_ref.at[pl.ds(p * piece, piece)], sems.at[p]
        )
        for p in range(pieces)
    ]
    rest = [
        pltpu.make_async_copy(a, b, sems.at[pieces + i]) for i, (a, b) in enumerate(zip(args[1:], held[1:]))
    ]
    for copy in copies[:1] + rest[:2] + copies[1:] + rest[2:]:
        copy.start()
    free = pieces + len(rest)

    def norm(p):
        gain = gain_ref[...].reshape(1, depth)
        bias = bias_ref[...].reshape(1, depth)
        step = min(4, piece)
        for s in range(p * piece, (p + 1) * piece, step):
            x = x_ref[s : s + step].reshape(step * residues, depth).astype(jnp.float32)
            x = x - jnp.mean(x, axis=-1, keepdims=True)
            spread = jnp.mean(x * x, axis=-1, keepdims=True)
            x = x * lax.rsqrt(spread + 1e-05) * gain + bias
            rows = pl.ds(s * residues, step * residues)
            lo_ref[rows, :] = x[:, :LANES]
            hi_ref[rows, :] = x[:, LANES:]

    for copy in rest[:2]:
        copy.wait()
    for p in range(pieces - 1):
        copies[p].wait()
        norm(p)
    for copy in copies[-1:] + rest[2:]:
        copy.wait()
    count = w_ref.shape[0]
    wf_ref[:count] = w_ref[...].astype(jnp.float32)
    wf_ref[count:] = jnp.broadcast_to(
        shift_ref[...].reshape(1, -1), (wf_ref.shape[0] - count, shift_ref.shape[0])
    )
    norm(pieces - 1)

    column, row = iota((hidden, LANES), 1) % hidden, iota((hidden, LANES), 0)
    spread_l = (column == row).astype(jnp.float32)
    spread_r = (column == (row ^ (own * minor))).astype(jnp.float32)

    def widen(m, pick):
        return lax.dot_general(
            m, pick.astype(jnp.bfloat16), (((0,), (0,)), ((), ())),
            preferred_element_type=jnp.float32,
        )

    lane = iota((8, LANES), 1)

    def widen_bias(b):
        b = jnp.concatenate([b.reshape(1, hidden)] * per, axis=1)
        return jnp.broadcast_to(b, (8, LANES))

    def swapped(b):
        bit = 1
        while bit < slots:
            step = bit * minor
            up, down = pltpu.roll(b, step, axis=1), pltpu.roll(b, LANES - step, axis=1)
            other = jnp.where(lane & step != 0, up, down)
            b = jnp.where(own & bit != 0, other, b)
            bit *= 2
        return b

    weights = jnp.concatenate(
        [widen(lm_ref[...], spread_l), widen(rm_ref[...], spread_r)], axis=1
    )
    shift = jnp.concatenate(
        [widen_bias(lb_ref[...]), swapped(widen_bias(rb_ref[...]))], axis=1
    )[:1]
    place = iota((depth, 2 * LANES), 1) % LANES // hidden
    sends = [pltpu.make_async_copy(wf_ref, wf_hbm, sems.at[free])]
    sends[0].start()

    total = None
    for k in range(per):
        part = jnp.concatenate(
            [
                jnp.concatenate(
                    [half[pl.ds(g * per + k, seqs, stride=residues), :] for half in (lo_ref, hi_ref)],
                    axis=1,
                )
                for g in range(groups)
            ],
            axis=0,
        ).astype(jnp.bfloat16)
        placed = jnp.where(place == k, weights, 0.0).astype(jnp.bfloat16)
        term = jnp.dot(part, placed, preferred_element_type=jnp.float32)
        total = term if total is None else total + term
    total = total + shift
    left_ref[...] = total[:, :LANES].astype(left_ref.dtype)

    slot = iota((minor, LANES), 1) // seqs
    for block in range(groups // slots):
        turned_ref[...] = total[block * LANES : (block + 1) * LANES, LANES:].T
        for k in range(per):
            parts_of = [turned_ref[pl.ds(k * hidden + q * minor, minor), :] for q in range(slots)]
            for g in range(slots):
                out = None
                for q in range(slots):
                    moved = parts_of[q]
                    if q != g:
                        moved = pltpu.roll(moved, (q - g) % slots * seqs, axis=1)
                    out = moved if out is None else jnp.where(slot == q, moved, out)
                j = (block * slots + g) * per + k
                rows_ref[pl.ds(j, minor, stride=residues), :] = out
    right_ref[...] = rows_ref[: minor * residues].astype(right_ref.dtype)

    mine = left_ref.shape[0] // parts
    for out, pack in zip(outs, packs):
        at = 0
        for item in pack:
            if item == RIGHT:
                rows = right_ref
            else:
                rows = left_ref.at[pl.ds(pl.multiple_of((own ^ item) * mine, 16), mine)]
            free += 1
            sends.append(
                pltpu.make_async_copy(rows, out.at[pl.ds(at, rows.shape[0])], sems.at[free])
            )
            sends[-1].start()
            at += rows.shape[0]
    for copy in sends:
        copy.wait()


def block_weights(wf_ref, wide_ref, *, parts, minor):
    cz = wf_ref.shape[1]
    hidden = parts * minor
    half = minor // 2
    rows_each = wide_ref.shape[0] // hidden // hidden
    own = lax.axis_index("narrow")
    wide_ref[...] = jnp.zeros_like(wide_ref)
    for e in range(hidden):
        rows = wf_ref[pl.ds(e ^ (own * minor), hidden, stride=hidden), :].astype(jnp.bfloat16)
        q, e2, t = e // minor, e % minor // half, e % half
        for k in range(rows_each):
            at = ((((q * half + t) * 2 + e2) * rows_each) + k) * hidden
            wide_ref[at : at + hidden, k * cz : (k + 1) * cz] = rows


def pack_kernel(*refs, count):
    out_ref, at = refs[-1], 0
    for ref in refs[:count]:
        out_ref[at : at + ref.shape[0]] = ref[...]
        at += ref.shape[0]


def spread_left(left_of, spread_ref, *, parts):
    seqs = LANES // parts
    low = iota((seqs, LANES), 1) < LANES // 2
    zero = jnp.zeros((seqs, LANES), jnp.float32)
    for m in range(parts):
        left = left_of(m)
        for g in range(left.shape[0] // seqs):
            rows = left[g * seqs : (g + 1) * seqs].astype(jnp.float32)
            turned = pltpu.roll(rows, LANES // 2, axis=1)
            for half, (first, second) in enumerate(((rows, turned), (turned, rows))):
                lanes = pl.ds((2 * g + half) * LANES, LANES)
                spread_ref[m, 0, :, lanes] = jnp.where(low, first, zero).astype(spread_ref.dtype)
                spread_ref[m, 1, :, lanes] = jnp.where(low, zero, second).astype(spread_ref.dtype)


def pair_rows(spread_ref, right_of, wide_ref, shift, outer_ref, store, *, wides, parts, minor, seqs_total):
    cz = shift.shape[1]
    half = minor // 2
    seqs = LANES // parts
    halves = spread_ref.shape[3] // LANES
    residues = right_of(0, 0).shape[0] // minor
    cols = wides * residues
    slot = iota((minor * residues, LANES), 1) // seqs
    for q in range(parts):
        left = jnp.concatenate([spread_ref[q ^ k, i] for i in range(2) for k in range(parts)], axis=0)
        rights = []
        for d in range(wides):
            right = None
            for k in range(parts):
                chunk = right_of(d, q ^ k)
                right = chunk if right is None else jnp.where(slot == k, chunk, right)
            rights.append(jnp.concatenate([right[: half * residues], right[half * residues :]], axis=1))
        right = jnp.concatenate(rights, axis=0)
        outer = jnp.dot(right, left, preferred_element_type=jnp.float32).astype(jnp.bfloat16)
        for d in range(wides):
            for t in range(half):
                at = (d * half + t) * residues
                for g in range(halves):
                    outer_ref[
                        pl.ds(g * cols + d * residues, residues),
                        (q * half + t) * LANES : (q * half + t + 1) * LANES,
                    ] = outer[at : at + residues, g * LANES : (g + 1) * LANES]

    pairs = jnp.dot(outer_ref[...], wide_ref[...], preferred_element_type=jnp.float32)
    rows_each = wide_ref.shape[1] // cz
    for g in range(halves):
        for k in range(rows_each):
            pair = pairs[g * cols : (g + 1) * cols, k * cz : (k + 1) * cz]
            store(g * rows_each + k, pair * (1.0 / seqs_total) + shift)


def pair_kernel(*refs, operands, rights, blocks, earlier, lefts=None, **sizes):
    parts, minor = sizes["parts"], sizes["minor"]
    inputs, refs = refs[:operands], refs[operands:]
    if lefts is not None:
        wf_ref, done_ref, spread_ref, wide_ref, shift_ref, outer_ref = refs
        own_rows = done_ref.shape[0]
        block_weights(wf_ref, wide_ref, parts=parts, minor=minor)
        shift_ref[...] = wf_ref[wf_ref.shape[0] - 8 :]
        count = own_rows * minor
        spread_left(lambda m: inputs[lefts[m][0]][lefts[m][1] : lefts[m][1] + count, :], spread_ref, parts=parts)
    elif not earlier:
        spread_ref, wide_ref, shift_ref, done_ref, outer_ref = refs
    else:
        spread_ref, wide_ref, shift_ref = refs[:3]
        before, (out_hbm, outer_ref, done_ref, sems) = refs[3 : 3 + len(earlier)], refs[3 + len(earlier) :]
    residues = done_ref.shape[1] // len(blocks)
    copies = []

    def write(ref, places):
        for d, block in enumerate(places):
            at = pl.multiple_of((lax.axis_index("wide") ^ block) * residues, 16)
            copies.append(
                pltpu.make_async_copy(
                    ref.at[:, pl.ds(d * residues, residues), :],
                    out_hbm.at[:, pl.ds(at, residues), :],
                    sems.at[len(copies)],
                )
            )
            copies[-1].start()

    if earlier:
        for ref, places in zip(before, earlier):
            write(ref, places)

    def right_of(d, m):
        ref, at = rights[d][m]
        return inputs[ref][at : at + minor * residues, :]

    def store(row, pair):
        done_ref[row] = pair.astype(done_ref.dtype)

    pair_rows(spread_ref, right_of, wide_ref, shift_ref[:1], outer_ref, store, wides=len(blocks), **sizes)
    if earlier:
        write(done_ref, blocks)
        for copy in copies:
            copy.wait()


def pair_blocks_kernel(*refs, wides, parts, minor, **sizes):
    left_refs, (right_ref, wf_ref, out_ref, spread_ref, wide_ref, outer_ref) = refs[:parts], refs[parts:]

    @pl.when(pl.program_id(0) == 0)
    def _():
        block_weights(wf_ref, wide_ref, parts=parts, minor=minor)
        spread_left(lambda m: left_refs[m][...], spread_ref, parts=parts)

    def store(row, pair):
        out_ref[row] = pair.astype(out_ref.dtype)

    pair_rows(
        spread_ref, lambda d, m: right_ref[d, m],
        wide_ref, wf_ref[wf_ref.shape[0] - 8 :][:1], outer_ref, store,
        wides=wides, parts=parts, minor=minor, **sizes,
    )


def on_device(wide, narrow, x, gain, bias, lm, lb, rm, rb, w, shift):
    seqs, residues, depth = x.shape
    hidden = lm.shape[1]
    cz = w.shape[1]
    per = LANES // hidden
    slots = LANES // seqs
    minor = hidden // slots
    own_rows = residues // narrow
    groups = own_rows // per
    pieces = 4
    hbm = pl.BlockSpec(memory_space=pltpu.HBM)
    vmem = pl.BlockSpec(memory_space=pltpu.VMEM)
    params = pltpu.CompilerParams(vmem_limit_bytes=VMEM_LIMIT)
    direct = wide == 4 and narrow == 4
    if direct:
        packs = ((0,), (RIGHT,), (1, RIGHT), (2, 3, RIGHT))
    else:
        packs = tuple((m,) for m in range(narrow)) + ((RIGHT,),)
    left_count, right_count = groups * seqs, minor * residues
    args = (x, gain, bias, lm.T, lb, rm.T, rb, w, shift)
    *made, w = pl.pallas_call(
        functools.partial(features_kernel, packs=packs, parts=narrow, pieces=pieces),
        out_shape=tuple(
            jax.ShapeDtypeStruct(
                (sum(right_count if i == RIGHT else left_count for i in pack), LANES), jnp.bfloat16
            )
            for pack in packs
        )
        + (jax.ShapeDtypeStruct((w.shape[0] + hidden + 8, cz), jnp.float32),),
        in_specs=[hbm] * len(args),
        out_specs=(hbm,) * (len(packs) + 1),
        scratch_shapes=[pltpu.VMEM(a.shape, a.dtype) for a in args]
        + [
            pltpu.VMEM(((seqs + 1) * residues, LANES), jnp.float32),
            pltpu.VMEM(((seqs + 1) * residues, LANES), jnp.float32),
            pltpu.VMEM((residues // per * seqs, LANES), jnp.bfloat16),
            pltpu.VMEM((LANES, LANES), jnp.float32),
            pltpu.VMEM(((minor + 1) * residues, LANES), jnp.float32),
            pltpu.VMEM((minor * residues, LANES), jnp.bfloat16),
            pltpu.VMEM((w.shape[0] + hidden + 8, cz), jnp.float32),
            pltpu.SemaphoreType.DMA((pieces + len(args) + sum(len(pack) for pack in packs),)),
        ],
        compiler_params=pltpu.CompilerParams(vmem_limit_bytes=VMEM_ALL),
        name="features",
    )(*args)

    def across(a, m):
        return lax.ppermute(a, "narrow", [(i, i ^ m) for i in range(narrow)])

    def along(a, d):
        return lax.ppermute(a, "wide", [(i, i ^ d) for i in range(wide)])

    sizes = dict(parts=narrow, minor=minor, seqs_total=seqs * narrow)
    out_shape = jax.ShapeDtypeStruct((own_rows, wide * residues, cz), jnp.bfloat16)
    if direct:
        return pairs_by_block(made, across, along, w, out_shape, residues, sizes, params)

    lefts = [made[0]] + [across(made[m], m) for m in range(1, narrow)]
    every = lax.all_gather(made[narrow], ("wide", "narrow"), axis=0, tiled=False)
    every = every.reshape(wide, narrow, right_count, LANES)
    every = jnp.take(every, lax.axis_index("narrow") ^ jnp.arange(narrow), axis=1)
    block = wide
    while block % 2 == 0 and block * residues > 192:
        block //= 2
    cols = block * residues
    return pl.pallas_call(
        functools.partial(pair_blocks_kernel, wides=block, **sizes),
        grid=(wide // block,),
        in_specs=[pl.BlockSpec((left_count, LANES), lambda b: (0, 0))] * narrow
        + [
            pl.BlockSpec((block, narrow, right_count, LANES), lambda b: (b, 0, 0, 0)),
            pl.BlockSpec(w.shape, lambda b: (0, 0)),
        ],
        out_specs=pl.BlockSpec((own_rows, cols, cz), lambda b: (0, b, 0)),
        out_shape=out_shape,
        scratch_shapes=[
            pltpu.VMEM((narrow, 2, seqs, 2 * groups * LANES), jnp.bfloat16),
            pltpu.VMEM((hidden * LANES // 2, 2 * cz), jnp.bfloat16),
            pltpu.VMEM((2 * groups * cols, hidden * LANES // 2), jnp.bfloat16),
        ],
        compiler_params=params,
        name="pairs",
    )(*lefts, every, w)


def pairs_by_block(made, across, along, w, out_shape, residues, sizes, params):
    left_own, right, to_core, to_chip = made
    left_count, right_count = left_own.shape[0], right.shape[0]
    hbm = pl.BlockSpec(memory_space=pltpu.HBM)
    vmem = pl.BlockSpec(memory_space=pltpu.VMEM)
    own_rows, _, cz = out_shape.shape
    narrow = sizes["parts"]
    hidden = narrow * sizes["minor"]
    groups = own_rows * hidden // LANES

    def pack(*chunks, after, weight=1):
        return pl.pallas_call(
            functools.partial(pack_kernel, count=len(chunks)),
            out_shape=jax.ShapeDtypeStruct((sum(c.shape[0] for c in chunks), LANES), jnp.bfloat16),
            in_specs=[vmem] * (len(chunks) + len(after)),
            out_specs=vmem,
            compiler_params=params,
            cost_estimate=pl.CostEstimate(flops=weight, bytes_accessed=1000, transcendentals=0),
            name="pack",
        )(*chunks, *after)

    def pairs(rights, blocks, *shared, lefts=None, earlier=()):
        operands = []

        def place(chunk, at):
            operands.append(chunk)
            return len(operands) - 1, at

        rights = [[place(*chunk) for chunk in block] for block in rights]
        lefts = lefts and [place(*chunk) for chunk in lefts]
        count = len(operands)
        operands += shared
        cols = len(blocks) * residues
        done = jax.ShapeDtypeStruct((own_rows, cols, cz), jnp.bfloat16)
        shapes, outs = [done], [vmem]
        scratch = [pltpu.VMEM((2 * groups * cols, hidden * LANES // 2), jnp.bfloat16)]
        if lefts is not None:
            shapes += [
                jax.ShapeDtypeStruct((narrow, 2, LANES // narrow, 2 * groups * LANES), jnp.bfloat16),
                jax.ShapeDtypeStruct((hidden * LANES // 2, 2 * cz), jnp.bfloat16),
                jax.ShapeDtypeStruct((8, cz), jnp.float32),
            ]
            outs += [vmem] * 3
        if earlier:
            operands += [ref for ref, _ in earlier]
            shapes, outs = [out_shape], [hbm]
            scratch += [
                pltpu.VMEM(done.shape, done.dtype),
                pltpu.SemaphoreType.DMA((len(blocks) + sum(len(b) for _, b in earlier),)),
            ]
        return pl.pallas_call(
            functools.partial(
                pair_kernel, operands=count, rights=rights, blocks=blocks,
                earlier=[b for _, b in earlier], lefts=lefts, **sizes,
            ),
            out_shape=shapes,
            in_specs=[vmem] * len(operands),
            out_specs=outs,
            scratch_shapes=scratch,
            compiler_params=params,
            cost_estimate=pl.CostEstimate(flops=1000, bytes_accessed=1000, transcendentals=0),
            name=f"pairs_{blocks[0]}",
        )(*operands)

    far = along(right, 2)
    near = along(right, 1)
    last = along(far, 1)
    chip = across(to_chip, 2)
    core = across(to_core, 1)
    middle = pack(near, far, after=(), weight=4_000_000_000)
    beside = across(middle, 1)
    both = across(pack(chip, after=(last, core)), 1)
    lefts = ((left_own, 0), (core, 0), (chip, 0), (both, left_count))
    own = ((right, 0), (core, left_count), (chip, 2 * left_count), (both, 2 * left_count))
    first, *shared = pairs((own,), (0,), w, lefts=lefts)

    other = across(middle, 2)
    onward = across(pack(other, after=(shared[1],)), 1)
    onward = ((onward, 0), (onward, right_count))
    blocks = [
        ((middle, at), (beside, at), (other, at), onward[i]) for i, at in enumerate((0, right_count))
    ]
    (second,) = pairs(blocks, (1, 2), *shared)

    other = across(last, 2)
    both = across(pack(last, other, after=()), 1)
    (out,) = pairs(
        (((last, 0), (both, 0), (other, 0), (both, right_count)),), (3,), *shared,
        earlier=((first, (0,)), (second, (1, 2))),
    )
    return out


def solution(mesh):
    in_specs = (P(("groups", "narrow"), "wide", None), P(), P(), P(), P(), P(), P(), P(), P())
    out_specs = P(("groups", "wide", "narrow"), None, None)
    return jax.shard_map(
        functools.partial(on_device, mesh.shape["wide"], mesh.shape["narrow"]),
        mesh=mesh,
        in_specs=in_specs,
        out_specs=out_specs,
        check_vma=False,
    )
```

```python
import functools

import jax
import jax.numpy as jnp
from jax import lax
from jax.experimental import pallas as pl
from jax.experimental.pallas import tpu as pltpu
from jax.sharding import PartitionSpec as P

LANES = 128
RIGHT = -1
VMEM_LIMIT = 40 * 1024 * 1024
VMEM_ALL = 62 * 1024 * 1024


def iota(shape, dim):
    return lax.broadcasted_iota(jnp.int32, shape, dim)


def features_kernel(*refs, packs, parts, pieces):
    args, refs = refs[:7], refs[7:]
    outs, refs = refs[: len(packs)], refs[len(packs) :]
    held, (lo_ref, hi_ref, left_ref, turned_ref, rows_ref, right_ref, sems) = refs[:7], refs[7:]
    x_ref, gain_ref, bias_ref, lm_ref, lb_ref, rm_ref, rb_ref = held
    seqs, residues, depth = x_ref.shape
    hidden = lm_ref.shape[0]
    per = LANES // hidden
    slots = LANES // seqs
    minor = hidden // slots
    groups = residues // per
    own = lax.axis_index("narrow")

    piece = seqs // pieces
    copies = [
        pltpu.make_async_copy(
            args[0].at[pl.ds(p * piece, piece)], x_ref.at[pl.ds(p * piece, piece)], sems.at[p]
        )
        for p in range(pieces)
    ]
    rest = [
        pltpu.make_async_copy(a, b, sems.at[pieces + i]) for i, (a, b) in enumerate(zip(args[1:], held[1:]))
    ]
    for copy in copies[:1] + rest[:2] + copies[1:] + rest[2:]:
        copy.start()
    free = pieces + len(rest)

    def norm(p):
        gain = gain_ref[...].reshape(1, depth)
        bias = bias_ref[...].reshape(1, depth)
        step = min(4, piece)
        for s in range(p * piece, (p + 1) * piece, step):
            x = x_ref[s : s + step].reshape(step * residues, depth).astype(jnp.float32)
            x = x - jnp.mean(x, axis=-1, keepdims=True)
            spread = jnp.mean(x * x, axis=-1, keepdims=True)
            x = x * lax.rsqrt(spread + 1e-05) * gain + bias
            rows = pl.ds(s * residues, step * residues)
            lo_ref[rows, :] = x[:, :LANES]
            hi_ref[rows, :] = x[:, LANES:]

    for copy in rest[:2]:
        copy.wait()
    for p in range(pieces - 1):
        copies[p].wait()
        norm(p)
    for copy in copies[-1:] + rest[2:]:
        copy.wait()
    norm(pieces - 1)

    column, row = iota((hidden, LANES), 1) % hidden, iota((hidden, LANES), 0)
    spread_l = (column == row).astype(jnp.float32)
    spread_r = (column == (row ^ (own * minor))).astype(jnp.float32)

    def widen(m, pick):
        return lax.dot_general(
            m, pick.astype(jnp.bfloat16), (((0,), (0,)), ((), ())),
            preferred_element_type=jnp.float32,
        )

    lane = iota((8, LANES), 1)

    def widen_bias(b):
        b = jnp.concatenate([b.reshape(1, hidden)] * per, axis=1)
        return jnp.broadcast_to(b, (8, LANES))

    def swapped(b):
        bit = 1
        while bit < slots:
            step = bit * minor
            up, down = pltpu.roll(b, step, axis=1), pltpu.roll(b, LANES - step, axis=1)
            other = jnp.where(lane & step != 0, up, down)
            b = jnp.where(own & bit != 0, other, b)
            bit *= 2
        return b

    weights = jnp.concatenate(
        [widen(lm_ref[...], spread_l), widen(rm_ref[...], spread_r)], axis=1
    )
    shift = jnp.concatenate(
        [widen_bias(lb_ref[...]), swapped(widen_bias(rb_ref[...]))], axis=1
    )[:1]
    place = iota((depth, 2 * LANES), 1) % LANES // hidden
    sends = []

    total = None
    for k in range(per):
        part = jnp.concatenate(
            [
                jnp.concatenate(
                    [half[pl.ds(g * per + k, seqs, stride=residues), :] for half in (lo_ref, hi_ref)],
                    axis=1,
                )
                for g in range(groups)
            ],
            axis=0,
        ).astype(jnp.bfloat16)
        placed = jnp.where(place == k, weights, 0.0).astype(jnp.bfloat16)
        term = jnp.dot(part, placed, preferred_element_type=jnp.float32)
        total = term if total is None else total + term
    total = total + shift
    left_ref[...] = total[:, :LANES].astype(left_ref.dtype)

    slot = iota((minor, LANES), 1) // seqs
    for block in range(groups // slots):
        turned_ref[...] = total[block * LANES : (block + 1) * LANES, LANES:].T
        for k in range(per):
            parts_of = [turned_ref[pl.ds(k * hidden + q * minor, minor), :] for q in range(slots)]
            for g in range(slots):
                out = None
                for q in range(slots):
                    moved = parts_of[q]
                    if q != g:
                        moved = pltpu.roll(moved, (q - g) % slots * seqs, axis=1)
                    out = moved if out is None else jnp.where(slot == q, moved, out)
                j = (block * slots + g) * per + k
                rows_ref[pl.ds(j, minor, stride=residues), :] = out
    right_ref[...] = rows_ref[: minor * residues].astype(right_ref.dtype)

    mine = left_ref.shape[0] // parts
    for out, pack in zip(outs, packs):
        at = 0
        for item in pack:
            if item == RIGHT:
                rows = right_ref
            else:
                rows = left_ref.at[pl.ds(pl.multiple_of((own ^ item) * mine, 16), mine)]
            free += 1
            sends.append(
                pltpu.make_async_copy(rows, out.at[pl.ds(at, rows.shape[0])], sems.at[free])
            )
            sends[-1].start()
            at += rows.shape[0]
    for copy in sends:
        copy.wait()


def load_kernel(w_ref, shift_ref, after_ref, wf_ref):
    del after_ref
    count = w_ref.shape[0]
    wf_ref[:count] = w_ref[...].astype(jnp.float32)
    wf_ref[count:] = jnp.broadcast_to(
        shift_ref[...].reshape(1, -1), (wf_ref.shape[0] - count, shift_ref.shape[0])
    )


def block_weights(wf_ref, wide_ref, *, parts, minor):
    cz = wf_ref.shape[1]
    hidden = parts * minor
    half = minor // 2
    rows_each = wide_ref.shape[0] // hidden // hidden
    own = lax.axis_index("narrow")
    wide_ref[...] = jnp.zeros_like(wide_ref)
    for e in range(hidden):
        rows = wf_ref[pl.ds(e ^ (own * minor), hidden, stride=hidden), :].astype(jnp.bfloat16)
        q, e2, t = e // minor, e % minor // half, e % half
        for k in range(rows_each):
            at = ((((q * half + t) * 2 + e2) * rows_each) + k) * hidden
            wide_ref[at : at + hidden, k * cz : (k + 1) * cz] = rows


def pack_kernel(*refs, count):
    out_ref, at = refs[-1], 0
    for ref in refs[:count]:
        out_ref[at : at + ref.shape[0]] = ref[...]
        at += ref.shape[0]


def spread_left(left_of, spread_ref, *, parts):
    seqs = LANES // parts
    low = iota((seqs, LANES), 1) < LANES // 2
    zero = jnp.zeros((seqs, LANES), jnp.float32)
    for m in range(parts):
        left = left_of(m)
        for g in range(left.shape[0] // seqs):
            rows = left[g * seqs : (g + 1) * seqs].astype(jnp.float32)
            turned = pltpu.roll(rows, LANES // 2, axis=1)
            for half, (first, second) in enumerate(((rows, turned), (turned, rows))):
                lanes = pl.ds((2 * g + half) * LANES, LANES)
                spread_ref[m, 0, :, lanes] = jnp.where(low, first, zero).astype(spread_ref.dtype)
                spread_ref[m, 1, :, lanes] = jnp.where(low, zero, second).astype(spread_ref.dtype)


def pair_rows(spread_ref, right_of, wide_ref, shift, outer_ref, store, *, wides, parts, minor, seqs_total):
    cz = shift.shape[1]
    half = minor // 2
    seqs = LANES // parts
    halves = spread_ref.shape[3] // LANES
    residues = right_of(0, 0).shape[0] // minor
    cols = wides * residues
    slot = iota((minor * residues, LANES), 1) // seqs
    for q in range(parts):
        left = jnp.concatenate([spread_ref[q ^ k, i] for i in range(2) for k in range(parts)], axis=0)
        rights = []
        for d in range(wides):
            right = None
            for k in range(parts):
                chunk = right_of(d, q ^ k)
                right = chunk if right is None else jnp.where(slot == k, chunk, right)
            rights.append(jnp.concatenate([right[: half * residues], right[half * residues :]], axis=1))
        right = jnp.concatenate(rights, axis=0)
        outer = jnp.dot(right, left, preferred_element_type=jnp.float32).astype(jnp.bfloat16)
        for d in range(wides):
            for t in range(half):
                at = (d * half + t) * residues
                for g in range(halves):
                    outer_ref[
                        pl.ds(g * cols + d * residues, residues),
                        (q * half + t) * LANES : (q * half + t + 1) * LANES,
                    ] = outer[at : at + residues, g * LANES : (g + 1) * LANES]

    pairs = jnp.dot(outer_ref[...], wide_ref[...], preferred_element_type=jnp.float32)
    rows_each = wide_ref.shape[1] // cz
    for g in range(halves):
        for k in range(rows_each):
            pair = pairs[g * cols : (g + 1) * cols, k * cz : (k + 1) * cz]
            store(g * rows_each + k, pair * (1.0 / seqs_total) + shift)


def pair_kernel(*refs, operands, rights, blocks, earlier, lefts=None, **sizes):
    parts, minor = sizes["parts"], sizes["minor"]
    inputs, refs = refs[:operands], refs[operands:]
    if lefts is not None:
        wf_ref, done_ref, spread_ref, wide_ref, shift_ref, outer_ref = refs
        own_rows = done_ref.shape[0]
        block_weights(wf_ref, wide_ref, parts=parts, minor=minor)
        shift_ref[...] = wf_ref[wf_ref.shape[0] - 8 :]
        count = own_rows * minor
        spread_left(lambda m: inputs[lefts[m][0]][lefts[m][1] : lefts[m][1] + count, :], spread_ref, parts=parts)
    elif not earlier:
        spread_ref, wide_ref, shift_ref, done_ref, outer_ref = refs
    else:
        spread_ref, wide_ref, shift_ref = refs[:3]
        before, (out_hbm, outer_ref, done_ref, sems) = refs[3 : 3 + len(earlier)], refs[3 + len(earlier) :]
    residues = done_ref.shape[1] // len(blocks)
    copies = []

    def write(ref, places):
        for d, block in enumerate(places):
            at = pl.multiple_of((lax.axis_index("wide") ^ block) * residues, 16)
            copies.append(
                pltpu.make_async_copy(
                    ref.at[:, pl.ds(d * residues, residues), :],
                    out_hbm.at[:, pl.ds(at, residues), :],
                    sems.at[len(copies)],
                )
            )
            copies[-1].start()

    if earlier:
        for ref, places in zip(before, earlier):
            write(ref, places)

    def right_of(d, m):
        ref, at = rights[d][m]
        return inputs[ref][at : at + minor * residues, :]

    def store(row, pair):
        done_ref[row] = pair.astype(done_ref.dtype)

    pair_rows(spread_ref, right_of, wide_ref, shift_ref[:1], outer_ref, store, wides=len(blocks), **sizes)
    if earlier:
        write(done_ref, blocks)
        for copy in copies:
            copy.wait()


def pair_blocks_kernel(*refs, wides, parts, minor, **sizes):
    left_refs, (right_ref, wf_ref, out_ref, spread_ref, wide_ref, outer_ref) = refs[:parts], refs[parts:]

    @pl.when(pl.program_id(0) == 0)
    def _():
        block_weights(wf_ref, wide_ref, parts=parts, minor=minor)
        spread_left(lambda m: left_refs[m][...], spread_ref, parts=parts)

    def store(row, pair):
        out_ref[row] = pair.astype(out_ref.dtype)

    pair_rows(
        spread_ref, lambda d, m: right_ref[d, m],
        wide_ref, wf_ref[wf_ref.shape[0] - 8 :][:1], outer_ref, store,
        wides=wides, parts=parts, minor=minor, **sizes,
    )


def on_device(wide, narrow, x, gain, bias, lm, lb, rm, rb, w, shift):
    seqs, residues, depth = x.shape
    hidden = lm.shape[1]
    cz = w.shape[1]
    per = LANES // hidden
    slots = LANES // seqs
    minor = hidden // slots
    own_rows = residues // narrow
    groups = own_rows // per
    pieces = 4
    hbm = pl.BlockSpec(memory_space=pltpu.HBM)
    vmem = pl.BlockSpec(memory_space=pltpu.VMEM)
    params = pltpu.CompilerParams(vmem_limit_bytes=VMEM_LIMIT)
    direct = wide == 4 and narrow == 4
    if direct:
        packs = ((0,), (RIGHT,), (1, RIGHT), (2, 3, RIGHT))
    else:
        packs = tuple((m,) for m in range(narrow)) + ((RIGHT,),)
    left_count, right_count = groups * seqs, minor * residues
    args = (x, gain, bias, lm.T, lb, rm.T, rb)
    made = pl.pallas_call(
        functools.partial(features_kernel, packs=packs, parts=narrow, pieces=pieces),
        out_shape=tuple(
            jax.ShapeDtypeStruct(
                (sum(right_count if i == RIGHT else left_count for i in pack), LANES), jnp.bfloat16
            )
            for pack in packs
        ),
        in_specs=[hbm] * len(args),
        out_specs=(hbm,) * len(packs),
        scratch_shapes=[pltpu.VMEM(a.shape, a.dtype) for a in args]
        + [
            pltpu.VMEM(((seqs + 1) * residues, LANES), jnp.float32),
            pltpu.VMEM(((seqs + 1) * residues, LANES), jnp.float32),
            pltpu.VMEM((residues // per * seqs, LANES), jnp.bfloat16),
            pltpu.VMEM((LANES, LANES), jnp.float32),
            pltpu.VMEM(((minor + 1) * residues, LANES), jnp.float32),
            pltpu.VMEM((minor * residues, LANES), jnp.bfloat16),
            pltpu.SemaphoreType.DMA((pieces + len(args) + sum(len(pack) for pack in packs),)),
        ],
        compiler_params=pltpu.CompilerParams(vmem_limit_bytes=VMEM_ALL),
        name="features",
    )(*args)

    def load(after):
        return pl.pallas_call(
            load_kernel,
            out_shape=jax.ShapeDtypeStruct((w.shape[0] + hidden + 8, cz), jnp.float32),
            in_specs=[vmem] * 3,
            out_specs=vmem,
            compiler_params=params,
            cost_estimate=pl.CostEstimate(flops=1, bytes_accessed=1000, transcendentals=0),
            name="load",
        )(w, shift, after)

    def across(a, m):
        return lax.ppermute(a, "narrow", [(i, i ^ m) for i in range(narrow)])

    def along(a, d):
        return lax.ppermute(a, "wide", [(i, i ^ d) for i in range(wide)])

    sizes = dict(parts=narrow, minor=minor, seqs_total=seqs * narrow)
    out_shape = jax.ShapeDtypeStruct((own_rows, wide * residues, cz), jnp.bfloat16)
    if direct:
        return pairs_by_block(made, across, along, load, out_shape, residues, sizes, params)

    lefts = [made[0]] + [across(made[m], m) for m in range(1, narrow)]
    every = lax.all_gather(made[narrow], ("wide", "narrow"), axis=0, tiled=False)
    every = every.reshape(wide, narrow, right_count, LANES)
    every = jnp.take(every, lax.axis_index("narrow") ^ jnp.arange(narrow), axis=1)
    block = wide
    while block % 2 == 0 and block * residues > 192:
        block //= 2
    cols = block * residues
    return pl.pallas_call(
        functools.partial(pair_blocks_kernel, wides=block, **sizes),
        grid=(wide // block,),
        in_specs=[pl.BlockSpec((left_count, LANES), lambda b: (0, 0))] * narrow
        + [
            pl.BlockSpec((block, narrow, right_count, LANES), lambda b: (b, 0, 0, 0)),
            pl.BlockSpec((w.shape[0] + hidden + 8, cz), lambda b: (0, 0)),
        ],
        out_specs=pl.BlockSpec((own_rows, cols, cz), lambda b: (0, b, 0)),
        out_shape=out_shape,
        scratch_shapes=[
            pltpu.VMEM((narrow, 2, seqs, 2 * groups * LANES), jnp.bfloat16),
            pltpu.VMEM((hidden * LANES // 2, 2 * cz), jnp.bfloat16),
            pltpu.VMEM((2 * groups * cols, hidden * LANES // 2), jnp.bfloat16),
        ],
        compiler_params=params,
        name="pairs",
    )(*lefts, every, load(lefts[0]))


def pairs_by_block(made, across, along, load, out_shape, residues, sizes, params):
    left_own, right, to_core, to_chip = made
    left_count, right_count = left_own.shape[0], right.shape[0]
    hbm = pl.BlockSpec(memory_space=pltpu.HBM)
    vmem = pl.BlockSpec(memory_space=pltpu.VMEM)
    own_rows, _, cz = out_shape.shape
    narrow = sizes["parts"]
    hidden = narrow * sizes["minor"]
    groups = own_rows * hidden // LANES

    def pack(*chunks, after, weight=1):
        return pl.pallas_call(
            functools.partial(pack_kernel, count=len(chunks)),
            out_shape=jax.ShapeDtypeStruct((sum(c.shape[0] for c in chunks), LANES), jnp.bfloat16),
            in_specs=[vmem] * (len(chunks) + len(after)),
            out_specs=vmem,
            compiler_params=params,
            cost_estimate=pl.CostEstimate(flops=weight, bytes_accessed=1000, transcendentals=0),
            name="pack",
        )(*chunks, *after)

    def pairs(rights, blocks, *shared, lefts=None, earlier=()):
        operands = []

        def place(chunk, at):
            operands.append(chunk)
            return len(operands) - 1, at

        rights = [[place(*chunk) for chunk in block] for block in rights]
        lefts = lefts and [place(*chunk) for chunk in lefts]
        count = len(operands)
        operands += shared
        cols = len(blocks) * residues
        done = jax.ShapeDtypeStruct((own_rows, cols, cz), jnp.bfloat16)
        shapes, outs = [done], [vmem]
        scratch = [pltpu.VMEM((2 * groups * cols, hidden * LANES // 2), jnp.bfloat16)]
        if lefts is not None:
            shapes += [
                jax.ShapeDtypeStruct((narrow, 2, LANES // narrow, 2 * groups * LANES), jnp.bfloat16),
                jax.ShapeDtypeStruct((hidden * LANES // 2, 2 * cz), jnp.bfloat16),
                jax.ShapeDtypeStruct((8, cz), jnp.float32),
            ]
            outs += [vmem] * 3
        if earlier:
            operands += [ref for ref, _ in earlier]
            shapes, outs = [out_shape], [hbm]
            scratch += [
                pltpu.VMEM(done.shape, done.dtype),
                pltpu.SemaphoreType.DMA((len(blocks) + sum(len(b) for _, b in earlier),)),
            ]
        return pl.pallas_call(
            functools.partial(
                pair_kernel, operands=count, rights=rights, blocks=blocks,
                earlier=[b for _, b in earlier], lefts=lefts, **sizes,
            ),
            out_shape=shapes,
            in_specs=[vmem] * len(operands),
            out_specs=outs,
            scratch_shapes=scratch,
            compiler_params=params,
            cost_estimate=pl.CostEstimate(flops=1000, bytes_accessed=1000, transcendentals=0),
            name=f"pairs_{blocks[0]}",
        )(*operands)

    far = along(right, 2)
    near = along(right, 1)
    last = along(far, 1)
    chip = across(to_chip, 2)
    core = across(to_core, 1)
    middle = pack(near, far, after=(), weight=4_000_000_000)
    beside = across(middle, 1)
    w = load(chip)
    both = across(pack(chip, after=(last, core, w)), 1)
    lefts = ((left_own, 0), (core, 0), (chip, 0), (both, left_count))
    own = ((right, 0), (core, left_count), (chip, 2 * left_count), (both, 2 * left_count))
    first, *shared = pairs((own,), (0,), w, lefts=lefts)

    other = across(middle, 2)
    onward = across(pack(other, after=(shared[1],)), 1)
    onward = ((onward, 0), (onward, right_count))
    blocks = [
        ((middle, at), (beside, at), (other, at), onward[i]) for i, at in enumerate((0, right_count))
    ]
    (second,) = pairs(blocks, (1, 2), *shared)

    other = across(last, 2)
    both = across(pack(last, other, after=()), 1)
    (out,) = pairs(
        (((last, 0), (both, 0), (other, 0), (both, right_count)),), (3,), *shared,
        earlier=((first, (0,)), (second, (1, 2))),
    )
    return out


def solution(mesh):
    in_specs = (P(("groups", "narrow"), "wide", None), P(), P(), P(), P(), P(), P(), P(), P())
    out_specs = P(("groups", "wide", "narrow"), None, None)
    return jax.shard_map(
        functools.partial(on_device, mesh.shape["wide"], mesh.shape["narrow"]),
        mesh=mesh,
        in_specs=in_specs,
        out_specs=out_specs,
        check_vma=False,
    )
```

```python
import functools

import jax
import jax.numpy as jnp
from jax import lax
from jax.experimental import pallas as pl
from jax.experimental.pallas import tpu as pltpu
from jax.sharding import PartitionSpec as P

LANES = 128
RIGHT = -1
VMEM_LIMIT = 40 * 1024 * 1024
VMEM_ALL = 62 * 1024 * 1024


def iota(shape, dim):
    return lax.broadcasted_iota(jnp.int32, shape, dim)


def features_kernel(*refs, packs, parts, pieces):
    args, refs = refs[:7], refs[7:]
    outs, refs = refs[: len(packs)], refs[len(packs) :]
    held, (lo_ref, hi_ref, left_ref, turned_ref, rows_ref, right_ref, sems) = refs[:7], refs[7:]
    x_ref, gain_ref, bias_ref, lm_ref, lb_ref, rm_ref, rb_ref = held
    seqs, residues, depth = x_ref.shape
    hidden = lm_ref.shape[0]
    per = LANES // hidden
    slots = LANES // seqs
    minor = hidden // slots
    groups = residues // per
    own = lax.axis_index("narrow")

    piece = seqs // pieces
    copies = [
        pltpu.make_async_copy(
            args[0].at[pl.ds(p * piece, piece)], x_ref.at[pl.ds(p * piece, piece)], sems.at[p]
        )
        for p in range(pieces)
    ]
    rest = [
        pltpu.make_async_copy(a, b, sems.at[pieces + i]) for i, (a, b) in enumerate(zip(args[1:], held[1:]))
    ]
    for copy in rest + copies:
        copy.start()
    free = pieces + len(rest)

    def norm(p):
        gain = gain_ref[...].reshape(1, depth)
        bias = bias_ref[...].reshape(1, depth)
        step = min(4, piece)
        for s in range(p * piece, (p + 1) * piece, step):
            x = x_ref[s : s + step].reshape(step * residues, depth).astype(jnp.float32)
            x = x - jnp.mean(x, axis=-1, keepdims=True)
            spread = jnp.mean(x * x, axis=-1, keepdims=True)
            x = x * lax.rsqrt(spread + 1e-05) * gain + bias
            rows = pl.ds(s * residues, step * residues)
            lo_ref[rows, :] = x[:, :LANES]
            hi_ref[rows, :] = x[:, LANES:]

    for copy in rest:
        copy.wait()

    column, row = iota((hidden, LANES), 1) % hidden, iota((hidden, LANES), 0)
    spread_l = (column == row).astype(jnp.float32)
    spread_r = (column == (row ^ (own * minor))).astype(jnp.float32)

    def widen(m, pick):
        return lax.dot_general(
            m, pick.astype(jnp.bfloat16), (((0,), (0,)), ((), ())),
            preferred_element_type=jnp.float32,
        )

    lane = iota((8, LANES), 1)

    def widen_bias(b):
        b = jnp.concatenate([b.reshape(1, hidden)] * per, axis=1)
        return jnp.broadcast_to(b, (8, LANES))

    def swapped(b):
        bit = 1
        while bit < slots:
            step = bit * minor
            up, down = pltpu.roll(b, step, axis=1), pltpu.roll(b, LANES - step, axis=1)
            other = jnp.where(lane & step != 0, up, down)
            b = jnp.where(own & bit != 0, other, b)
            bit *= 2
        return b

    weights = jnp.concatenate(
        [widen(lm_ref[...], spread_l), widen(rm_ref[...], spread_r)], axis=1
    )
    shift = jnp.concatenate(
        [widen_bias(lb_ref[...]), swapped(widen_bias(rb_ref[...]))], axis=1
    )[:1]
    place = iota((depth, 2 * LANES), 1) % LANES // hidden

    for p in range(pieces):
        copies[p].wait()
        norm(p)
    sends = []

    total = None
    for k in range(per):
        part = jnp.concatenate(
            [
                jnp.concatenate(
                    [half[pl.ds(g * per + k, seqs, stride=residues), :] for half in (lo_ref, hi_ref)],
                    axis=1,
                )
                for g in range(groups)
            ],
            axis=0,
        ).astype(jnp.bfloat16)
        placed = jnp.where(place == k, weights, 0.0).astype(jnp.bfloat16)
        term = jnp.dot(part, placed, preferred_element_type=jnp.float32)
        total = term if total is None else total + term
    total = total + shift
    left_ref[...] = total[:, :LANES].astype(left_ref.dtype)

    slot = iota((minor, LANES), 1) // seqs
    for block in range(groups // slots):
        turned_ref[...] = total[block * LANES : (block + 1) * LANES, LANES:].T
        for k in range(per):
            parts_of = [turned_ref[pl.ds(k * hidden + q * minor, minor), :] for q in range(slots)]
            for g in range(slots):
                out = None
                for q in range(slots):
                    moved = parts_of[q]
                    if q != g:
                        moved = pltpu.roll(moved, (q - g) % slots * seqs, axis=1)
                    out = moved if out is None else jnp.where(slot == q, moved, out)
                j = (block * slots + g) * per + k
                rows_ref[pl.ds(j, minor, stride=residues), :] = out
    right_ref[...] = rows_ref[: minor * residues].astype(right_ref.dtype)

    mine = left_ref.shape[0] // parts
    for out, pack in zip(outs, packs):
        at = 0
        for item in pack:
            if item == RIGHT:
                rows = right_ref
            else:
                rows = left_ref.at[pl.ds(pl.multiple_of((own ^ item) * mine, 16), mine)]
            free += 1
            sends.append(
                pltpu.make_async_copy(rows, out.at[pl.ds(at, rows.shape[0])], sems.at[free])
            )
            sends[-1].start()
            at += rows.shape[0]
    for copy in sends:
        copy.wait()


def load_kernel(w_ref, shift_ref, after_ref, wf_ref):
    del after_ref
    count = w_ref.shape[0]
    wf_ref[:count] = w_ref[...].astype(jnp.float32)
    wf_ref[count:] = jnp.broadcast_to(
        shift_ref[...].reshape(1, -1), (wf_ref.shape[0] - count, shift_ref.shape[0])
    )


def block_weights(wf_ref, wide_ref, *, parts, minor):
    cz = wf_ref.shape[1]
    hidden = parts * minor
    half = minor // 2
    rows_each = wide_ref.shape[0] // hidden // hidden
    own = lax.axis_index("narrow")
    wide_ref[...] = jnp.zeros_like(wide_ref)
    for e in range(hidden):
        rows = wf_ref[pl.ds(e ^ (own * minor), hidden, stride=hidden), :].astype(jnp.bfloat16)
        q, e2, t = e // minor, e % minor // half, e % half
        for k in range(rows_each):
            at = ((((q * half + t) * 2 + e2) * rows_each) + k) * hidden
            wide_ref[at : at + hidden, k * cz : (k + 1) * cz] = rows


def pack_kernel(*refs, count):
    out_ref, at = refs[-1], 0
    for ref in refs[:count]:
        out_ref[at : at + ref.shape[0]] = ref[...]
        at += ref.shape[0]


def spread_left(left_of, spread_ref, *, parts):
    seqs = LANES // parts
    low = iota((seqs, LANES), 1) < LANES // 2
    zero = jnp.zeros((seqs, LANES), jnp.float32)
    for m in range(parts):
        left = left_of(m)
        for g in range(left.shape[0] // seqs):
            rows = left[g * seqs : (g + 1) * seqs].astype(jnp.float32)
            turned = pltpu.roll(rows, LANES // 2, axis=1)
            for half, (first, second) in enumerate(((rows, turned), (turned, rows))):
                lanes = pl.ds((2 * g + half) * LANES, LANES)
                spread_ref[m, 0, :, lanes] = jnp.where(low, first, zero).astype(spread_ref.dtype)
                spread_ref[m, 1, :, lanes] = jnp.where(low, zero, second).astype(spread_ref.dtype)


def pair_rows(spread_ref, right_of, wide_ref, shift, outer_ref, store, *, wides, parts, minor, seqs_total):
    cz = shift.shape[1]
    half = minor // 2
    seqs = LANES // parts
    halves = spread_ref.shape[3] // LANES
    residues = right_of(0, 0).shape[0] // minor
    cols = wides * residues
    slot = iota((minor * residues, LANES), 1) // seqs
    for q in range(parts):
        left = jnp.concatenate([spread_ref[q ^ k, i] for i in range(2) for k in range(parts)], axis=0)
        rights = []
        for d in range(wides):
            right = None
            for k in range(parts):
                chunk = right_of(d, q ^ k)
                right = chunk if right is None else jnp.where(slot == k, chunk, right)
            rights.append(jnp.concatenate([right[: half * residues], right[half * residues :]], axis=1))
        right = jnp.concatenate(rights, axis=0)
        outer = jnp.dot(right, left, preferred_element_type=jnp.float32).astype(jnp.bfloat16)
        for d in range(wides):
            for t in range(half):
                at = (d * half + t) * residues
                for g in range(halves):
                    outer_ref[
                        pl.ds(g * cols + d * residues, residues),
                        (q * half + t) * LANES : (q * half + t + 1) * LANES,
                    ] = outer[at : at + residues, g * LANES : (g + 1) * LANES]

    pairs = jnp.dot(outer_ref[...], wide_ref[...], preferred_element_type=jnp.float32)
    rows_each = wide_ref.shape[1] // cz
    for g in range(halves):
        for k in range(rows_each):
            pair = pairs[g * cols : (g + 1) * cols, k * cz : (k + 1) * cz]
            store(g * rows_each + k, pair * (1.0 / seqs_total) + shift)


def pair_kernel(*refs, operands, rights, blocks, earlier, lefts=None, **sizes):
    parts, minor = sizes["parts"], sizes["minor"]
    inputs, refs = refs[:operands], refs[operands:]
    if lefts is not None:
        wf_ref, done_ref, spread_ref, wide_ref, shift_ref, outer_ref = refs
        own_rows = done_ref.shape[0]
        block_weights(wf_ref, wide_ref, parts=parts, minor=minor)
        shift_ref[...] = wf_ref[wf_ref.shape[0] - 8 :]
        count = own_rows * minor
        spread_left(lambda m: inputs[lefts[m][0]][lefts[m][1] : lefts[m][1] + count, :], spread_ref, parts=parts)
    elif not earlier:
        spread_ref, wide_ref, shift_ref, done_ref, outer_ref = refs
    else:
        spread_ref, wide_ref, shift_ref = refs[:3]
        before, (out_hbm, outer_ref, done_ref, sems) = refs[3 : 3 + len(earlier)], refs[3 + len(earlier) :]
    residues = done_ref.shape[1] // len(blocks)
    copies = []

    def write(ref, places):
        for d, block in enumerate(places):
            at = pl.multiple_of((lax.axis_index("wide") ^ block) * residues, 16)
            copies.append(
                pltpu.make_async_copy(
                    ref.at[:, pl.ds(d * residues, residues), :],
                    out_hbm.at[:, pl.ds(at, residues), :],
                    sems.at[len(copies)],
                )
            )
            copies[-1].start()

    if earlier:
        for ref, places in zip(before, earlier):
            write(ref, places)

    def right_of(d, m):
        ref, at = rights[d][m]
        return inputs[ref][at : at + minor * residues, :]

    def store(row, pair):
        done_ref[row] = pair.astype(done_ref.dtype)

    pair_rows(spread_ref, right_of, wide_ref, shift_ref[:1], outer_ref, store, wides=len(blocks), **sizes)
    if earlier:
        write(done_ref, blocks)
        for copy in copies:
            copy.wait()


def pair_blocks_kernel(*refs, wides, parts, minor, **sizes):
    left_refs, (right_ref, wf_ref, out_ref, spread_ref, wide_ref, outer_ref) = refs[:parts], refs[parts:]

    @pl.when(pl.program_id(0) == 0)
    def _():
        block_weights(wf_ref, wide_ref, parts=parts, minor=minor)
        spread_left(lambda m: left_refs[m][...], spread_ref, parts=parts)

    def store(row, pair):
        out_ref[row] = pair.astype(out_ref.dtype)

    pair_rows(
        spread_ref, lambda d, m: right_ref[d, m],
        wide_ref, wf_ref[wf_ref.shape[0] - 8 :][:1], outer_ref, store,
        wides=wides, parts=parts, minor=minor, **sizes,
    )


def on_device(wide, narrow, x, gain, bias, lm, lb, rm, rb, w, shift):
    seqs, residues, depth = x.shape
    hidden = lm.shape[1]
    cz = w.shape[1]
    per = LANES // hidden
    slots = LANES // seqs
    minor = hidden // slots
    own_rows = residues // narrow
    groups = own_rows // per
    pieces = 4
    hbm = pl.BlockSpec(memory_space=pltpu.HBM)
    vmem = pl.BlockSpec(memory_space=pltpu.VMEM)
    params = pltpu.CompilerParams(vmem_limit_bytes=VMEM_LIMIT)
    direct = wide == 4 and narrow == 4
    if direct:
        packs = ((0,), (RIGHT,), (1, RIGHT), (2, 3, RIGHT))
    else:
        packs = tuple((m,) for m in range(narrow)) + ((RIGHT,),)
    left_count, right_count = groups * seqs, minor * residues
    args = (x, gain, bias, lm.T, lb, rm.T, rb)
    made = pl.pallas_call(
        functools.partial(features_kernel, packs=packs, parts=narrow, pieces=pieces),
        out_shape=tuple(
            jax.ShapeDtypeStruct(
                (sum(right_count if i == RIGHT else left_count for i in pack), LANES), jnp.bfloat16
            )
            for pack in packs
        ),
        in_specs=[hbm] * len(args),
        out_specs=(hbm,) * len(packs),
        scratch_shapes=[pltpu.VMEM(a.shape, a.dtype) for a in args]
        + [
            pltpu.VMEM(((seqs + 1) * residues, LANES), jnp.float32),
            pltpu.VMEM(((seqs + 1) * residues, LANES), jnp.float32),
            pltpu.VMEM((residues // per * seqs, LANES), jnp.bfloat16),
            pltpu.VMEM((LANES, LANES), jnp.float32),
            pltpu.VMEM(((minor + 1) * residues, LANES), jnp.float32),
            pltpu.VMEM((minor * residues, LANES), jnp.bfloat16),
            pltpu.SemaphoreType.DMA((pieces + len(args) + sum(len(pack) for pack in packs),)),
        ],
        compiler_params=pltpu.CompilerParams(vmem_limit_bytes=VMEM_ALL),
        name="features",
    )(*args)

    def load(after):
        return pl.pallas_call(
            load_kernel,
            out_shape=jax.ShapeDtypeStruct((w.shape[0] + hidden + 8, cz), jnp.float32),
            in_specs=[vmem] * 3,
            out_specs=vmem,
            compiler_params=params,
            cost_estimate=pl.CostEstimate(flops=1, bytes_accessed=1000, transcendentals=0),
            name="load",
        )(w, shift, after)

    def across(a, m):
        return lax.ppermute(a, "narrow", [(i, i ^ m) for i in range(narrow)])

    def along(a, d):
        return lax.ppermute(a, "wide", [(i, i ^ d) for i in range(wide)])

    sizes = dict(parts=narrow, minor=minor, seqs_total=seqs * narrow)
    out_shape = jax.ShapeDtypeStruct((own_rows, wide * residues, cz), jnp.bfloat16)
    if direct:
        return pairs_by_block(made, across, along, load, out_shape, residues, sizes, params)

    lefts = [made[0]] + [across(made[m], m) for m in range(1, narrow)]
    every = lax.all_gather(made[narrow], ("wide", "narrow"), axis=0, tiled=False)
    every = every.reshape(wide, narrow, right_count, LANES)
    every = jnp.take(every, lax.axis_index("narrow") ^ jnp.arange(narrow), axis=1)
    block = wide
    while block % 2 == 0 and block * residues > 192:
        block //= 2
    cols = block * residues
    return pl.pallas_call(
        functools.partial(pair_blocks_kernel, wides=block, **sizes),
        grid=(wide // block,),
        in_specs=[pl.BlockSpec((left_count, LANES), lambda b: (0, 0))] * narrow
        + [
            pl.BlockSpec((block, narrow, right_count, LANES), lambda b: (b, 0, 0, 0)),
            pl.BlockSpec((w.shape[0] + hidden + 8, cz), lambda b: (0, 0)),
        ],
        out_specs=pl.BlockSpec((own_rows, cols, cz), lambda b: (0, b, 0)),
        out_shape=out_shape,
        scratch_shapes=[
            pltpu.VMEM((narrow, 2, seqs, 2 * groups * LANES), jnp.bfloat16),
            pltpu.VMEM((hidden * LANES // 2, 2 * cz), jnp.bfloat16),
            pltpu.VMEM((2 * groups * cols, hidden * LANES // 2), jnp.bfloat16),
        ],
        compiler_params=params,
        name="pairs",
    )(*lefts, every, load(lefts[0]))


def pairs_by_block(made, across, along, load, out_shape, residues, sizes, params):
    left_own, right, to_core, to_chip = made
    left_count, right_count = left_own.shape[0], right.shape[0]
    hbm = pl.BlockSpec(memory_space=pltpu.HBM)
    vmem = pl.BlockSpec(memory_space=pltpu.VMEM)
    own_rows, _, cz = out_shape.shape
    narrow = sizes["parts"]
    hidden = narrow * sizes["minor"]
    groups = own_rows * hidden // LANES

    def pack(*chunks, after, weight=1):
        return pl.pallas_call(
            functools.partial(pack_kernel, count=len(chunks)),
            out_shape=jax.ShapeDtypeStruct((sum(c.shape[0] for c in chunks), LANES), jnp.bfloat16),
            in_specs=[vmem] * (len(chunks) + len(after)),
            out_specs=vmem,
            compiler_params=params,
            cost_estimate=pl.CostEstimate(flops=weight, bytes_accessed=1000, transcendentals=0),
            name="pack",
        )(*chunks, *after)

    def pairs(rights, blocks, *shared, lefts=None, earlier=()):
        operands = []

        def place(chunk, at):
            operands.append(chunk)
            return len(operands) - 1, at

        rights = [[place(*chunk) for chunk in block] for block in rights]
        lefts = lefts and [place(*chunk) for chunk in lefts]
        count = len(operands)
        operands += shared
        cols = len(blocks) * residues
        done = jax.ShapeDtypeStruct((own_rows, cols, cz), jnp.bfloat16)
        shapes, outs = [done], [vmem]
        scratch = [pltpu.VMEM((2 * groups * cols, hidden * LANES // 2), jnp.bfloat16)]
        if lefts is not None:
            shapes += [
                jax.ShapeDtypeStruct((narrow, 2, LANES // narrow, 2 * groups * LANES), jnp.bfloat16),
                jax.ShapeDtypeStruct((hidden * LANES // 2, 2 * cz), jnp.bfloat16),
                jax.ShapeDtypeStruct((8, cz), jnp.float32),
            ]
            outs += [vmem] * 3
        if earlier:
            operands += [ref for ref, _ in earlier]
            shapes, outs = [out_shape], [hbm]
            scratch += [
                pltpu.VMEM(done.shape, done.dtype),
                pltpu.SemaphoreType.DMA((len(blocks) + sum(len(b) for _, b in earlier),)),
            ]
        return pl.pallas_call(
            functools.partial(
                pair_kernel, operands=count, rights=rights, blocks=blocks,
                earlier=[b for _, b in earlier], lefts=lefts, **sizes,
            ),
            out_shape=shapes,
            in_specs=[vmem] * len(operands),
            out_specs=outs,
            scratch_shapes=scratch,
            compiler_params=params,
            cost_estimate=pl.CostEstimate(flops=1000, bytes_accessed=1000, transcendentals=0),
            name=f"pairs_{blocks[0]}",
        )(*operands)

    far = along(right, 2)
    near = along(right, 1)
    last = along(far, 1)
    chip = across(to_chip, 2)
    core = across(to_core, 1)
    middle = pack(near, far, after=(), weight=4_000_000_000)
    beside = across(middle, 1)
    w = load(chip)
    both = across(pack(chip, after=(last, core, w)), 1)
    lefts = ((left_own, 0), (core, 0), (chip, 0), (both, left_count))
    own = ((right, 0), (core, left_count), (chip, 2 * left_count), (both, 2 * left_count))
    first, *shared = pairs((own,), (0,), w, lefts=lefts)

    other = across(middle, 2)
    onward = across(pack(other, after=(shared[1],)), 1)
    onward = ((onward, 0), (onward, right_count))
    blocks = [
        ((middle, at), (beside, at), (other, at), onward[i]) for i, at in enumerate((0, right_count))
    ]
    (second,) = pairs(blocks, (1, 2), *shared)

    other = across(last, 2)
    both = across(pack(last, other, after=()), 1)
    (out,) = pairs(
        (((last, 0), (both, 0), (other, 0), (both, right_count)),), (3,), *shared,
        earlier=((first, (0,)), (second, (1, 2))),
    )
    return out


def solution(mesh):
    in_specs = (P(("groups", "narrow"), "wide", None), P(), P(), P(), P(), P(), P(), P(), P())
    out_specs = P(("groups", "wide", "narrow"), None, None)
    return jax.shard_map(
        functools.partial(on_device, mesh.shape["wide"], mesh.shape["narrow"]),
        mesh=mesh,
        in_specs=in_specs,
        out_specs=out_specs,
        check_vma=False,
    )
```

```python
import functools

import jax
import jax.numpy as jnp
from jax import lax
from jax.experimental import pallas as pl
from jax.experimental.pallas import tpu as pltpu
from jax.sharding import PartitionSpec as P

LANES = 128
RIGHT = -1
VMEM_LIMIT = 40 * 1024 * 1024
VMEM_ALL = 62 * 1024 * 1024


def iota(shape, dim):
    return lax.broadcasted_iota(jnp.int32, shape, dim)


def features_kernel(*refs, packs, parts, pieces):
    args, refs = refs[:7], refs[7:]
    outs, refs = refs[: len(packs)], refs[len(packs) :]
    held, (lo_ref, hi_ref, left_ref, turned_ref, rows_ref, right_ref, sems) = refs[:7], refs[7:]
    x_ref, gain_ref, bias_ref, lm_ref, lb_ref, rm_ref, rb_ref = held
    seqs, residues, depth = x_ref.shape
    hidden = lm_ref.shape[0]
    per = LANES // hidden
    slots = LANES // seqs
    minor = hidden // slots
    groups = residues // per
    own = lax.axis_index("narrow")

    piece = seqs // pieces
    copies = [
        pltpu.make_async_copy(
            args[0].at[pl.ds(p * piece, piece)], x_ref.at[pl.ds(p * piece, piece)], sems.at[p]
        )
        for p in range(pieces)
    ]
    rest = [
        pltpu.make_async_copy(a, b, sems.at[pieces + i]) for i, (a, b) in enumerate(zip(args[1:], held[1:]))
    ]
    for copy in rest + copies:
        copy.start()
    free = pieces + len(rest)

    def norm(p):
        gain = gain_ref[...].reshape(1, depth)
        bias = bias_ref[...].reshape(1, depth)
        step = min(4, piece)
        for s in range(p * piece, (p + 1) * piece, step):
            x = x_ref[s : s + step].reshape(step * residues, depth).astype(jnp.float32)
            x = x - jnp.mean(x, axis=-1, keepdims=True)
            spread = jnp.mean(x * x, axis=-1, keepdims=True)
            x = x * lax.rsqrt(spread + 1e-05) * gain + bias
            rows = pl.ds(s * residues, step * residues)
            lo_ref[rows, :] = x[:, :LANES]
            hi_ref[rows, :] = x[:, LANES:]

    for copy in rest:
        copy.wait()

    column, row = iota((hidden, LANES), 1) % hidden, iota((hidden, LANES), 0)
    spread_l = (column == row).astype(jnp.float32)
    spread_r = (column == (row ^ (own * minor))).astype(jnp.float32)

    def widen(m, pick):
        return lax.dot_general(
            m, pick.astype(jnp.bfloat16), (((0,), (0,)), ((), ())),
            preferred_element_type=jnp.float32,
        )

    lane = iota((8, LANES), 1)

    def widen_bias(b):
        b = jnp.concatenate([b.reshape(1, hidden)] * per, axis=1)
        return jnp.broadcast_to(b, (8, LANES))

    def swapped(b):
        bit = 1
        while bit < slots:
            step = bit * minor
            up, down = pltpu.roll(b, step, axis=1), pltpu.roll(b, LANES - step, axis=1)
            other = jnp.where(lane & step != 0, up, down)
            b = jnp.where(own & bit != 0, other, b)
            bit *= 2
        return b

    weights = jnp.concatenate(
        [widen(lm_ref[...], spread_l), widen(rm_ref[...], spread_r)], axis=1
    )
    shift = jnp.concatenate(
        [widen_bias(lb_ref[...]), swapped(widen_bias(rb_ref[...]))], axis=1
    )[:1]
    place = iota((depth, 2 * LANES), 1) % LANES // hidden

    for p in range(pieces):
        copies[p].wait()
        norm(p)
    sends = []

    total = None
    for k in range(per):
        part = jnp.concatenate(
            [
                jnp.concatenate(
                    [half[pl.ds(g * per + k, seqs, stride=residues), :] for half in (lo_ref, hi_ref)],
                    axis=1,
                )
                for g in range(groups)
            ],
            axis=0,
        ).astype(jnp.bfloat16)
        placed = jnp.where(place == k, weights, 0.0).astype(jnp.bfloat16)
        term = jnp.dot(part, placed, preferred_element_type=jnp.float32)
        total = term if total is None else total + term
    total = total + shift
    left_ref[...] = total[:, :LANES].astype(left_ref.dtype)

    slot = iota((minor, LANES), 1) // seqs
    for block in range(groups // slots):
        turned_ref[...] = total[block * LANES : (block + 1) * LANES, LANES:].T
        for k in range(per):
            parts_of = [turned_ref[pl.ds(k * hidden + q * minor, minor), :] for q in range(slots)]
            for g in range(slots):
                out = None
                for q in range(slots):
                    moved = parts_of[q]
                    if q != g:
                        moved = pltpu.roll(moved, (q - g) % slots * seqs, axis=1)
                    out = moved if out is None else jnp.where(slot == q, moved, out)
                j = (block * slots + g) * per + k
                rows_ref[pl.ds(j, minor, stride=residues), :] = out
    right_ref[...] = rows_ref[: minor * residues].astype(right_ref.dtype)

    mine = left_ref.shape[0] // parts
    for out, pack in zip(outs, packs):
        at = 0
        for item in pack:
            if item == RIGHT:
                rows = right_ref
            else:
                rows = left_ref.at[pl.ds(pl.multiple_of((own ^ item) * mine, 16), mine)]
            free += 1
            sends.append(
                pltpu.make_async_copy(rows, out.at[pl.ds(at, rows.shape[0])], sems.at[free])
            )
            sends[-1].start()
            at += rows.shape[0]
    for copy in sends:
        copy.wait()


def load_kernel(w_ref, shift_ref, after_ref, wf_ref):
    del after_ref
    count = w_ref.shape[0]
    wf_ref[:count] = w_ref[...].astype(jnp.float32)
    wf_ref[count:] = jnp.broadcast_to(
        shift_ref[...].reshape(1, -1), (wf_ref.shape[0] - count, shift_ref.shape[0])
    )


def block_weights(wf_ref, wide_ref, *, parts, minor):
    cz = wf_ref.shape[1]
    hidden = parts * minor
    half = minor // 2
    rows_each = wide_ref.shape[0] // hidden // hidden
    own = lax.axis_index("narrow")
    wide_ref[...] = jnp.zeros_like(wide_ref)
    for e in range(hidden):
        rows = wf_ref[pl.ds(e ^ (own * minor), hidden, stride=hidden), :].astype(jnp.bfloat16)
        q, e2, t = e // minor, e % minor // half, e % half
        for k in range(rows_each):
            at = ((((q * half + t) * 2 + e2) * rows_each) + k) * hidden
            wide_ref[at : at + hidden, k * cz : (k + 1) * cz] = rows


def pack_kernel(*refs, count):
    out_ref, at = refs[-1], 0
    for ref in refs[:count]:
        out_ref[at : at + ref.shape[0]] = ref[...]
        at += ref.shape[0]


def spread_left(left_of, spread_ref, *, parts):
    seqs = LANES // parts
    low = iota((seqs, LANES), 1) < LANES // 2
    zero = jnp.zeros((seqs, LANES), jnp.float32)
    for m in range(parts):
        left = left_of(m)
        for g in range(left.shape[0] // seqs):
            rows = left[g * seqs : (g + 1) * seqs].astype(jnp.float32)
            turned = pltpu.roll(rows, LANES // 2, axis=1)
            for half, (first, second) in enumerate(((rows, turned), (turned, rows))):
                lanes = pl.ds((2 * g + half) * LANES, LANES)
                spread_ref[m, 0, :, lanes] = jnp.where(low, first, zero).astype(spread_ref.dtype)
                spread_ref[m, 1, :, lanes] = jnp.where(low, zero, second).astype(spread_ref.dtype)


def pair_rows(spread_ref, right_of, wide_ref, shift, outer_ref, store, *, wides, parts, minor, seqs_total):
    cz = shift.shape[1]
    half = minor // 2
    seqs = LANES // parts
    halves = spread_ref.shape[3] // LANES
    residues = right_of(0, 0).shape[0] // minor
    cols = wides * residues
    slot = iota((minor * residues, LANES), 1) // seqs
    for q in range(parts):
        left = jnp.concatenate([spread_ref[q ^ k, i] for i in range(2) for k in range(parts)], axis=0)
        rights = []
        for d in range(wides):
            right = None
            for k in range(parts):
                chunk = right_of(d, q ^ k)
                right = chunk if right is None else jnp.where(slot == k, chunk, right)
            rights.append(jnp.concatenate([right[: half * residues], right[half * residues :]], axis=1))
        right = jnp.concatenate(rights, axis=0)
        outer = jnp.dot(right, left, preferred_element_type=jnp.float32).astype(jnp.bfloat16)
        for d in range(wides):
            for t in range(half):
                at = (d * half + t) * residues
                for g in range(halves):
                    outer_ref[
                        pl.ds(g * cols + d * residues, residues),
                        (q * half + t) * LANES : (q * half + t + 1) * LANES,
                    ] = outer[at : at + residues, g * LANES : (g + 1) * LANES]

    pairs = jnp.dot(outer_ref[...], wide_ref[...], preferred_element_type=jnp.float32)
    rows_each = wide_ref.shape[1] // cz
    for g in range(halves):
        for k in range(rows_each):
            pair = pairs[g * cols : (g + 1) * cols, k * cz : (k + 1) * cz]
            store(g * rows_each + k, pair * (1.0 / seqs_total) + shift)


def pair_kernel(*refs, operands, rights, blocks, earlier, lefts=None, **sizes):
    parts, minor = sizes["parts"], sizes["minor"]
    inputs, refs = refs[:operands], refs[operands:]
    if lefts is not None:
        wf_ref, done_ref, spread_ref, wide_ref, shift_ref, outer_ref = refs
        own_rows = done_ref.shape[0]
        block_weights(wf_ref, wide_ref, parts=parts, minor=minor)
        shift_ref[...] = wf_ref[wf_ref.shape[0] - 8 :]
        count = own_rows * minor
        spread_left(lambda m: inputs[lefts[m][0]][lefts[m][1] : lefts[m][1] + count, :], spread_ref, parts=parts)
    elif not earlier:
        spread_ref, wide_ref, shift_ref, done_ref, outer_ref = refs
    else:
        spread_ref, wide_ref, shift_ref = refs[:3]
        before, (out_hbm, outer_ref, done_ref, sems) = refs[3 : 3 + len(earlier)], refs[3 + len(earlier) :]
    residues = done_ref.shape[1] // len(blocks)
    copies = []

    def write(ref, places):
        for d, block in enumerate(places):
            at = pl.multiple_of((lax.axis_index("wide") ^ block) * residues, 16)
            copies.append(
                pltpu.make_async_copy(
                    ref.at[:, pl.ds(d * residues, residues), :],
                    out_hbm.at[:, pl.ds(at, residues), :],
                    sems.at[len(copies)],
                )
            )
            copies[-1].start()

    if earlier:
        for ref, places in zip(before, earlier):
            write(ref, places)

    def right_of(d, m):
        ref, at = rights[d][m]
        return inputs[ref][at : at + minor * residues, :]

    def store(row, pair):
        done_ref[row] = pair.astype(done_ref.dtype)

    pair_rows(spread_ref, right_of, wide_ref, shift_ref[:1], outer_ref, store, wides=len(blocks), **sizes)
    if earlier:
        write(done_ref, blocks)
        for copy in copies:
            copy.wait()


def pair_blocks_kernel(*refs, wides, parts, minor, **sizes):
    left_refs, (right_ref, wf_ref, out_ref, spread_ref, wide_ref, outer_ref) = refs[:parts], refs[parts:]

    @pl.when(pl.program_id(0) == 0)
    def _():
        block_weights(wf_ref, wide_ref, parts=parts, minor=minor)
        spread_left(lambda m: left_refs[m][...], spread_ref, parts=parts)

    def store(row, pair):
        out_ref[row] = pair.astype(out_ref.dtype)

    pair_rows(
        spread_ref, lambda d, m: right_ref[d, m],
        wide_ref, wf_ref[wf_ref.shape[0] - 8 :][:1], outer_ref, store,
        wides=wides, parts=parts, minor=minor, **sizes,
    )


def on_device(wide, narrow, x, gain, bias, lm, lb, rm, rb, w, shift):
    seqs, residues, depth = x.shape
    hidden = lm.shape[1]
    cz = w.shape[1]
    per = LANES // hidden
    slots = LANES // seqs
    minor = hidden // slots
    own_rows = residues // narrow
    groups = own_rows // per
    pieces = 2
    hbm = pl.BlockSpec(memory_space=pltpu.HBM)
    vmem = pl.BlockSpec(memory_space=pltpu.VMEM)
    params = pltpu.CompilerParams(vmem_limit_bytes=VMEM_LIMIT)
    direct = wide == 4 and narrow == 4
    if direct:
        packs = ((0,), (RIGHT,), (1, RIGHT), (2, 3, RIGHT))
    else:
        packs = tuple((m,) for m in range(narrow)) + ((RIGHT,),)
    left_count, right_count = groups * seqs, minor * residues
    args = (x, gain, bias, lm.T, lb, rm.T, rb)
    made = pl.pallas_call(
        functools.partial(features_kernel, packs=packs, parts=narrow, pieces=pieces),
        out_shape=tuple(
            jax.ShapeDtypeStruct(
                (sum(right_count if i == RIGHT else left_count for i in pack), LANES), jnp.bfloat16
            )
            for pack in packs
        ),
        in_specs=[hbm] * len(args),
        out_specs=(hbm,) * len(packs),
        scratch_shapes=[pltpu.VMEM(a.shape, a.dtype) for a in args]
        + [
            pltpu.VMEM(((seqs + 1) * residues, LANES), jnp.float32),
            pltpu.VMEM(((seqs + 1) * residues, LANES), jnp.float32),
            pltpu.VMEM((residues // per * seqs, LANES), jnp.bfloat16),
            pltpu.VMEM((LANES, LANES), jnp.float32),
            pltpu.VMEM(((minor + 1) * residues, LANES), jnp.float32),
            pltpu.VMEM((minor * residues, LANES), jnp.bfloat16),
            pltpu.SemaphoreType.DMA((pieces + len(args) + sum(len(pack) for pack in packs),)),
        ],
        compiler_params=pltpu.CompilerParams(vmem_limit_bytes=VMEM_ALL),
        name="features",
    )(*args)

    def load(after):
        return pl.pallas_call(
            load_kernel,
            out_shape=jax.ShapeDtypeStruct((w.shape[0] + hidden + 8, cz), jnp.float32),
            in_specs=[vmem] * 3,
            out_specs=vmem,
            compiler_params=params,
            cost_estimate=pl.CostEstimate(flops=1, bytes_accessed=1000, transcendentals=0),
            name="load",
        )(w, shift, after)

    def across(a, m):
        return lax.ppermute(a, "narrow", [(i, i ^ m) for i in range(narrow)])

    def along(a, d):
        return lax.ppermute(a, "wide", [(i, i ^ d) for i in range(wide)])

    sizes = dict(parts=narrow, minor=minor, seqs_total=seqs * narrow)
    out_shape = jax.ShapeDtypeStruct((own_rows, wide * residues, cz), jnp.bfloat16)
    if direct:
        return pairs_by_block(made, across, along, load, out_shape, residues, sizes, params)

    lefts = [made[0]] + [across(made[m], m) for m in range(1, narrow)]
    every = lax.all_gather(made[narrow], ("wide", "narrow"), axis=0, tiled=False)
    every = every.reshape(wide, narrow, right_count, LANES)
    every = jnp.take(every, lax.axis_index("narrow") ^ jnp.arange(narrow), axis=1)
    block = wide
    while block % 2 == 0 and block * residues > 192:
        block //= 2
    cols = block * residues
    return pl.pallas_call(
        functools.partial(pair_blocks_kernel, wides=block, **sizes),
        grid=(wide // block,),
        in_specs=[pl.BlockSpec((left_count, LANES), lambda b: (0, 0))] * narrow
        + [
            pl.BlockSpec((block, narrow, right_count, LANES), lambda b: (b, 0, 0, 0)),
            pl.BlockSpec((w.shape[0] + hidden + 8, cz), lambda b: (0, 0)),
        ],
        out_specs=pl.BlockSpec((own_rows, cols, cz), lambda b: (0, b, 0)),
        out_shape=out_shape,
        scratch_shapes=[
            pltpu.VMEM((narrow, 2, seqs, 2 * groups * LANES), jnp.bfloat16),
            pltpu.VMEM((hidden * LANES // 2, 2 * cz), jnp.bfloat16),
            pltpu.VMEM((2 * groups * cols, hidden * LANES // 2), jnp.bfloat16),
        ],
        compiler_params=params,
        name="pairs",
    )(*lefts, every, load(lefts[0]))


def pairs_by_block(made, across, along, load, out_shape, residues, sizes, params):
    left_own, right, to_core, to_chip = made
    left_count, right_count = left_own.shape[0], right.shape[0]
    hbm = pl.BlockSpec(memory_space=pltpu.HBM)
    vmem = pl.BlockSpec(memory_space=pltpu.VMEM)
    own_rows, _, cz = out_shape.shape
    narrow = sizes["parts"]
    hidden = narrow * sizes["minor"]
    groups = own_rows * hidden // LANES

    def pack(*chunks, after, weight=1):
        return pl.pallas_call(
            functools.partial(pack_kernel, count=len(chunks)),
            out_shape=jax.ShapeDtypeStruct((sum(c.shape[0] for c in chunks), LANES), jnp.bfloat16),
            in_specs=[vmem] * (len(chunks) + len(after)),
            out_specs=vmem,
            compiler_params=params,
            cost_estimate=pl.CostEstimate(flops=weight, bytes_accessed=1000, transcendentals=0),
            name="pack",
        )(*chunks, *after)

    def pairs(rights, blocks, *shared, lefts=None, earlier=()):
        operands = []

        def place(chunk, at):
            operands.append(chunk)
            return len(operands) - 1, at

        rights = [[place(*chunk) for chunk in block] for block in rights]
        lefts = lefts and [place(*chunk) for chunk in lefts]
        count = len(operands)
        operands += shared
        cols = len(blocks) * residues
        done = jax.ShapeDtypeStruct((own_rows, cols, cz), jnp.bfloat16)
        shapes, outs = [done], [vmem]
        scratch = [pltpu.VMEM((2 * groups * cols, hidden * LANES // 2), jnp.bfloat16)]
        if lefts is not None:
            shapes += [
                jax.ShapeDtypeStruct((narrow, 2, LANES // narrow, 2 * groups * LANES), jnp.bfloat16),
                jax.ShapeDtypeStruct((hidden * LANES // 2, 2 * cz), jnp.bfloat16),
                jax.ShapeDtypeStruct((8, cz), jnp.float32),
            ]
            outs += [vmem] * 3
        if earlier:
            operands += [ref for ref, _ in earlier]
            shapes, outs = [out_shape], [hbm]
            scratch += [
                pltpu.VMEM(done.shape, done.dtype),
                pltpu.SemaphoreType.DMA((len(blocks) + sum(len(b) for _, b in earlier),)),
            ]
        return pl.pallas_call(
            functools.partial(
                pair_kernel, operands=count, rights=rights, blocks=blocks,
                earlier=[b for _, b in earlier], lefts=lefts, **sizes,
            ),
            out_shape=shapes,
            in_specs=[vmem] * len(operands),
            out_specs=outs,
            scratch_shapes=scratch,
            compiler_params=params,
            cost_estimate=pl.CostEstimate(flops=1000, bytes_accessed=1000, transcendentals=0),
            name=f"pairs_{blocks[0]}",
        )(*operands)

    far = along(right, 2)
    near = along(right, 1)
    last = along(far, 1)
    chip = across(to_chip, 2)
    core = across(to_core, 1)
    middle = pack(near, far, after=(), weight=4_000_000_000)
    beside = across(middle, 1)
    w = load(chip)
    both = across(pack(chip, after=(last, core, w)), 1)
    lefts = ((left_own, 0), (core, 0), (chip, 0), (both, left_count))
    own = ((right, 0), (core, left_count), (chip, 2 * left_count), (both, 2 * left_count))
    first, *shared = pairs((own,), (0,), w, lefts=lefts)

    other = across(middle, 2)
    onward = across(pack(other, after=(shared[1],)), 1)
    onward = ((onward, 0), (onward, right_count))
    blocks = [
        ((middle, at), (beside, at), (other, at), onward[i]) for i, at in enumerate((0, right_count))
    ]
    (second,) = pairs(blocks, (1, 2), *shared)

    other = across(last, 2)
    both = across(pack(last, other, after=()), 1)
    (out,) = pairs(
        (((last, 0), (both, 0), (other, 0), (both, right_count)),), (3,), *shared,
        earlier=((first, (0,)), (second, (1, 2))),
    )
    return out


def solution(mesh):
    in_specs = (P(("groups", "narrow"), "wide", None), P(), P(), P(), P(), P(), P(), P(), P())
    out_specs = P(("groups", "wide", "narrow"), None, None)
    return jax.shard_map(
        functools.partial(on_device, mesh.shape["wide"], mesh.shape["narrow"]),
        mesh=mesh,
        in_specs=in_specs,
        out_specs=out_specs,
        check_vma=False,
    )
```
